32 devices in a mesh: ctx: 4 (over z), tp: 8 (over y, x, core).
Axes of the slice: x: 2, y: 2, z: 4, core: 2. Of those that a mesh axis runs over, the one named last changes fastest.
Arguments:
- byte_embeds: bfloat16 [6144, 1024], P(('ctx', 'tp')), may hold values from -6 to 6
- local_embeds: bfloat16 [6144, 1024], P(('ctx', 'tp')), may hold values from -6 to 6
- global_qkv: bfloat16 [3, 8192, 4096], P(None, None, 'tp'), may hold values from -0.0625 to 0.0625
- global_out: bfloat16 [4096, 8192], P('tp'), may hold values from -1.5 to 1.5
- local_qkv: bfloat16 [1, 1024, 3072], replicated, may hold values from -0.1875 to 0.1875
- local_out: bfloat16 [1, 1024, 1024], replicated, may hold values from -0.1875 to 0.1875
- cotangent: bfloat16 [6144, 1024], P(('ctx', 'tp')), may hold values from -6 to 6
Outputs:
- hidden: bfloat16 [6144, 1024], P(('ctx', 'tp'))
- grad_qkv: float32 [1, 1024, 3072], P(None, ('ctx', 'tp'))
- grad_out: float32 [1, 1024, 1024], P(None, ('ctx', 'tp'))
The draws below stay inside these ranges and needn't reach their ends.
All inputs are finite; a program needn't handle non-finite values.
Results may differ from the reference program's by a relative error of at most 0.028.
Values may be sent and summed in bfloat16 or wider, within the bound.
No kernel may reach another device: no remote copies, remote signals or barrier semaphores. Data moves between devices by JAX's collectives and lax.ppermute only.
A program may use at most 128 MiB of HBM per device.

```python
import math
import jax
import jax.numpy as jnp
from jax import lax

PATCH = 8
LOCAL_WIDTH = 1024
HEADS = 32
HEAD_DIM = 128
LOCAL_HEADS = 8
LOCAL_HEAD_DIM = 128
LAYERS = 1
GLOBAL_WIDTH = 8192
ATTN_WIDTH = 4096
BYTES = 6144


def block_levels(stream_key, shape, cuts, low, top_value):
    def one(axis_at, shards_of):
        steps = jax.random.uniform(jax.random.fold_in(jax.random.fold_in(stream_key, 6), axis_at), (shards_of,), jnp.float32, low / len(cuts), top_value / len(cuts))
        return jnp.repeat(jnp.exp(steps), shape[axis_at] // shards_of).reshape((-1,) + (1,) * (len(shape) - axis_at - 1))

    gain = one(*cuts[0])
    for cut in cuts[1:]:
        gain = gain * one(*cut)
    return gain


def gaussian(stream_key, extent, scale, reach, shards=(), dtype=jnp.bfloat16):
    drawn = jax.random.normal(stream_key, extent, jnp.float32) * scale
    if len(shards) > 0:
        drawn = block_levels(stream_key, extent, shards, -0.22, 0.18) * drawn
    return jnp.clip(drawn, min=-reach, max=reach).astype(dtype)


def setup_inputs(seed: int = 0) -> dict:
    splits = jax.random.split(jax.random.key(seed), 8)
    return {
        "byte_embeds": gaussian(splits[0], (BYTES, LOCAL_WIDTH), 1.0, 6.0, ((0, 32),)),
        "local_embeds": gaussian(splits[1], (BYTES, LOCAL_WIDTH), 1.0, 6.0, ((0, 32),)),
        "global_qkv": gaussian(splits[2], (3, GLOBAL_WIDTH, ATTN_WIDTH), GLOBAL_WIDTH ** -0.5, 0.0625, ((2, 8),)),
        "global_out": gaussian(splits[3], (ATTN_WIDTH, GLOBAL_WIDTH), 0.25, 1.5, ((0, 8),)),
        "local_qkv": gaussian(splits[4], (LAYERS, LOCAL_WIDTH, 3 * LOCAL_WIDTH), LOCAL_WIDTH ** -0.5, 0.1875),
        "local_out": gaussian(splits[5], (LAYERS, LOCAL_WIDTH, LOCAL_WIDTH), LOCAL_WIDTH ** -0.5, 0.1875),
        "cotangent": gaussian(splits[6], (BYTES, LOCAL_WIDTH), 1.0, 6.0, ((0, 32),)),
    }


def rms_norm(values):
    return values * lax.rsqrt(lax.optimization_barrier(jnp.mean(values * values, axis=-1, keepdims=True)) + 1e-06)

def local_core(qkv_rows):
    total = qkv_rows.shape[0]
    groups = total // PATCH
    width = qkv_rows.shape[1] // 3
    parts = qkv_rows.reshape(groups, PATCH, 3, LOCAL_HEADS, LOCAL_HEAD_DIM)
    queries = rms_norm(parts[:, :, 0])
    keys_all = rms_norm(parts[:, :, 1])
    values = parts[:, :, 2]
    scores = jnp.einsum('npha,nqha->nhpq', queries, keys_all) / math.sqrt(LOCAL_HEAD_DIM)
    causal = jnp.arange(PATCH)[:, None] >= jnp.arange(PATCH)[None, :]
    weights = jnp.where(causal[None, None], jnp.exp(scores), 0.0)
    numerator = jnp.einsum('nhpq,nqha->npha', weights, values)
    denominator = lax.optimization_barrier(jnp.sum(weights, axis=-1)).transpose(0, 2, 1)[..., None]
    return (numerator / denominator).reshape(total, width)

def local_pass(state, local_qkv, local_out, cotangent):
    saved = []
    for layer in range(LAYERS):
        normed = rms_norm(state).astype(jnp.bfloat16)
        qkv_rows = jnp.dot(normed, local_qkv[layer], preferred_element_type=jnp.float32)
        core, core_back = jax.vjp(local_core, qkv_rows)
        attended = core.astype(jnp.bfloat16)
        saved.append((state, normed, core_back, attended))
        state = state + jnp.dot(attended, local_out[layer], preferred_element_type=jnp.float32)
    hidden = state.astype(jnp.bfloat16)
    grad_state = cotangent.astype(jnp.float32)
    grads_qkv = []
    grads_out = []
    for layer in range(LAYERS - 1, -1, -1):
        before, normed, core_back, attended = saved[layer]
        grad_round = grad_state.astype(jnp.bfloat16)
        grads_out.append(jnp.dot(attended.T, grad_round, preferred_element_type=jnp.float32))
        grad_core = jnp.dot(grad_round, local_out[layer].T, preferred_element_type=jnp.float32)
        grad_rows = core_back(grad_core)[0].astype(jnp.bfloat16)
        grads_qkv.append(jnp.dot(normed.T, grad_rows, preferred_element_type=jnp.float32))
        if layer > 0:
            grad_normed = jnp.dot(grad_rows, local_qkv[layer].T, preferred_element_type=jnp.float32)
            norm_back = jax.vjp(rms_norm, before)[1]
            grad_state = grad_state + norm_back(grad_normed)[0]
    return (hidden, jnp.stack(grads_qkv[::-1]), jnp.stack(grads_out[::-1]))

def reference(byte_embeds, local_embeds, global_qkv, global_out, local_qkv, local_out, cotangent):
    patch_count = byte_embeds.shape[0] // PATCH
    patch_in = byte_embeds.reshape(patch_count, PATCH * LOCAL_WIDTH).astype(jnp.float32)
    normed = rms_norm(patch_in).astype(jnp.bfloat16)
    query_proj = jnp.dot(normed, global_qkv[0], preferred_element_type=jnp.float32)
    key_proj = jnp.dot(normed, global_qkv[1], preferred_element_type=jnp.float32)
    value_proj = jnp.dot(normed, global_qkv[2], preferred_element_type=jnp.float32)
    queries = rms_norm(query_proj.reshape(patch_count, HEADS, HEAD_DIM)).astype(jnp.bfloat16)
    keys_all = rms_norm(key_proj.reshape(patch_count, HEADS, HEAD_DIM)).astype(jnp.bfloat16)
    values = value_proj.reshape(patch_count, HEADS, HEAD_DIM).astype(jnp.bfloat16)
    causal = jnp.arange(patch_count)[:, None] >= jnp.arange(patch_count)[None, :]

    def one_head(operands):
        head_q, head_k, head_v = operands
        scores = jnp.dot(head_q, head_k.T, preferred_element_type=jnp.float32) / math.sqrt(HEAD_DIM)
        expo = jnp.where(causal, jnp.exp(scores), 0.0)
        numerator = jnp.dot(expo.astype(jnp.bfloat16), head_v, preferred_element_type=jnp.float32)
        denominator = lax.optimization_barrier(jnp.sum(expo, axis=1))
        return numerator / denominator[:, None]
    per_head = lax.map(one_head, (queries.transpose(1, 0, 2), keys_all.transpose(1, 0, 2), values.transpose(1, 0, 2)))
    attended = per_head.transpose(1, 0, 2).reshape(patch_count, HEADS * HEAD_DIM).astype(jnp.bfloat16)
    patch_out = jnp.dot(attended, global_out, preferred_element_type=jnp.float32).astype(jnp.bfloat16)
    shifted = jnp.concatenate([jnp.zeros((1, patch_out.shape[1]), jnp.bfloat16), patch_out[:-1]], axis=0)
    context = shifted.reshape(byte_embeds.shape[0], LOCAL_WIDTH)
    state = local_embeds.astype(jnp.float32) + context.astype(jnp.float32)
    return local_pass(state, local_qkv, local_out, cotangent)
```

```python
import functools
import math

import jax
import jax.numpy as jnp
from jax import lax
from jax.experimental import pallas as pl
from jax.experimental.pallas import tpu as pltpu
from jax.sharding import PartitionSpec as P

PATCH = 8
HEAD_DIM = 128
LOCAL_HEADS = 8
LOCAL_HEAD_DIM = 128
EPS = 1e-06
F32 = jnp.float32
BF16 = jnp.bfloat16
MIB = 1 << 20
LANES = 128


def params(mib):
    return pltpu.CompilerParams(vmem_limit_bytes=mib * MIB)


def call(body, outs, scratch=(), mib=32):
    return pl.pallas_call(
        body,
        out_shape=[jax.ShapeDtypeStruct(shape, dtype) for shape, dtype in outs],
        scratch_shapes=list(scratch),
        compiler_params=params(mib),
    )


def dot(a, b, dims=((1,), (0,))):
    return lax.dot_general(a, b, (dims, ((), ())), preferred_element_type=F32)


def swap(value, bits):
    count = lax.axis_size("tp")
    return lax.ppermute(value, "tp", [(source, source ^ bits) for source in range(count)])


def block_order(size):
    return list(range(0, size, 2)) + list(range(1, size, 2))


def gather(value, size):
    even = [value] + [swap(value, bits) for bits in range(2, size, 2)]
    return even + [swap(piece, 1) for piece in even]


def patch_norm_body(x_ref, low_ref, high_ref, wide):
    patches = low_ref.shape[0]
    width = x_ref.shape[1]
    total = jnp.zeros((patches, LANES), F32)
    for c in range(width // LANES):
        wide[c] = x_ref[:, c * LANES : (c + 1) * LANES].astype(F32)
    for c in range(width // LANES):
        for b in range(PATCH):
            part = wide[c, pl.ds(b, patches, stride=PATCH), :]
            total += part * part
    scale = lax.rsqrt(jnp.sum(total, axis=-1, keepdims=True) / (PATCH * width) + EPS)
    half = PATCH // 2
    for b in range(PATCH):
        out_ref = low_ref if b < half else high_ref
        for c in range(width // LANES):
            part = wide[c, pl.ds(b, patches, stride=PATCH), :]
            at = (b % half) * width + c * LANES
            out_ref[:, at : at + LANES] = (part * scale).astype(BF16)


def patch_norm(byte_embeds):
    rows, width = byte_embeds.shape
    half = (rows // PATCH, PATCH * width // 2)
    return call(
        patch_norm_body,
        [(half, BF16), (half, BF16)],
        [pltpu.VMEM((width // LANES, rows, LANES), F32)],
    )(byte_embeds)


def project_low_body(x_ref, w_ref, out_ref, total):
    step = pl.program_id(1)
    depth = w_ref.shape[1]
    x = x_ref[:, pl.ds(pl.multiple_of(step * depth, depth), depth)]

    @pl.when(step == 0)
    def _():
        total[...] = dot(x, w_ref[0])

    @pl.when(step > 0)
    def _():
        total[...] += dot(x, w_ref[0])

    @pl.when(step == pl.num_programs(1) - 1)
    def _():
        out_ref[0] = total[...]


def project_high_body(x_ref, low_ref, w_ref, out_ref, total):
    which, step = pl.program_id(0), pl.program_id(1)
    depth = w_ref.shape[1]
    x = x_ref[:, pl.ds(pl.multiple_of(step * depth, depth), depth)]

    @pl.when(step == 0)
    def _():
        total[...] = low_ref[0] + dot(x, w_ref[0])

    @pl.when(step > 0)
    def _():
        total[...] += dot(x, w_ref[0])

    last = step == pl.num_programs(1) - 1

    @pl.when(last & (which < 2))
    def _():
        for h in range(total.shape[1] // HEAD_DIM):
            part = total[:, h * HEAD_DIM : (h + 1) * HEAD_DIM]
            mean = jnp.mean(part * part, axis=-1, keepdims=True)
            out_ref[0, :, h * HEAD_DIM : (h + 1) * HEAD_DIM] = (part * lax.rsqrt(mean + EPS)).astype(
                BF16
            )

    @pl.when(last & (which == 2))
    def _():
        out_ref[0] = total[...].astype(BF16)


def project(x, weights, low=None):
    rows, half = x.shape
    kinds, _, width = weights.shape
    depth = min(half, 1024)
    steps = half // depth
    offset = 0 if low is None else steps
    x_spec = pl.BlockSpec((rows, half), lambda c, k: (0, 0))
    w_spec = pl.BlockSpec((1, depth, width), lambda c, k: (c, k + offset, 0))
    out_spec = pl.BlockSpec((1, rows, width), lambda c, k: (c, 0, 0))
    first = low is None
    return pl.pallas_call(
        project_low_body if first else project_high_body,
        grid=(kinds, steps),
        in_specs=[x_spec, w_spec] if first else [x_spec, out_spec, w_spec],
        out_specs=out_spec,
        out_shape=jax.ShapeDtypeStruct((kinds, rows, width), F32 if first else BF16),
        scratch_shapes=[pltpu.VMEM((rows, width), F32)],
        compiler_params=params(24),
        cost_estimate=pl.CostEstimate(
            flops=2 * rows * half * kinds * width,
            bytes_accessed=2 * half * kinds * width,
            transcendentals=0,
        ),
    )(*((x, weights) if first else (x, low, weights)))


def attend_body(mask_ref, qkv_ref, k_ref, v_ref, out_ref):
    rows = qkv_ref.shape[1]
    keys = k_ref.shape[0]
    allowed = mask_ref[...] > 0
    for h in range(qkv_ref.shape[2] // HEAD_DIM):
        at = slice(h * HEAD_DIM, (h + 1) * HEAD_DIM)
        scores = dot(qkv_ref[0, :, at], k_ref[:, at], ((1,), (1,))) * (1.0 / math.sqrt(HEAD_DIM))
        expo = jnp.where(allowed, jnp.exp(scores), 0.0)
        top = dot(expo.astype(BF16), v_ref[:, at])
        out_ref[:, at] = (top / jnp.sum(expo, axis=-1, keepdims=True)).astype(BF16)


def attend(qkv, keys, values, mask):
    return call(attend_body, [(qkv.shape[1:], BF16)])(mask, qkv, keys, values)[0]


def output_body(a_ref, w_ref, even_ref, odd_ref):
    half = even_ref.shape[0]
    out = dot(a_ref[...], w_ref[...])
    even_ref[...] = out[:half].astype(BF16)
    odd_ref[...] = out[half:].astype(BF16)


def output_project(attended, weights):
    rows, depth = attended.shape
    width = weights.shape[1]
    step = min(width, 1024)
    out = jax.ShapeDtypeStruct((rows // 2, width), BF16)
    out_spec = pl.BlockSpec((rows // 2, step), lambda n: (0, n))
    return pl.pallas_call(
        output_body,
        grid=(width // step,),
        in_specs=[
            pl.BlockSpec((rows, depth), lambda n: (0, 0)),
            pl.BlockSpec((depth, step), lambda n: (0, n)),
        ],
        out_specs=[out_spec, out_spec],
        out_shape=[out, out],
        compiler_params=params(24),
    )(attended, weights)


def pair_sum_body(mine_ref, other_ref, own_ref, *send_refs):
    patches = own_ref.shape[0]
    total = mine_ref[...].astype(F32) + other_ref[...].astype(F32)
    own_ref[...] = total[:patches]
    for index, ref in enumerate(send_refs):
        ref[...] = total[(index + 1) * patches : (index + 2) * patches].astype(BF16)


def scatter_sum(even, odd, patches):
    blocks = even.shape[0] // patches
    block = (patches, even.shape[1])
    pieces = call(pair_sum_body, [(block, F32)] + [(block, BF16)] * (blocks - 1))(
        even, swap(odd, 1)
    )
    return [pieces[0]] + [swap(piece, 2 * (index + 1)) for index, piece in enumerate(pieces[1:])]


def block_sum_body(*refs):
    (*terms, out_ref, last_ref) = refs
    total = terms[0][...]
    for term in terms[1:]:
        total += term[...].astype(F32)
    total = total.astype(BF16).astype(F32)
    out_ref[...] = total
    last_ref[...] = total[-1:].astype(BF16)


def state_body(patch_ref, prev_ref, local_ref, state_ref, normed_ref, wide):
    patches = patch_ref.shape[0]
    width = state_ref.shape[1]
    first = lax.broadcasted_iota(jnp.int32, (patches, 1), 0) == 0
    chunks = width // LANES
    for b in range(PATCH):
        at = slice(b * width, (b + 1) * width)
        rolled = pltpu.roll(patch_ref[:, at], 1, 0)
        part = jnp.where(first, prev_ref[:, at].astype(F32), rolled)
        for c in range(chunks):
            wide[c, pl.ds(b, patches, stride=PATCH), :] = part[:, c * LANES : (c + 1) * LANES]
    context = jnp.concatenate([wide[c] for c in range(chunks)], axis=1)
    state = local_ref[...].astype(F32) + context
    state_ref[...] = state
    mean = jnp.mean(state * state, axis=-1, keepdims=True)
    normed_ref[...] = (state * lax.rsqrt(mean + EPS)).astype(BF16)


def unit(x):
    scale = lax.rsqrt(jnp.mean(x * x, axis=-1, keepdims=True) + EPS)
    return x * scale, scale


def unit_back(grad, y, scale):
    return scale * (grad - y * jnp.mean(grad * y, axis=-1, keepdims=True))


def local_body(order, head_ref, *refs):
    count = len(order)
    x_refs = refs[:count]
    (gb_ref, wq_ref, wk_ref, wv_ref, wo_ref, ab_ref, gqkv_ref, gout_ref, gqkv, gout) = refs[count:]
    rows = x_refs[0].shape[0]
    me = head_ref[1]
    row = lax.broadcasted_iota(jnp.int32, (rows, rows), 0)
    column = lax.broadcasted_iota(jnp.int32, (rows, rows), 1)
    allowed = (row // PATCH == column // PATCH) & (column <= row)
    root = 1.0 / math.sqrt(LOCAL_HEAD_DIM)
    weights = jnp.concatenate([wq_ref[0], wk_ref[0], wv_ref[0]], axis=1)
    wo = wo_ref[0]
    d = LOCAL_HEAD_DIM
    ab_ref[...] = jnp.zeros_like(ab_ref)
    for index, bits in enumerate(order):
        peer = me ^ bits
        x = x_refs[index][...]
        gb = gb_ref[pl.ds(pl.multiple_of(peer * rows, rows), rows), :]
        qkv = dot(x, weights)
        grad = dot(gb, wo, ((1,), (1,)))
        q, q_scale = unit(qkv[:, :d])
        k, k_scale = unit(qkv[:, d : 2 * d])
        qb, kb, vb, gradb = q.astype(BF16), k.astype(BF16), qkv[:, 2 * d :].astype(BF16), grad.astype(BF16)
        expo = jnp.where(allowed, jnp.exp(dot(qb, kb, ((1,), (1,))) * root), 0.0)
        weight = expo / jnp.sum(expo, axis=-1, keepdims=True)
        wb = weight.astype(BF16)
        ab = dot(wb, vb).astype(BF16)
        ab_ref[peer] = ab
        grad_v = dot(wb, gradb, ((0,), (0,)))
        grad_w = dot(gradb, vb, ((1,), (1,)))
        mean = jnp.sum(weight * grad_w, axis=-1, keepdims=True)
        grad_s = (weight * (grad_w - mean) * root).astype(BF16)
        grad_q = unit_back(dot(grad_s, kb), q, q_scale)
        grad_k = unit_back(dot(grad_s, qb, ((0,), (0,))), k, k_scale)
        gq = jnp.concatenate([grad_q, grad_k, grad_v], axis=1).astype(BF16)
        term_qkv = dot(x, gq, ((0,), (0,)))
        term_out = dot(ab, gb, ((0,), (0,)))
        if index == 0:
            gqkv[...] = term_qkv
            gout[...] = term_out
        else:
            gqkv[...] += term_qkv
            gout[...] += term_out
    gqkv_ref[...] = gqkv[...].astype(BF16)
    gout_ref[...] = jnp.zeros_like(gout_ref)
    share = gout_ref.shape[1]
    pieces = d // share
    base = head_ref[2]
    for piece in range(pieces):
        gout_ref[base + piece] = gout[piece * share : (piece + 1) * share, :].astype(BF16)


def local_layer(blocks, order, gb_all, local_qkv, local_out, head_info, tp_count, share):
    rows, width = blocks[0].shape
    count = len(blocks)
    d = LOCAL_HEAD_DIM
    heads = LOCAL_HEADS

    def whole(shape):
        return pl.BlockSpec(shape, lambda i, info: (0,) * len(shape))

    def qkv_spec(kind):
        return pl.BlockSpec((1, width, d), lambda i, info: (0, 0, kind * heads + info[0]))

    outs = [((tp_count, rows, d), BF16), ((width, 3 * d), BF16), ((tp_count, share, width), BF16)]
    return pl.pallas_call(
        functools.partial(local_body, order),
        grid_spec=pltpu.PrefetchScalarGridSpec(
            num_scalar_prefetch=1,
            grid=(1,),
            in_specs=[whole((rows, width))] * count
            + [whole(gb_all.shape)]
            + [qkv_spec(0), qkv_spec(1), qkv_spec(2)]
            + [pl.BlockSpec((1, d, width), lambda i, info: (0, info[0], 0))],
            out_specs=[whole(shape) for shape, _ in outs],
            scratch_shapes=[pltpu.VMEM((width, 3 * d), F32), pltpu.VMEM((d, width), F32)],
        ),
        out_shape=[jax.ShapeDtypeStruct(shape, dtype) for shape, dtype in outs],
        compiler_params=params(48),
    )(head_info, *blocks, gb_all, local_qkv, local_qkv, local_qkv, local_out)


def hidden_body(state_ref, ab_ref, w_ref, out_ref):
    d = ab_ref.shape[2]
    total = state_ref[...]
    for h in range(ab_ref.shape[0]):
        total += dot(ab_ref[h], w_ref[0, h * d : (h + 1) * d, :])
    out_ref[...] = total.astype(BF16)


def grad_qkv_body(heads, parts_ref, out_ref):
    d = LOCAL_HEAD_DIM
    sources = parts_ref.shape[0]
    for h in range(heads):
        total = parts_ref[h].astype(F32)
        for source in range(h + heads, sources, heads):
            total += parts_ref[source].astype(F32)
        for kind in range(3):
            at = (kind * heads + h) * d
            out_ref[0, :, at : at + d] = total[:, kind * d : (kind + 1) * d]


def plane_sum_body(groups, parts_ref, out_ref):
    for plane, sources in enumerate(groups):
        total = parts_ref[sources[0]].astype(F32)
        for source in sources[1:]:
            total += parts_ref[source].astype(F32)
        out_ref[plane] = total.astype(BF16)


def final_sum_body(parts_ref, out_ref):
    total = parts_ref[0].astype(F32)
    for source in range(1, parts_ref.shape[0]):
        total += parts_ref[source].astype(F32)
    out_ref[0] = total


def per_device(byte_embeds, local_embeds, global_qkv, global_out, local_qkv, local_out, cotangent):
    byte_count, width = byte_embeds.shape
    patches = byte_count // PATCH
    planes, tp_count = lax.axis_size("ctx"), lax.axis_size("tp")
    plane, me = lax.axis_index("ctx"), lax.axis_index("tp")
    order = block_order(tp_count)
    shard_rows = tp_count * patches

    low, high = patch_norm(byte_embeds)
    total = project(jnp.concatenate(gather(low, tp_count), axis=0), global_qkv)
    qkv = project(jnp.concatenate(gather(high, tp_count), axis=0), global_qkv, total)

    place = (
        (me ^ jnp.array(order, jnp.int32))[:, None] * patches
        + jnp.arange(patches, dtype=jnp.int32)[None, :]
    ).reshape(-1)
    keys = lax.all_gather(qkv[1], "ctx", axis=0, tiled=True)
    values = lax.all_gather(qkv[2], "ctx", axis=0, tiled=True)
    key_place = (jnp.arange(planes, dtype=jnp.int32)[:, None] * shard_rows + place[None, :]).reshape(-1)
    mask = (key_place[None, :] <= (plane * shard_rows + place)[:, None]).astype(F32)
    attended = attend(qkv, keys, values, mask)

    even, odd = output_project(attended, global_out)
    terms = scatter_sum(even, odd, patches)
    patch_out, last = call(
        block_sum_body, [(terms[0].shape, F32), ((1, terms[0].shape[1]), BF16)]
    )(*terms)
    devices = planes * tp_count
    prev = lax.ppermute(last, ("ctx", "tp"), [(d, d + 1) for d in range(devices - 1)])
    state, normed = call(
        state_body,
        [((byte_count, width), F32), ((byte_count, width), BF16)],
        [pltpu.VMEM((width // LANES, byte_count, LANES), F32)],
    )(patch_out, prev, local_embeds)

    group = min(tp_count, LOCAL_HEADS)
    share = width // devices
    pieces = LOCAL_HEAD_DIM // share
    plane_heads = LOCAL_HEADS // planes
    head = me % group
    gb_all = lax.all_gather(cotangent, "tp", axis=0, tiled=True)
    head_info = jnp.stack([head, me, (head % plane_heads) * pieces]).astype(jnp.int32)
    ab, grad_qkv, grad_out = local_layer(
        gather(normed, group), block_order(group), gb_all, local_qkv, local_out, head_info, tp_count, share
    )

    grad_qkv = lax.all_to_all(grad_qkv, ("ctx", "tp"), 0, 0, tiled=True)
    ab = lax.all_to_all(ab, "tp", 0, 0, tiled=True)
    grad_out = lax.all_to_all(grad_out, "tp", 0, 0, tiled=True)
    if group < tp_count:
        ab = lax.dynamic_slice_in_dim(ab, (me // group) * group, group, 0)
    hidden = call(hidden_body, [((byte_count, width), BF16)])(state, ab, local_out)[0]
    groups = [
        [t for t in range(tp_count) if (t % group) // plane_heads == c] for c in range(planes)
    ]
    grad_out = call(
        functools.partial(plane_sum_body, groups), [((planes, share, width), BF16)]
    )(grad_out)[0]
    grad_out = lax.all_to_all(grad_out, "ctx", 0, 0, tiled=True)
    grad_out = call(final_sum_body, [((1, share, width), F32)])(grad_out)[0]
    grad_qkv = call(functools.partial(grad_qkv_body, LOCAL_HEADS), [((1, share, 3 * width), F32)])(
        grad_qkv.reshape(devices, share, 3 * LOCAL_HEAD_DIM)
    )[0]
    return (hidden, grad_qkv, grad_out)


def solution(mesh):
    in_specs = (
        P(("ctx", "tp"), None),
        P(("ctx", "tp"), None),
        P(None, None, "tp"),
        P("tp", None),
        P(),
        P(),
        P(("ctx", "tp"), None),
    )
    out_specs = (P(("ctx", "tp"), None), P(None, ("ctx", "tp"), None), P(None, ("ctx", "tp"), None))
    return jax.shard_map(
        per_device, mesh=mesh, in_specs=in_specs, out_specs=out_specs, check_vma=False
    )
```

```python
import functools
import math

import jax
import jax.numpy as jnp
from jax import lax
from jax.experimental import pallas as pl
from jax.experimental.pallas import tpu as pltpu
from jax.sharding import PartitionSpec as P

PATCH = 8
HEAD_DIM = 128
LOCAL_HEADS = 8
LOCAL_HEAD_DIM = 128
EPS = 1e-06
F32 = jnp.float32
BF16 = jnp.bfloat16
MIB = 1 << 20
LANES = 128


def params(mib):
    return pltpu.CompilerParams(vmem_limit_bytes=mib * MIB)


def call(body, outs, scratch=(), mib=32):
    return pl.pallas_call(
        body,
        out_shape=[jax.ShapeDtypeStruct(shape, dtype) for shape, dtype in outs],
        scratch_shapes=list(scratch),
        compiler_params=params(mib),
    )


def dot(a, b, dims=((1,), (0,))):
    return lax.dot_general(a, b, (dims, ((), ())), preferred_element_type=F32)


def swap(value, bits):
    count = lax.axis_size("tp")
    return lax.ppermute(value, "tp", [(source, source ^ bits) for source in range(count)])


def block_order(size):
    return list(range(0, size, 2)) + list(range(1, size, 2))


def gather(value, size):
    even = [value] + [swap(value, bits) for bits in range(2, size, 2)]
    return even + [swap(piece, 1) for piece in even]


def patch_norm_body(x_ref, low_ref, high_ref, wide):
    patches = low_ref.shape[0]
    width = x_ref.shape[1]
    total = jnp.zeros((patches, LANES), F32)
    for c in range(width // LANES):
        wide[c] = x_ref[:, c * LANES : (c + 1) * LANES].astype(F32)
    for c in range(width // LANES):
        for b in range(PATCH):
            part = wide[c, pl.ds(b, patches, stride=PATCH), :]
            total += part * part
    scale = lax.rsqrt(jnp.sum(total, axis=-1, keepdims=True) / (PATCH * width) + EPS)
    half = PATCH // 2
    for b in range(PATCH):
        out_ref = low_ref if b < half else high_ref
        for c in range(width // LANES):
            part = wide[c, pl.ds(b, patches, stride=PATCH), :]
            at = (b % half) * width + c * LANES
            out_ref[:, at : at + LANES] = (part * scale).astype(BF16)


def patch_norm(byte_embeds):
    rows, width = byte_embeds.shape
    half = (rows // PATCH, PATCH * width // 2)
    return call(
        patch_norm_body,
        [(half, BF16), (half, BF16)],
        [pltpu.VMEM((width // LANES, rows, LANES), F32)],
    )(byte_embeds)


def project_low_body(x_ref, w_ref, out_ref, total):
    step = pl.program_id(1)
    depth = w_ref.shape[1]
    x = x_ref[:, pl.ds(pl.multiple_of(step * depth, depth), depth)]

    @pl.when(step == 0)
    def _():
        total[...] = dot(x, w_ref[0])

    @pl.when(step > 0)
    def _():
        total[...] += dot(x, w_ref[0])

    @pl.when(step == pl.num_programs(1) - 1)
    def _():
        out_ref[0] = total[...]


def project_high_body(x_ref, low_ref, pass_ref, w_ref, out_ref, passed_ref, total):
    which, step = pl.program_id(0), pl.program_id(1)

    @pl.when((which == 0) & (step == 0))
    def _():
        passed_ref[...] = pass_ref[...]

    depth = w_ref.shape[1]
    x = x_ref[:, pl.ds(pl.multiple_of(step * depth, depth), depth)]

    @pl.when(step == 0)
    def _():
        total[...] = low_ref[0] + dot(x, w_ref[0])

    @pl.when(step > 0)
    def _():
        total[...] += dot(x, w_ref[0])

    last = step == pl.num_programs(1) - 1

    @pl.when(last & (which < 2))
    def _():
        for h in range(total.shape[1] // HEAD_DIM):
            part = total[:, h * HEAD_DIM : (h + 1) * HEAD_DIM]
            mean = jnp.mean(part * part, axis=-1, keepdims=True)
            out_ref[0, :, h * HEAD_DIM : (h + 1) * HEAD_DIM] = (part * lax.rsqrt(mean + EPS)).astype(
                BF16
            )

    @pl.when(last & (which == 2))
    def _():
        out_ref[0] = total[...].astype(BF16)


def project(x, weights, low=None, passed=None):
    rows, half = x.shape
    kinds, _, width = weights.shape
    depth = min(half, 1024)
    steps = half // depth
    offset = 0 if low is None else steps
    x_spec = pl.BlockSpec((rows, half), lambda c, k: (0, 0))
    w_spec = pl.BlockSpec((1, depth, width), lambda c, k: (c, k + offset, 0))
    out_spec = pl.BlockSpec((1, rows, width), lambda c, k: (c, 0, 0))
    cost = pl.CostEstimate(
        flops=2 * rows * half * kinds * width,
        bytes_accessed=2 * half * kinds * width,
        transcendentals=0,
    )
    scratch = [pltpu.VMEM((rows, width), F32)]
    if low is None:
        return pl.pallas_call(
            project_low_body,
            grid=(kinds, steps),
            in_specs=[x_spec, w_spec],
            out_specs=out_spec,
            out_shape=jax.ShapeDtypeStruct((kinds, rows, width), F32),
            scratch_shapes=scratch,
            compiler_params=params(60),
            cost_estimate=cost,
        )(x, weights)
    pass_spec = pl.BlockSpec(passed.shape, lambda c, k: (0, 0))
    return pl.pallas_call(
        project_high_body,
        grid=(kinds, steps),
        in_specs=[x_spec, out_spec, pass_spec, w_spec],
        out_specs=[out_spec, pass_spec],
        out_shape=[
            jax.ShapeDtypeStruct((kinds, rows, width), BF16),
            jax.ShapeDtypeStruct(passed.shape, passed.dtype),
        ],
        scratch_shapes=scratch,
        compiler_params=params(60),
        cost_estimate=cost,
    )(x, low, passed, weights)


def attend_body(mask_ref, qkv_ref, k_ref, v_ref, out_ref):
    rows = qkv_ref.shape[1]
    keys = k_ref.shape[0]
    allowed = mask_ref[...] > 0
    for h in range(qkv_ref.shape[2] // HEAD_DIM):
        at = slice(h * HEAD_DIM, (h + 1) * HEAD_DIM)
        scores = dot(qkv_ref[0, :, at], k_ref[:, at], ((1,), (1,))) * (1.0 / math.sqrt(HEAD_DIM))
        expo = jnp.where(allowed, jnp.exp(scores), 0.0)
        top = dot(expo.astype(BF16), v_ref[:, at])
        out_ref[:, at] = (top / jnp.sum(expo, axis=-1, keepdims=True)).astype(BF16)


def attend(qkv, keys, values, mask):
    return call(attend_body, [(qkv.shape[1:], BF16)])(mask, qkv, keys, values)[0]


def output_body(a_ref, w_ref, even_ref, odd_ref):
    half = even_ref.shape[0]
    out = dot(a_ref[...], w_ref[...])
    even_ref[...] = out[:half].astype(BF16)
    odd_ref[...] = out[half:].astype(BF16)


def output_project(attended, weights):
    rows, depth = attended.shape
    width = weights.shape[1]
    step = min(width, 1024)
    out = jax.ShapeDtypeStruct((rows // 2, width), BF16)
    out_spec = pl.BlockSpec((rows // 2, step), lambda n: (0, n))
    return pl.pallas_call(
        output_body,
        grid=(width // step,),
        in_specs=[
            pl.BlockSpec((rows, depth), lambda n: (0, 0)),
            pl.BlockSpec((depth, step), lambda n: (0, n)),
        ],
        out_specs=[out_spec, out_spec],
        out_shape=[out, out],
        compiler_params=params(24),
    )(attended, weights)


def pair_sum_body(mine_ref, other_ref, own_ref, *send_refs):
    patches = own_ref.shape[0]
    total = mine_ref[...].astype(F32) + other_ref[...].astype(F32)
    own_ref[...] = total[:patches]
    for index, ref in enumerate(send_refs):
        ref[...] = total[(index + 1) * patches : (index + 2) * patches].astype(BF16)


def scatter_sum(even, odd, patches):
    blocks = even.shape[0] // patches
    block = (patches, even.shape[1])
    pieces = call(pair_sum_body, [(block, F32)] + [(block, BF16)] * (blocks - 1))(
        even, swap(odd, 1)
    )
    return [pieces[0]] + [swap(piece, 2 * (index + 1)) for index, piece in enumerate(pieces[1:])]


def block_sum_body(*refs):
    (*terms, out_ref, last_ref) = refs
    total = terms[0][...]
    for term in terms[1:]:
        total += term[...].astype(F32)
    total = total.astype(BF16).astype(F32)
    out_ref[...] = total
    last_ref[...] = total[-1:].astype(BF16)


def state_body(patch_ref, prev_ref, local_ref, state_ref, normed_ref, wide):
    patches = patch_ref.shape[0]
    width = state_ref.shape[1]
    first = lax.broadcasted_iota(jnp.int32, (patches, 1), 0) == 0
    chunks = width // LANES
    for b in range(PATCH):
        at = slice(b * width, (b + 1) * width)
        rolled = pltpu.roll(patch_ref[:, at], 1, 0)
        part = jnp.where(first, prev_ref[:, at].astype(F32), rolled)
        for c in range(chunks):
            wide[c, pl.ds(b, patches, stride=PATCH), :] = part[:, c * LANES : (c + 1) * LANES]
    context = jnp.concatenate([wide[c] for c in range(chunks)], axis=1)
    state = local_ref[...].astype(F32) + context
    state_ref[...] = state
    mean = jnp.mean(state * state, axis=-1, keepdims=True)
    normed_ref[...] = (state * lax.rsqrt(mean + EPS)).astype(BF16)


def unit(x):
    scale = lax.rsqrt(jnp.mean(x * x, axis=-1, keepdims=True) + EPS)
    return x * scale, scale


def unit_back(grad, y, scale):
    return scale * (grad - y * jnp.mean(grad * y, axis=-1, keepdims=True))


def core_grad_body(head_ref, gb_ref, wo_ref, out_ref):
    out_ref[...] = dot(gb_ref[...], wo_ref[0], ((1,), (1,))).astype(BF16)


def core_grad(head_info, gb_all, local_out):
    rows, width = gb_all.shape
    d = LOCAL_HEAD_DIM
    return pl.pallas_call(
        core_grad_body,
        grid_spec=pltpu.PrefetchScalarGridSpec(
            num_scalar_prefetch=1,
            grid=(1,),
            in_specs=[
                pl.BlockSpec((rows, width), lambda i, info: (0, 0)),
                pl.BlockSpec((1, d, width), lambda i, info: (0, info[0], 0)),
            ],
            out_specs=pl.BlockSpec((rows, d), lambda i, info: (0, 0)),
        ),
        out_shape=jax.ShapeDtypeStruct((rows, d), BF16),
        compiler_params=params(24),
    )(head_info, gb_all, local_out)


def local_body(orders, step, head_ref, *refs):
    refs = list(refs)

    def take(count):
        taken = refs[:count]
        del refs[:count]
        return taken

    order = orders[step]
    count = len(order)
    last = step == len(orders) - 1
    x_refs = take(count)
    gb_ref, gcore_ref, wq_ref, wk_ref, wv_ref = take(5)
    carry = take(2) if step else None
    earlier = take(step) if last else []
    rows = x_refs[0].shape[0]
    me = head_ref[1]
    d = LOCAL_HEAD_DIM
    row = lax.broadcasted_iota(jnp.int32, (rows, rows), 0)
    column = lax.broadcasted_iota(jnp.int32, (rows, rows), 1)
    allowed = (row // PATCH == column // PATCH) & (column <= row)
    root = 1.0 / math.sqrt(d)

    def block_of(ref, bits):
        return ref[pl.ds(pl.multiple_of((me ^ bits) * rows, rows), rows), :]

    x = jnp.concatenate([ref[...] for ref in x_refs], axis=0)
    gb = jnp.concatenate([block_of(gb_ref, bits) for bits in order], axis=0)
    weights = jnp.concatenate([wq_ref[0], wk_ref[0], wv_ref[0]], axis=1)
    qkv = dot(x, weights)
    abs_, gqs = [], []
    for index, bits in enumerate(order):
        at = slice(index * rows, (index + 1) * rows)
        gradb = block_of(gcore_ref, bits)
        q, q_scale = unit(qkv[at, :d])
        k, k_scale = unit(qkv[at, d : 2 * d])
        qb, kb, vb = q.astype(BF16), k.astype(BF16), qkv[at, 2 * d :].astype(BF16)
        expo = jnp.where(allowed, jnp.exp(dot(qb, kb, ((1,), (1,))) * root), 0.0)
        weight = expo / jnp.sum(expo, axis=-1, keepdims=True)
        wb = weight.astype(BF16)
        abs_.append(dot(wb, vb).astype(BF16))
        grad_v = dot(wb, gradb, ((0,), (0,)))
        grad_w = dot(gradb, vb, ((1,), (1,)))
        mean = jnp.sum(weight * grad_w, axis=-1, keepdims=True)
        grad_s = (weight * (grad_w - mean) * root).astype(BF16)
        grad_q = unit_back(dot(grad_s, kb), q, q_scale)
        grad_k = unit_back(dot(grad_s, qb, ((0,), (0,))), k, k_scale)
        gqs.append(jnp.concatenate([grad_q, grad_k, grad_v], axis=1).astype(BF16))
    gqkv = dot(jnp.concatenate(gqs, axis=0), x, ((0,), (0,)))
    gout = dot(jnp.concatenate(abs_, axis=0), gb, ((0,), (0,)))
    if carry:
        gqkv += carry[0][...]
        gout += carry[1][...]
    if not last:
        gqkv_ref, gout_ref, ab_ref = refs
        gqkv_ref[...] = gqkv
        gout_ref[...] = gout
        for index, ab in enumerate(abs_):
            ab_ref[index] = ab
        return
    *plane_refs, send_ref, gqkv_total, gout_total = refs
    gqkv_total[...] = gqkv
    gout_total[...] = gout
    piece = plane_refs[0].shape[1]
    for k, ref in enumerate(plane_refs):
        at = pl.multiple_of((head_ref[3] ^ k) * piece, piece)
        ref[...] = gqkv_total[:, pl.ds(at, piece)].astype(BF16)
    send_ref[...] = jnp.zeros_like(send_ref)
    for ref, bits_list in zip(earlier, orders):
        for index, bits in enumerate(bits_list):
            send_ref[me ^ bits, :rows, :] = ref[index]
    for bits, ab in zip(order, abs_):
        send_ref[me ^ bits, :rows, :] = ab
    chunks = gout_total.shape[1] // d
    share = (send_ref.shape[1] - rows) // chunks
    for part in range(d // share):
        for c in range(chunks):
            send_ref[head_ref[2] + part, rows + c * share : rows + (c + 1) * share, :] = gout_total[
                part * share : (part + 1) * share, c * d : (c + 1) * d
            ].astype(BF16)


def local_layer(blocks, gb_all, gcore, local_qkv, head_info, tp_count, planes):
    rows, width = blocks[0].shape
    group = len(blocks)
    order = block_order(group)
    by_bits = dict(zip(order, blocks))
    orders = [part for part in ([0, 1], [2, 3], list(range(4, group))) if part and part[0] < group]
    d = LOCAL_HEAD_DIM
    heads = LOCAL_HEADS
    share = width // (planes * tp_count)

    def whole(shape):
        return pl.BlockSpec(shape, lambda i, info: (0,) * len(shape))

    def qkv_spec(kind):
        return pl.BlockSpec((1, width, d), lambda i, info: (0, 0, kind * heads + info[0]))

    carry, abs_ = [], []
    for step, part in enumerate(orders):
        last = step == len(orders) - 1
        plain = [by_bits[bits] for bits in part] + [gb_all, gcore]
        extra = carry + (abs_ if last else [])
        totals = [((3 * d, width), F32), ((d, width), F32)]
        if last:
            outs = [((3 * d, width // planes), BF16)] * planes
            outs += [((tp_count, rows + share * (width // d), d), BF16)]
        else:
            outs = totals + [((len(part), rows, d), BF16)]
        result = pl.pallas_call(
            functools.partial(local_body, orders, step),
            grid_spec=pltpu.PrefetchScalarGridSpec(
                num_scalar_prefetch=1,
                grid=(1,),
                in_specs=[whole(a.shape) for a in plain]
                + [qkv_spec(0), qkv_spec(1), qkv_spec(2)]
                + [whole(a.shape) for a in extra],
                out_specs=[whole(shape) for shape, _ in outs],
                scratch_shapes=[pltpu.VMEM(s, t) for s, t in totals] if last else [],
            ),
            out_shape=[jax.ShapeDtypeStruct(shape, dtype) for shape, dtype in outs],
            compiler_params=params(48),
        )(head_info, *plain, local_qkv, local_qkv, local_qkv, *extra)
        if not last:
            carry = list(result[:2])
            abs_.append(result[2])
    return result[:-1], result[-1]


def hidden_body(rows, state_ref, parts_ref, w_ref, out_ref):
    ab = jnp.concatenate([parts_ref[h, :rows, :] for h in range(parts_ref.shape[0])], axis=1)
    out_ref[...] = (state_ref[...] + dot(ab, w_ref[0])).astype(BF16)


def plane_sum_body(groups, rows, info_ref, parts_ref, *refs):
    *out_refs, sums = refs
    for plane, sources in enumerate(groups):
        total = parts_ref[sources[0], rows:, :].astype(F32)
        for source in sources[1:]:
            total += parts_ref[source, rows:, :].astype(F32)
        sums[plane] = total
    for k, ref in enumerate(out_refs):
        ref[...] = sums[info_ref[3] ^ k].astype(BF16)


def grad_out_body(*refs):
    *terms, out_ref = refs
    total = terms[0][...].astype(F32)
    for term in terms[1:]:
        total += term[...].astype(F32)
    share = out_ref.shape[1]
    for c in range(out_ref.shape[2] // LANES):
        out_ref[0, :, c * LANES : (c + 1) * LANES] = total[c * share : (c + 1) * share]


def turn_body(*refs):
    *terms, out_ref = refs
    total = terms[0][...].astype(F32)
    for term in terms[1:]:
        total += term[...].astype(F32)
    out_ref[...] = total.T.astype(BF16)


def grad_qkv_body(heads, parts_ref, out_ref):
    d = LOCAL_HEAD_DIM
    sources = parts_ref.shape[0]
    for h in range(heads):
        total = parts_ref[h].astype(F32)
        for source in range(h + heads, sources, heads):
            total += parts_ref[source].astype(F32)
        for kind in range(3):
            at = (kind * heads + h) * d
            out_ref[0, :, at : at + d] = total[:, kind * d : (kind + 1) * d]


def swap_planes(pieces):
    count = len(pieces)
    return [pieces[0]] + [
        lax.ppermute(pieces[k], "ctx", [(c, c ^ k) for c in range(count)]) for k in range(1, count)
    ]


def per_device(byte_embeds, local_embeds, global_qkv, global_out, local_qkv, local_out, cotangent):
    byte_count, width = byte_embeds.shape
    patches = byte_count // PATCH
    planes, tp_count = lax.axis_size("ctx"), lax.axis_size("tp")
    plane, me = lax.axis_index("ctx"), lax.axis_index("tp")
    order = block_order(tp_count)
    shard_rows = tp_count * patches

    low, high = patch_norm(byte_embeds)
    total = project(jnp.concatenate(gather(low, tp_count), axis=0), global_qkv)
    qkv, gb = project(
        jnp.concatenate(gather(high, tp_count), axis=0), global_qkv, total, cotangent
    )

    place = (
        (me ^ jnp.array(order, jnp.int32))[:, None] * patches
        + jnp.arange(patches, dtype=jnp.int32)[None, :]
    ).reshape(-1)
    keys = lax.all_gather(qkv[1], "ctx", axis=0, tiled=True)
    values = lax.all_gather(qkv[2], "ctx", axis=0, tiled=True)
    key_place = (jnp.arange(planes, dtype=jnp.int32)[:, None] * shard_rows + place[None, :]).reshape(-1)
    mask = (key_place[None, :] <= (plane * shard_rows + place)[:, None]).astype(F32)
    attended = attend(qkv, keys, values, mask)

    even, odd = output_project(attended, global_out)
    terms = scatter_sum(even, odd, patches)
    patch_out, last = call(
        block_sum_body, [(terms[0].shape, F32), ((1, terms[0].shape[1]), BF16)]
    )(*terms)
    devices = planes * tp_count
    prev = lax.ppermute(last, ("ctx", "tp"), [(d, d + 1) for d in range(devices - 1)])
    state, normed = call(
        state_body,
        [((byte_count, width), F32), ((byte_count, width), BF16)],
        [pltpu.VMEM((width // LANES, byte_count, LANES), F32)],
    )(patch_out, prev, local_embeds)

    group = min(tp_count, LOCAL_HEADS)
    share = width // devices
    pieces = LOCAL_HEAD_DIM // share
    plane_heads = LOCAL_HEADS // planes
    head = me % group
    gb_all = lax.all_gather(gb, "tp", axis=0, tiled=True)
    head_info = jnp.stack([head, me, (head % plane_heads) * pieces, plane]).astype(jnp.int32)
    gcore = core_grad(head_info, gb_all, local_out)
    plane_pieces, send = local_layer(
        gather(normed, group), gb_all, gcore, local_qkv, head_info, tp_count, planes
    )

    plane_pieces = swap_planes(plane_pieces)
    parts = lax.all_to_all(send, "tp", 0, 0, tiled=True)
    groups = [
        [t for t in range(tp_count) if (t % group) // plane_heads == c] for c in range(planes)
    ]
    flat = share * width // LANES
    out_pieces = pl.pallas_call(
        functools.partial(plane_sum_body, groups, byte_count),
        in_specs=[pl.BlockSpec(memory_space=pltpu.SMEM), pl.BlockSpec(memory_space=pltpu.VMEM)],
        out_shape=[jax.ShapeDtypeStruct((flat, LANES), BF16)] * planes,
        scratch_shapes=[pltpu.VMEM((planes, flat, LANES), F32)],
        compiler_params=params(32),
    )(head_info, parts)
    out_pieces = swap_planes(out_pieces)
    mine = parts
    if group < tp_count:
        mine = lax.dynamic_slice_in_dim(parts, (me // group) * group, group, 0)
    hidden = call(functools.partial(hidden_body, byte_count), [((byte_count, width), BF16)])(
        state, mine, local_out
    )[0]
    grad_out = call(grad_out_body, [((1, share, width), F32)])(*out_pieces)[0]
    turned = call(turn_body, [((tp_count * share, 3 * LOCAL_HEAD_DIM), BF16)])(*plane_pieces)[0]
    grad_qkv = lax.all_to_all(
        turned.reshape(tp_count, share, 3 * LOCAL_HEAD_DIM), "tp", 0, 0, tiled=True
    )
    grad_qkv = call(functools.partial(grad_qkv_body, LOCAL_HEADS), [((1, share, 3 * width), F32)])(
        grad_qkv
    )[0]
    return (hidden, grad_qkv, grad_out)


def solution(mesh):
    in_specs = (
        P(("ctx", "tp"), None),
        P(("ctx", "tp"), None),
        P(None, None, "tp"),
        P("tp", None),
        P(),
        P(),
        P(("ctx", "tp"), None),
    )
    out_specs = (P(("ctx", "tp"), None), P(None, ("ctx", "tp"), None), P(None, ("ctx", "tp"), None))
    return jax.shard_map(
        per_device, mesh=mesh, in_specs=in_specs, out_specs=out_specs, check_vma=False
    )
```

```python
import functools
import math

import jax
import jax.numpy as jnp
from jax import lax
from jax.experimental import pallas as pl
from jax.experimental.pallas import tpu as pltpu
from jax.sharding import PartitionSpec as P

PATCH = 8
HEAD_DIM = 128
LOCAL_HEADS = 8
LOCAL_HEAD_DIM = 128
EPS = 1e-06
F32 = jnp.float32
BF16 = jnp.bfloat16
MIB = 1 << 20
LARGE = 60
TOKEN = jax.ShapeDtypeStruct((8, 128), jnp.float32)
LANES = 128


def params(mib):
    return pltpu.CompilerParams(vmem_limit_bytes=mib * MIB)


def call(body, outs, scratch=(), mib=32):
    return pl.pallas_call(
        body,
        out_shape=[jax.ShapeDtypeStruct(shape, dtype) for shape, dtype in outs],
        scratch_shapes=list(scratch),
        compiler_params=params(mib),
    )


class Held:
    def __init__(self, source, target, sem):
        self.ref, self.copy, self.waited = target, pltpu.make_async_copy(source, target, sem), False
        self.copy.start()

    def __call__(self):
        if not self.waited:
            self.copy.wait()
            self.waited = True
        return self.ref


class Sent:
    def __init__(self, source, target, sem):
        self.ref, self.copy, self.started = source, pltpu.make_async_copy(source, target, sem), False

    def send(self):
        self.copy.start()
        self.started = True


def staged(body, args, sent, outs=(), scratch=(), info=None, mib=16, flops=0, after=None, held=()):
    tokens = [] if after is None else [after]
    counts = [len(args), len(held), len(tokens), len(sent), len(outs)]
    counts += [len(held), len(sent), len(scratch)]

    def kernel(*refs):
        refs = list(refs)
        info_ref = [refs.pop(0)] if info is not None else []
        groups = []
        for count in counts:
            groups.append(refs[:count])
            del refs[:count]
        in_refs, held_far, _, sent_far, out_refs, held_near, sent_near, own = groups
        in_sems, out_sems = refs
        inputs = [Held(f, n, in_sems.at[i]) for i, (f, n) in enumerate(zip(held_far, held_near))]
        outputs = [Sent(n, f, out_sems.at[i]) for i, (f, n) in enumerate(zip(sent_far, sent_near))]
        body(*info_ref, *in_refs, *inputs, *outputs, *out_refs, *own)
        for output in outputs:
            if not output.started:
                output.send()
        for value in inputs:
            value()
        for output in outputs:
            output.copy.wait()

    here, there = pl.BlockSpec(memory_space=pltpu.VMEM), pl.BlockSpec(memory_space=pltpu.HBM)
    free = pl.BlockSpec(memory_space=pl.ANY)
    scalars = [] if info is None else [info]
    return pl.pallas_call(
        kernel,
        in_specs=[pl.BlockSpec(memory_space=pltpu.SMEM)] * len(scalars)
        + [here] * len(args)
        + [free] * (len(held) + len(tokens)),
        out_specs=[there] * len(sent) + [here] * len(outs),
        out_shape=[pltpu.HBM(shape, dtype) for shape, dtype in sent]
        + [jax.ShapeDtypeStruct(shape, dtype) for shape, dtype in outs],
        scratch_shapes=[pltpu.VMEM(value.shape, value.dtype) for value in held]
        + [pltpu.VMEM(shape, dtype) for shape, dtype in sent]
        + list(scratch)
        + [pltpu.SemaphoreType.DMA((max(1, count),)) for count in (len(held), len(sent))],
        compiler_params=params(mib),
        cost_estimate=pl.CostEstimate(flops=flops, bytes_accessed=1 << 22, transcendentals=0),
    )(*scalars, *args, *held, *tokens)


def dot(a, b, dims=((1,), (0,))):
    return lax.dot_general(a, b, (dims, ((), ())), preferred_element_type=F32)


def swap(value, bits):
    count = lax.axis_size("tp")
    return lax.ppermute(value, "tp", [(source, source ^ bits) for source in range(count)])


def block_order(size):
    return list(range(0, size, 2)) + list(range(1, size, 2))


def gather(value, size):
    even = [value] + [swap(value, bits) for bits in range(2, size, 2)]
    return even + [swap(piece, 1) for piece in even]


def tie_body(*refs):
    pass


def tie(value, *after):
    there = pl.BlockSpec(memory_space=pl.ANY)
    return pl.pallas_call(
        tie_body,
        in_specs=[there] * (1 + len(after)),
        out_specs=there,
        out_shape=jax.ShapeDtypeStruct(value.shape, value.dtype),
        input_output_aliases={0: 0},
        compiler_params=params(1),
    )(value, *after)


def preload_body(parts, info_ref, w_ref, _, out_ref, info_out, sems):
    for index in range(info_ref.shape[0]):
        info_out[index] = info_ref[index]
    source = w_ref.at[0] if len(w_ref.shape) == 3 else w_ref
    size = source.shape[0] // parts
    copies = []
    for part in range(parts):
        at = pl.ds(part * size, size)
        copies.append(pltpu.make_async_copy(source.at[at], out_ref.at[at], sems.at[part]))
        copies[-1].start()
    for copy in copies:
        copy.wait()


def preload(weights, info, after, parts=8):
    there = pl.BlockSpec(memory_space=pl.ANY)
    scalar = pl.BlockSpec(memory_space=pltpu.SMEM)
    shape = weights.shape[-2:]
    return pl.pallas_call(
        functools.partial(preload_body, parts),
        in_specs=[scalar, there, there],
        out_specs=[pl.BlockSpec(memory_space=pltpu.VMEM), scalar],
        out_shape=[
            pltpu.VMEM(shape, weights.dtype),
            jax.ShapeDtypeStruct(info.shape, info.dtype),
        ],
        scratch_shapes=[pltpu.SemaphoreType.DMA((parts,))],
        compiler_params=params(50),
        cost_estimate=pl.CostEstimate(
            flops=0, bytes_accessed=2 * math.prod(shape), transcendentals=0
        ),
    )(info, weights, after)


def patch_norm_body(x_ref, out_ref, wide):
    patches = out_ref.shape[0]
    width = x_ref.shape[1]
    total = jnp.zeros((patches, LANES), F32)
    for c in range(width // LANES):
        wide[c] = x_ref[:, c * LANES : (c + 1) * LANES].astype(F32)
    for c in range(width // LANES):
        for b in range(PATCH):
            part = wide[c, pl.ds(b, patches, stride=PATCH), :]
            total += part * part
    scale = lax.rsqrt(jnp.sum(total, axis=-1, keepdims=True) / (PATCH * width) + EPS)
    for b in range(PATCH):
        for c in range(width // LANES):
            part = wide[c, pl.ds(b, patches, stride=PATCH), :]
            at = b * width + c * LANES
            out_ref[:, at : at + LANES] = (part * scale).astype(BF16)


def patch_norm(byte_embeds):
    rows, width = byte_embeds.shape
    return call(
        patch_norm_body,
        [((rows // PATCH, PATCH * width), BF16)],
        [pltpu.VMEM((width // LANES, rows, LANES), F32)],
        16,
    )(byte_embeds)[0]


def stack(refs):
    return jnp.concatenate([ref[...].astype(F32) for ref in refs], axis=0).astype(BF16)


def project_body(count, *refs):
    x_refs, refs = refs[:count], refs[count:]
    first_ref, pass_ref, w_ref, q, kv, passed, held, sems = refs
    kinds, rows, _ = held.shape
    depth = math.gcd(rows, 1024)
    copies = {}
    for c in range(kinds):
        for k in range(0, rows, depth):
            at = pl.ds(k, depth)
            copies[c, k] = pltpu.make_async_copy(
                w_ref.at[c + 1, at], held.at[c, at], sems.at[len(copies)]
            )
            copies[c, k].start()
    x = stack(x_refs)
    passed.ref[...] = pass_ref[...]
    passed.send()
    for c in range(kinds + 1):
        total = None
        for k in range(0, rows, depth):
            if c:
                copies[c - 1, k].wait()
                w = held[c - 1, k : k + depth, :]
            else:
                w = first_ref[k : k + depth, :]
            term = dot(x[:, k : k + depth], w)
            total = term if total is None else total + term
        for h in range(total.shape[1] // HEAD_DIM):
            at = slice(h * HEAD_DIM, (h + 1) * HEAD_DIM)
            part = total[:, at]
            if c < 2:
                part = part * lax.rsqrt(jnp.mean(part * part, axis=-1, keepdims=True) + EPS)
            if c == 0:
                q.ref[:, at] = part.astype(BF16)
            else:
                kv.ref[c - 1, :, at] = part.astype(BF16)
        if c == 0:
            q.send()


def project(pieces, first, weights, passed):
    rows = sum(piece.shape[0] for piece in pieces)
    kinds, deep, width = weights.shape
    here, there = pl.BlockSpec(memory_space=pltpu.VMEM), pl.BlockSpec(memory_space=pltpu.HBM)
    outs = [((rows, width), BF16), ((kinds - 1, rows, width), BF16), (passed.shape, passed.dtype)]
    count = len(pieces)

    def body(*refs):
        in_refs, far, near = refs[: count + 3], refs[count + 3 : count + 6], refs[count + 6 : count + 9]
        held, sems, out_sems = refs[count + 9 :]
        outputs = [Sent(n, f, out_sems.at[i]) for i, (f, n) in enumerate(zip(far, near))]
        project_body(count, *in_refs, *outputs, held, sems)
        outputs[1].send()
        for output in outputs:
            output.copy.wait()

    return pl.pallas_call(
        body,
        in_specs=[here] * (count + 2) + [pl.BlockSpec(memory_space=pl.ANY)],
        out_specs=[there] * 3,
        out_shape=[pltpu.HBM(shape, dtype) for shape, dtype in outs],
        scratch_shapes=[pltpu.VMEM(shape, dtype) for shape, dtype in outs]
        + [
            pltpu.VMEM((kinds - 1, deep, width), BF16),
            pltpu.SemaphoreType.DMA(((kinds - 1) * deep // math.gcd(deep, 1024),)),
            pltpu.SemaphoreType.DMA((3,)),
        ],
        compiler_params=params(40),
    )(*pieces, first, passed, weights)


def heads_of(ref_width):
    return [slice(at, at + HEAD_DIM) for at in range(0, ref_width, HEAD_DIM)]


def last_row(info_ref, rows, tp_count):
    return block_place(info_ref[1] ^ (tp_count - 1), tp_count) * (rows // tp_count) + (
        rows // tp_count - 1
    )


def block_place(bits, size):
    return bits // 2 + (bits % 2) * (size // 2)


def split_den(dens, count):
    high = dens.astype(BF16).astype(F32)
    return high + pltpu.roll(dens - high, count, 1)


def attend_body(tp_count, info_ref, kv_in_ref, q3_ref, q2_ref, mask_ref, *refs):
    q_in, kv_here, back3, back2, top_ref, den_ref, far_top, far_den = refs
    back3_ref, back2_ref = back3.ref, back2.ref
    q_ref, kv_ref = q_in(), kv_here()
    rows, width = q_ref.shape
    root = 1.0 / math.sqrt(HEAD_DIM)
    allowed = mask_ref[...] > 0
    linked = jnp.where(info_ref[3] % 2 == 1, 1.0, 0.0)
    heads = heads_of(width)
    count = len(heads)
    lane = lax.broadcasted_iota(jnp.int32, (rows, LANES), 1)
    dens = jnp.zeros((rows, LANES), F32)
    far_dens = [dens, dens]
    for h, at in enumerate(heads):
        q, k, v = q_ref[:, at], kv_ref[0, :, at], kv_ref[1, :, at]
        k_in, v_in = kv_in_ref[0, :, at], kv_in_ref[1, :, at]
        own = jnp.where(allowed, jnp.exp(dot(q, k, ((1,), (1,))) * root), 0.0)
        other = jnp.exp(dot(q, k_in, ((1,), (1,))) * root) * linked
        top_ref[:, at] = dot(own.astype(BF16), v) + dot(other.astype(BF16), v_in)
        den = jnp.sum(own, axis=-1, keepdims=True) + jnp.sum(other, axis=-1, keepdims=True)
        dens = jnp.where(lane == h, den, dens)
        for index, far_ref in enumerate((q3_ref, q2_ref)):
            far = far_ref[:, at]
            own = jnp.exp(dot(far, k, ((1,), (1,))) * root)
            other = jnp.exp(dot(far, k_in, ((1,), (1,))) * root)
            far_top[index, :, at] = dot(own.astype(BF16), v) + dot(other.astype(BF16), v_in)
            den = jnp.sum(own, axis=-1, keepdims=True) + jnp.sum(other, axis=-1, keepdims=True)
            far_dens[index] = jnp.where(lane == h, den, far_dens[index])
    den_ref[...] = dens
    last = last_row(info_ref, rows, tp_count)
    edge_rows = EDGE_ROWS

    def fill(ref, at, top, den):
        ref[at, :width] = top.astype(BF16)
        ref[at, width:] = split_den(den, count).astype(BF16)

    def spread(row):
        return jnp.broadcast_to(row, (edge_rows, row.shape[1]))

    far_den[...] = far_dens[1]
    fill(back3_ref, slice(0, rows), far_top[0], far_dens[0])
    fill(
        back3_ref,
        slice(rows, rows + edge_rows),
        spread(far_top[1, pl.ds(last, 1), :]),
        spread(far_den[pl.ds(last, 1), :]),
    )
    back3.send()
    fill(back2_ref, slice(0, rows), far_top[1], far_dens[1])
    fill(
        back2_ref,
        slice(rows, rows + edge_rows),
        spread(top_ref[pl.ds(last, 1), :]),
        spread(den_ref[pl.ds(last, 1), :]),
    )


EDGE_ROWS = 16


def attend_paired(info, q, kv, mask, tp_count):
    kv_in = lax.ppermute(kv, "ctx", [(0, 1), (2, 3)])
    far = [lax.ppermute(q, "ctx", [(c, 1)]) for c in (3, 2)]
    rows, width = q.shape
    back = ((rows + EDGE_ROWS, width + LANES), BF16)
    back3, back2, top, den = staged(
        functools.partial(attend_body, tp_count),
        [kv_in, *far, mask],
        [back, back],
        [((rows, width), F32), ((rows, LANES), F32)],
        [pltpu.VMEM((2, rows, width), F32), pltpu.VMEM((rows, LANES), F32)],
        info,
        held=[q, kv],
    )
    back3 = lax.ppermute(back3, "ctx", [(1, 3)])
    back2 = lax.ppermute(back2, "ctx", [(c, c + 1) for c in range(3)])
    return top, den, [back2, back3]


def attend_all_body(tp_count, info_ref, mask_ref, q_ref, k_ref, v_ref, top_ref, den_ref, edge_ref):
    rows, width = q_ref.shape
    allowed = mask_ref[...] > 0
    lane = lax.broadcasted_iota(jnp.int32, den_ref.shape, 1)
    dens = jnp.zeros(den_ref.shape, F32)
    heads = heads_of(width)
    for h, at in enumerate(heads):
        scores = dot(q_ref[:, at], k_ref[:, at], ((1,), (1,))) * (1.0 / math.sqrt(HEAD_DIM))
        expo = jnp.where(allowed, jnp.exp(scores), 0.0)
        top_ref[:, at] = dot(expo.astype(BF16), v_ref[:, at])
        dens = jnp.where(lane == h, jnp.sum(expo, axis=-1, keepdims=True), dens)
    den_ref[...] = dens
    last = last_row(info_ref, rows, tp_count)
    count = edge_ref.shape[0]
    top = jnp.broadcast_to(top_ref[pl.ds(last, 1), :], (count, width))
    den = jnp.broadcast_to(den_ref[pl.ds(last, 1), :], (count, LANES))
    edge_ref[:, :width] = top.astype(BF16)
    edge_ref[:, width:] = split_den(den, len(heads)).astype(BF16)


def attend_all(info, q, kv, mask, tp_count):
    planes = lax.axis_size("ctx")
    keys = lax.all_gather(kv[0], "ctx", axis=0, tiled=True)
    values = lax.all_gather(kv[1], "ctx", axis=0, tiled=True)
    rows, width = q.shape
    here = pl.BlockSpec(memory_space=pltpu.VMEM)
    outs = [((rows, width), F32), ((rows, LANES), F32), ((EDGE_ROWS, width + LANES), BF16)]
    top, den, edge = pl.pallas_call(
        functools.partial(attend_all_body, tp_count),
        in_specs=[pl.BlockSpec(memory_space=pltpu.SMEM)] + [here] * 4,
        out_specs=[here] * 3,
        out_shape=[jax.ShapeDtypeStruct(shape, dtype) for shape, dtype in outs],
        compiler_params=params(48),
    )(info, mask, q, keys, values)
    back = jnp.concatenate([jnp.zeros((rows, width + LANES), BF16), edge], axis=0)
    return top, den, [lax.ppermute(back, "ctx", [(c, c + 1) for c in range(planes - 1)])]


def output_body(count, tp_count, info_ref, *refs):
    back_refs = refs[:count]
    top_ref, den_ref, w_ref, odd_out, even_ref, whole, odd_ref, out_sems = refs[count:]
    depth = w_ref.shape[0]
    blocks, _, step = odd_ref.shape
    rows = top_ref.shape[0]
    heads = heads_of(depth)
    edges = []

    def column(ref, at, h):
        high, low = depth + h, depth + len(heads) + h
        return ref[at, high : high + 1].astype(F32) + ref[at, low : low + 1].astype(F32)

    for h, lanes in enumerate(heads):
        top, den = top_ref[:, lanes], den_ref[:, h : h + 1]
        edge, edge_den = 0.0, 0.0
        for index, ref in enumerate(back_refs):
            mine, mine_den = ref[:rows, lanes].astype(F32), column(ref, slice(0, rows), h)
            if index == 0:
                taken = info_ref[3] == 2
                mine, mine_den = jnp.where(taken, mine, 0.0), jnp.where(taken, mine_den, 0.0)
            top += mine
            den += mine_den
            edge += ref[rows:, lanes].astype(F32)
            edge_den += column(ref, slice(rows, None), h)
        whole[:, lanes] = top / den
        edges.append(jnp.where(edge_den > 0, edge / jnp.where(edge_den > 0, edge_den, 1.0), 0.0))
    edge = jnp.concatenate(edges, axis=1)[:1]
    patches = rows // tp_count
    me = info_ref[1]
    before = []
    for bits in block_order(tp_count):
        peer = me ^ bits
        source = block_place(me ^ ((peer + tp_count - 1) % tp_count), tp_count)
        row = whole[pl.ds(source * patches + patches - 1, 1), :]
        before.append(jnp.where(peer == 0, edge, row))
    for index, row in enumerate(before):
        at = index * patches + patches - 1
        whole[at : at + 1, :] = row
    attended = whole[...].astype(BF16)
    half = rows // 2
    sends = []
    for n in range(blocks):
        at = pl.ds(n * step, step)
        out = dot(attended, w_ref[:, at])
        odd_ref[n] = out[half:].astype(BF16)
        sends.append(pltpu.make_async_copy(odd_ref.at[n], odd_out.at[:, at], out_sems.at[n]))
        sends[-1].start()
        even_ref[:, at] = out[:half].astype(BF16)
    for copy in sends:
        copy.wait()


def output_project(info, top, den, back, weights, tp_count):
    rows, depth = top.shape
    width = weights.shape[1]
    step = min(width, 1024)
    here, there = pl.BlockSpec(memory_space=pltpu.VMEM), pl.BlockSpec(memory_space=pltpu.HBM)
    blocks = width // step
    odd, even = pl.pallas_call(
        functools.partial(output_body, len(back), tp_count),
        in_specs=[pl.BlockSpec(memory_space=pltpu.SMEM)] + [here] * (3 + len(back)),
        out_specs=[there, here],
        out_shape=[
            pltpu.HBM((rows // 2, width), BF16),
            jax.ShapeDtypeStruct((rows // 2, width), BF16),
        ],
        scratch_shapes=[
            pltpu.VMEM((rows, depth), F32),
            pltpu.VMEM((blocks, rows // 2, step), BF16),
            pltpu.SemaphoreType.DMA((blocks,)),
        ],
        compiler_params=params(16),
    )(info, *back, top, den, weights)
    return even, odd


def pair_sum_body(mine_ref, other_ref, own_ref, *send_refs):
    patches = own_ref.shape[0]
    total = mine_ref[...].astype(F32) + other_ref[...].astype(F32)
    own_ref[...] = total[:patches]
    for index, ref in enumerate(send_refs):
        ref[...] = total[(index + 1) * patches : (index + 2) * patches].astype(BF16)


def scatter_sum(even, odd, patches):
    blocks = even.shape[0] // patches
    block = (patches, even.shape[1])
    pieces = call(pair_sum_body, [(block, F32)] + [(block, BF16)] * (blocks - 1))(
        even, swap(odd, 1)
    )
    return [pieces[0]] + [swap(piece, 2 * (index + 1)) for index, piece in enumerate(pieces[1:])]


def state_body(count, *refs):
    terms = refs[:count]
    local_ref, normed, state_out, normed_ref, wide = refs[count:]
    patches = terms[0].shape[0]
    width = normed_ref.shape[1]
    chunks = width // LANES
    for b in range(PATCH):
        at = slice(b * width, (b + 1) * width)
        total = terms[0][:, at]
        for term in terms[1:]:
            total += term[:, at].astype(F32)
        part = pltpu.roll(total.astype(BF16).astype(F32), 1, 0)
        for c in range(chunks):
            wide[c, pl.ds(b, patches, stride=PATCH), :] = part[:, c * LANES : (c + 1) * LANES]
    context = jnp.concatenate([wide[c] for c in range(chunks)], axis=1)
    state = local_ref[...].astype(F32) + context
    state_out.ref[...] = state
    state_out.send()
    mean = jnp.mean(state * state, axis=-1, keepdims=True)
    normed_ref[...] = (state * lax.rsqrt(mean + EPS)).astype(BF16)
    normed.ref[...] = normed_ref[...]


def byte_state(terms, local_embeds, after):
    rows, width = local_embeds.shape
    normed, state, normed_near = staged(
        functools.partial(state_body, len(terms)),
        [*terms, local_embeds],
        [((rows, width), BF16), ((rows, width), F32)],
        [((rows, width), BF16)],
        [pltpu.VMEM((width // LANES, rows, LANES), F32)],
        after=after,
    )
    return state, normed, normed_near


def unit(x):
    scale = lax.rsqrt(jnp.mean(x * x, axis=-1, keepdims=True) + EPS)
    return x * scale, scale


def unit_back(grad, y, scale):
    return scale * (grad - y * jnp.mean(grad * y, axis=-1, keepdims=True))


def prepare_body(parts, info_ref, gb_ref, wq_ref, wk_ref, wv_ref, wo_ref, *refs):
    weights_ref = refs[0]
    d = LOCAL_HEAD_DIM
    rows = refs[1].shape[0] // len(parts[0])
    for kind, ref in enumerate((wq_ref, wk_ref, wv_ref)):
        weights_ref[:, kind * d : (kind + 1) * d] = ref[0]
    for index, part in enumerate(parts):
        out_ref, core_ref = refs[1 + 2 * index : 3 + 2 * index]
        for place, bits in enumerate(part):
            at = pl.multiple_of((info_ref[1] ^ bits) * rows, rows)
            out_ref[place * rows : (place + 1) * rows, :] = gb_ref[pl.ds(at, rows), :]
        core_ref[...] = dot(out_ref[...], wo_ref[0], ((1,), (1,))).astype(BF16)


def prepare(info, gb_all, local_qkv, local_out, rows, parts):
    width = gb_all.shape[1]
    d = LOCAL_HEAD_DIM
    heads = LOCAL_HEADS

    def qkv_spec(kind):
        return pl.BlockSpec((1, width, d), lambda i, info: (0, 0, kind * heads + info[0]))

    outs = [(width, 3 * d)]
    for part in parts:
        outs += [(len(part) * rows, width), (len(part) * rows, d)]
    weights, *blocks = pl.pallas_call(
        functools.partial(prepare_body, parts),
        grid_spec=pltpu.PrefetchScalarGridSpec(
            num_scalar_prefetch=1,
            grid=(1,),
            in_specs=[
                pl.BlockSpec(gb_all.shape, lambda i, info: (0, 0)),
                qkv_spec(0),
                qkv_spec(1),
                qkv_spec(2),
                pl.BlockSpec((1, d, width), lambda i, info: (0, info[0], 0)),
            ],
            out_specs=[pl.BlockSpec(shape, lambda i, info: (0, 0)) for shape in outs],
        ),
        out_shape=[jax.ShapeDtypeStruct(shape, BF16) for shape in outs],
        compiler_params=params(LARGE),
    )(info, gb_all, local_qkv, local_qkv, local_qkv, local_out)
    return weights, blocks[0::2], blocks[1::2]


def window(rows):
    row = lax.broadcasted_iota(jnp.int32, (rows, rows), 0)
    column = lax.broadcasted_iota(jnp.int32, (rows, rows), 1)
    return (row // PATCH == column // PATCH) & (column <= row)


def core_weights(qkv, allowed):
    d = LOCAL_HEAD_DIM
    q, q_scale = unit(qkv[:, :d])
    k, k_scale = unit(qkv[:, d : 2 * d])
    qb, kb, vb = q.astype(BF16), k.astype(BF16), qkv[:, 2 * d :].astype(BF16)
    expo = jnp.where(allowed, jnp.exp(dot(qb, kb, ((1,), (1,))) * (1.0 / math.sqrt(d))), 0.0)
    weight = expo / jnp.sum(expo, axis=-1, keepdims=True)
    return (q, q_scale, qb), (k, k_scale, kb), vb, weight


def core_forward(weight, vb):
    return dot(weight.astype(BF16), vb).astype(BF16)


def core_backward(query, key, vb, weight, gradb):
    q, q_scale, qb = query
    k, k_scale, kb = key
    grad_v = dot(weight.astype(BF16), gradb, ((0,), (0,)))
    grad_w = dot(gradb, vb, ((1,), (1,)))
    mean = jnp.sum(weight * grad_w, axis=-1, keepdims=True)
    grad_s = (weight * (grad_w - mean) * (1.0 / math.sqrt(LOCAL_HEAD_DIM))).astype(BF16)
    grad_q = unit_back(dot(grad_s, kb), q, q_scale)
    grad_k = unit_back(dot(grad_s, qb, ((0,), (0,))), k, k_scale)
    return jnp.concatenate([grad_q, grad_k, grad_v], axis=1).astype(BF16)


def chunks_in(piece):
    return jnp.concatenate(
        [piece[:, at : at + LANES] for at in range(0, piece.shape[1], LANES)], axis=0
    )


def chunks_out(value, rows):
    return jnp.concatenate(
        [value[at : at + rows] for at in range(0, value.shape[0], rows)], axis=1
    )


def rows_of(refs):
    return jnp.concatenate([ref[...] for ref in refs], axis=0)


def local_body(count, *refs):
    x_refs, refs = refs[:count], refs[count:]
    (gb_ref, core_ref, w_ref), refs = refs[:3], refs[3:]
    carry, (gqkv_ref, gout_ref, ab_ref, token_ref) = refs[:-4], refs[-4:]
    token_ref[...] = jnp.zeros_like(token_ref)
    gqkv, gout, abs_ = local_grads(x_refs, gb_ref, core_ref, w_ref, carry)
    gqkv_ref[...] = gqkv
    gout_ref[...] = gout
    ab_ref[...] = jnp.concatenate(abs_, axis=0)


def local_grads(x_refs, gb_ref, core_ref, w_ref, carry):
    x = rows_of(x_refs)
    rows = x_refs[0].shape[0]
    allowed = window(rows)
    qkv = dot(x, w_ref[...])
    abs_, gqs = [], []
    for index in range(len(x_refs)):
        at = slice(index * rows, (index + 1) * rows)
        query, key, vb, weight = core_weights(qkv[at], allowed)
        abs_.append(core_forward(weight, vb))
        gqs.append(core_backward(query, key, vb, weight, core_ref[at, :]))
    gqkv = dot(jnp.concatenate(gqs, axis=0), x, ((0,), (0,)))
    gout = dot(jnp.concatenate(abs_, axis=0), gb_ref[...], ((0,), (0,)))
    if carry:
        gqkv += carry[0][...]
        gout += carry[1][...]
    return gqkv, gout, abs_


def local_last_body(count, info_ref, *refs):
    x_refs, refs = refs[:count], refs[count:]
    gb_ref, core_ref, w_ref, *carry, ab0_ref, gqkv_out, message, kept_ref, held = refs
    gqkv, gout, abs_ = local_grads(x_refs, gb_ref, core_ref, w_ref, carry)
    gqkv_out.ref[...] = gqkv.T.astype(BF16)
    gqkv_out.send()
    held[...] = gout
    rows = x_refs[0].shape[0]
    message.ref[:rows, :] = ab0_ref[rows:, :]
    for index, ab in enumerate(abs_):
        message.ref[(index + 1) * rows : (index + 2) * rows, :] = ab
    deep = kept_ref.shape[1]
    piece_rows = deep * LANES // held.shape[1]
    for k in range(held.shape[0] // piece_rows):
        at = pl.multiple_of((info_ref[2] ^ k) * piece_rows, piece_rows)
        piece = chunks_in(held[pl.ds(at, piece_rows), :]).astype(BF16)
        if k % 2:
            start = (count + 1) * rows + k // 2 * deep
            message.ref[start : start + deep, :] = piece
        else:
            kept_ref[k // 2] = piece


def relay_body(count, ab0_ref, ab1_ref, kept_ref, there_ref, *refs):
    rows = ab0_ref.shape[0] // 2
    deep = kept_ref.shape[1]
    *messages, own = refs
    for k, message in enumerate([own, *messages]):
        parts = []
        if k <= count:
            parts.append(ab0_ref[:rows, :] if k == 0 else ab1_ref[(k - 1) * rows : k * rows, :])
            parts.append(there_ref[k * rows : (k + 1) * rows, :])
        if k < kept_ref.shape[0]:
            start = (count + 1) * rows + k * deep
            parts.append(kept_ref[k])
            parts.append(there_ref[start : start + deep, :])
        at = 0
        target = message if k == 0 else message.ref
        for part in parts:
            target[at : at + part.shape[0], :] = part
            at += part.shape[0]
        if k:
            message.send()


def local_layer(normed, normed_near, info, parts, gbs, cores, weights, rounds, tp_count):
    rows, width = normed.shape
    d = LOCAL_HEAD_DIM
    near = [swap(normed, bits) for bits in parts[1]]
    count = len(near)
    totals = [((3 * d, width), F32), ((d, width), F32)]

    def step(index, xs, carry):
        return staged(
            functools.partial(local_body, len(xs)),
            [*xs, gbs[index], cores[index], weights, *carry],
            [],
            [*totals, ((len(xs) * rows, d), BF16), (TOKEN.shape, F32)],
            flops=1 << 34,
            mib=20,
        )

    *carry, ab0, done = step(0, [normed_near, swap(normed, 1)], [])
    near = [tie(block, done) for block in near]
    far = [swap(block, 1) for block in near]
    *carry, ab1, _ = step(1, near, carry)
    deep = d // rounds * width // LANES
    halves = rounds // 2
    length = (count + 1) * rows + halves * deep
    grad_qkv, message, kept = staged(
        functools.partial(local_last_body, count),
        [*far, gbs[2], cores[2], weights, *carry, ab0],
        [((width, 3 * d), BF16), ((length, d), BF16)],
        [((halves, deep, d), BF16)],
        [pltpu.VMEM((d, width), F32)],
        info,
        flops=1 << 34,
        mib=20,
    )
    sizes = [2 * rows * (k <= count) + 2 * deep * (k < halves) for k in range(max(count + 1, halves))]
    *messages, own = staged(
        functools.partial(relay_body, count),
        [ab0, ab1, kept, swap(message, 1)],
        [((size, d), BF16) for size in sizes[1:]],
        [((sizes[0], d), BF16)],
    )
    messages = [own] + [swap(value, 2 * (k + 1)) for k, value in enumerate(messages)]
    return messages, grad_qkv


def hidden_body(heads, count, info_ref, state_ref, w_ref, *refs):
    *messages, out_ref, token_ref = refs
    token_ref[...] = jnp.zeros_like(token_ref)
    rows = state_ref.shape[0]
    d = LOCAL_HEAD_DIM
    total = state_ref[...]
    for bits in range(2 * count + 2):
        at = bits % 2 * rows
        head = heads(info_ref[1] ^ bits)
        weights = w_ref[0, pl.ds(pl.multiple_of(head * d, d), d), :]
        total += dot(messages[bits // 2][at : at + rows, :], weights)
    out_ref[...] = total.astype(BF16)


def planes_body(planes, count, rounds, rows, info_ref, *refs):
    half = rounds // 2
    messages, outs, held = refs[:half], refs[half:-1], refs[-1]
    deep = held.shape[1]
    for k in range(rounds):
        start = 2 * rows * (k // 2 <= count) + k % 2 * deep
        held[k] = messages[k // 2][start : start + deep, :].astype(F32)
    for z, out in enumerate(outs):
        total = None
        for outer in range(rounds // planes):
            term = held[info_ref[2] ^ ((info_ref[3] ^ z) + outer * planes)]
            total = term if total is None else total + term
        out.ref[...] = total.astype(BF16)
        out.send()


def final_body(heads, parts_ref, *refs):
    *terms, gqkv_ref, gout_ref = refs
    gout = sum(term[...].astype(F32) for term in terms)
    gout_ref[0] = chunks_out(gout, gout_ref.shape[1])
    d = LOCAL_HEAD_DIM
    tp_count = len(heads)
    for h in range(LOCAL_HEADS):
        total = None
        for source in range(parts_ref.shape[0]):
            if heads[source % tp_count] == h:
                term = parts_ref[source].astype(F32)
                total = term if total is None else total + term
        for kind in range(3):
            at = (kind * LOCAL_HEADS + h) * d
            gqkv_ref[0, :, at : at + d] = total[:, kind * d : (kind + 1) * d]


def swap_planes(pieces):
    count = len(pieces)
    return [pieces[0]] + [
        lax.ppermute(pieces[k], "ctx", [(c, c ^ k) for c in range(count)]) for k in range(1, count)
    ]


def per_device(byte_embeds, local_embeds, global_qkv, global_out, local_qkv, local_out, cotangent):
    byte_count, width = byte_embeds.shape
    patches = byte_count // PATCH
    planes, tp_count = lax.axis_size("ctx"), lax.axis_size("tp")
    plane, me = lax.axis_index("ctx"), lax.axis_index("tp")
    order = block_order(tp_count)
    shard_rows = tp_count * patches
    devices = planes * tp_count

    group = min(tp_count, LOCAL_HEADS)
    share = width // devices
    rounds = LOCAL_HEAD_DIM // share
    plane_heads = LOCAL_HEADS // planes

    def head_of(t):
        return (t % rounds) % planes * plane_heads + t // rounds

    heads = [head_of(t) for t in range(tp_count)]
    head_info = jnp.stack([head_of(me), me, me % rounds, plane]).astype(jnp.int32)

    patch_in = patch_norm(byte_embeds)
    mine = swap(patch_in, 1)
    weights_in, head_info = preload(global_qkv, head_info, mine)
    even = [tie(swap(patch_in, bits), head_info) for bits in range(2, tp_count, 2)]
    pieces = [patch_in, *even, mine, *(swap(piece, 1) for piece in even)]
    q, kv, gb = project(pieces, weights_in, global_qkv, cotangent)

    place = (
        (me ^ jnp.array(order, jnp.int32))[:, None] * patches
        + jnp.arange(patches, dtype=jnp.int32)[None, :]
    ).reshape(-1)
    weights_out, head_info = preload(global_out, head_info, q)
    if planes == 4:
        mask = (place[None, :] <= place[:, None]).astype(F32)
        top, den, back = attend_paired(
            head_info, q, kv, mask, tp_count
        )
    else:
        key_place = (
            jnp.arange(planes, dtype=jnp.int32)[:, None] * shard_rows + place[None, :]
        ).reshape(-1)
        mask = (key_place[None, :] <= (plane * shard_rows + place)[:, None]).astype(F32)
        top, den, back = attend_all(head_info, q, kv, mask, tp_count)

    even, odd = output_project(head_info, top, den, back, weights_out, tp_count)

    parts = [[0, 1], list(range(2, group, 2)), list(range(3, group, 2))]
    gb_all = lax.all_gather(gb, "tp", axis=0, tiled=True)
    weights, gbs, cores = prepare(head_info, gb_all, local_qkv, local_out, byte_count, parts)
    state, normed, normed_near = byte_state(scatter_sum(even, odd, patches), local_embeds, cores[0])
    messages, grad_qkv = local_layer(
        normed, normed_near, head_info, parts, gbs, cores, weights, rounds, tp_count
    )
    grad_qkv = lax.all_to_all(grad_qkv, ("ctx", "tp"), 0, 0, tiled=True)
    flat = (share * width // LANES, LANES)
    count = group // 2 - 1
    out_pieces = staged(
        functools.partial(planes_body, planes, count, rounds, byte_count),
        messages[: rounds // 2],
        [(flat, BF16)] * planes,
        scratch=[pltpu.VMEM((rounds,) + flat, F32)],
        info=head_info,
    )
    out_pieces = swap_planes(out_pieces)
    here = pl.BlockSpec(memory_space=pltpu.VMEM)
    hidden, done = pl.pallas_call(
        functools.partial(hidden_body, head_of, count),
        in_specs=[pl.BlockSpec(memory_space=pltpu.SMEM)] + [here] * (3 + count),
        out_specs=[here, here],
        out_shape=[jax.ShapeDtypeStruct((byte_count, width), BF16), TOKEN],
        compiler_params=params(LARGE),
    )(head_info, state, local_out, *messages[: count + 1])
    out_pieces[0] = tie(out_pieces[0], done)
    grad_qkv, grad_out = call(
        functools.partial(final_body, heads),
        [((1, share, 3 * width), F32), ((1, share, width), F32)],
        mib=LARGE,
    )(grad_qkv.reshape(devices, share, 3 * LOCAL_HEAD_DIM), *out_pieces)
    return (hidden, grad_qkv, grad_out)


def solution(mesh):
    in_specs = (
        P(("ctx", "tp"), None),
        P(("ctx", "tp"), None),
        P(None, None, "tp"),
        P("tp", None),
        P(),
        P(),
        P(("ctx", "tp"), None),
    )
    out_specs = (P(("ctx", "tp"), None), P(None, ("ctx", "tp"), None), P(None, ("ctx", "tp"), None))
    return jax.shard_map(
        per_device, mesh=mesh, in_specs=in_specs, out_specs=out_specs, check_vma=False
    )
```

```python
import functools
import math

import jax
import jax.numpy as jnp
from jax import lax
from jax.experimental import pallas as pl
from jax.experimental.pallas import tpu as pltpu
from jax.sharding import PartitionSpec as P

PATCH = 8
HEAD_DIM = 128
LOCAL_HEADS = 8
LOCAL_HEAD_DIM = 128
EPS = 1e-06
F32 = jnp.float32
BF16 = jnp.bfloat16
MIB = 1 << 20
LARGE = 60
TOKEN = pltpu.VMEM((8, 128), jnp.float32)
LANES = 128
EDGE_ROWS = 16


def params(mib):
    return pltpu.CompilerParams(vmem_limit_bytes=mib * MIB)


def call(body, outs, scratch=(), mib=32):
    return pl.pallas_call(
        body,
        out_shape=[out if out is TOKEN else jax.ShapeDtypeStruct(*out) for out in outs],
        scratch_shapes=list(scratch),
        compiler_params=params(mib),
    )


class Held:
    def __init__(self, source, target, sem):
        self.ref, self.copy, self.waited = target, pltpu.make_async_copy(source, target, sem), False
        self.copy.start()

    def __call__(self):
        if not self.waited:
            self.copy.wait()
            self.waited = True
        return self.ref


class Sent:
    def __init__(self, source, target, sem):
        self.ref, self.copy, self.started = source, pltpu.make_async_copy(source, target, sem), False

    def send(self):
        self.copy.start()
        self.started = True


def staged(body, args, sent, outs=(), scratch=(), info=None, mib=16, flops=0, after=None, held=()):
    tokens = [] if after is None else [after]
    counts = [len(args), len(held), len(tokens), len(sent), len(outs)]
    counts += [len(held), len(sent), len(scratch)]

    def kernel(*refs):
        refs = list(refs)
        info_ref = [refs.pop(0)] if info is not None else []
        groups = []
        for count in counts:
            groups.append(refs[:count])
            del refs[:count]
        in_refs, held_far, _, sent_far, out_refs, held_near, sent_near, own = groups
        in_sems, out_sems = refs
        inputs = [Held(f, n, in_sems.at[i]) for i, (f, n) in enumerate(zip(held_far, held_near))]
        outputs = [Sent(n, f, out_sems.at[i]) for i, (f, n) in enumerate(zip(sent_far, sent_near))]
        body(*info_ref, *in_refs, *inputs, *outputs, *out_refs, *own)
        for output in outputs:
            if not output.started:
                output.send()
        for value in inputs:
            value()
        for output in outputs:
            output.copy.wait()

    here, there = pl.BlockSpec(memory_space=pltpu.VMEM), pl.BlockSpec(memory_space=pltpu.HBM)
    free = pl.BlockSpec(memory_space=pl.ANY)
    scalars = [] if info is None else [info]
    return pl.pallas_call(
        kernel,
        in_specs=[pl.BlockSpec(memory_space=pltpu.SMEM)] * len(scalars)
        + [here] * len(args)
        + [free] * (len(held) + len(tokens)),
        out_specs=[there] * len(sent) + [here] * len(outs),
        out_shape=[pltpu.HBM(shape, dtype) for shape, dtype in sent]
        + [out if out is TOKEN else jax.ShapeDtypeStruct(*out) for out in outs],
        scratch_shapes=[pltpu.VMEM(value.shape, value.dtype) for value in held]
        + [pltpu.VMEM(shape, dtype) for shape, dtype in sent]
        + list(scratch)
        + [pltpu.SemaphoreType.DMA((max(1, count),)) for count in (len(held), len(sent))],
        compiler_params=params(mib),
        cost_estimate=pl.CostEstimate(flops=flops, bytes_accessed=1 << 22, transcendentals=0),
    )(*scalars, *args, *held, *tokens)


def dot(a, b, dims=((1,), (0,))):
    return lax.dot_general(a, b, (dims, ((), ())), preferred_element_type=F32)


def swap(value, bits):
    count = lax.axis_size("tp")
    return lax.ppermute(value, "tp", [(source, source ^ bits) for source in range(count)])


def block_order(size):
    return list(range(0, size, 2)) + list(range(1, size, 2))


def gather(value, size):
    even = [value] + [swap(value, bits) for bits in range(2, size, 2)]
    return even + [swap(piece, 1) for piece in even]


def tie_body(*refs):
    pass


def tie(value, *after, mib=1):
    there = pl.BlockSpec(memory_space=pl.ANY)
    return pl.pallas_call(
        tie_body,
        in_specs=[there] * (1 + len(after)),
        out_specs=there,
        out_shape=jax.ShapeDtypeStruct(value.shape, value.dtype),
        input_output_aliases={0: 0},
        compiler_params=params(mib),
    )(value, *after)


def preload_body(parts, info_ref, w_ref, _, out_ref, info_out, sems):
    for index in range(info_ref.shape[0]):
        info_out[index] = info_ref[index]
    source = w_ref.at[0] if len(w_ref.shape) == 3 else w_ref
    size = source.shape[0] // parts
    copies = []
    for part in range(parts):
        at = pl.ds(part * size, size)
        copies.append(pltpu.make_async_copy(source.at[at], out_ref.at[at], sems.at[part]))
        copies[-1].start()
    for copy in copies:
        copy.wait()


def preload(weights, info, after, parts=8):
    there = pl.BlockSpec(memory_space=pl.ANY)
    scalar = pl.BlockSpec(memory_space=pltpu.SMEM)
    shape = weights.shape[-2:]
    return pl.pallas_call(
        functools.partial(preload_body, parts),
        in_specs=[scalar, there, there],
        out_specs=[pl.BlockSpec(memory_space=pltpu.VMEM), scalar],
        out_shape=[
            pltpu.VMEM(shape, weights.dtype),
            jax.ShapeDtypeStruct(info.shape, info.dtype),
        ],
        scratch_shapes=[pltpu.SemaphoreType.DMA((parts,))],
        compiler_params=params(50),
        cost_estimate=pl.CostEstimate(
            flops=0, bytes_accessed=2 * math.prod(shape), transcendentals=0
        ),
    )(info, weights, after)


def patch_norm_body(x_ref, out_ref, wide):
    patches = out_ref.shape[0]
    width = x_ref.shape[1]
    total = jnp.zeros((patches, LANES), F32)
    for c in range(width // LANES):
        wide[c] = x_ref[:, c * LANES : (c + 1) * LANES].astype(F32)
    for c in range(width // LANES):
        for b in range(PATCH):
            part = wide[c, pl.ds(b, patches, stride=PATCH), :]
            total += part * part
    scale = lax.rsqrt(jnp.sum(total, axis=-1, keepdims=True) / (PATCH * width) + EPS)
    for b in range(PATCH):
        for c in range(width // LANES):
            part = wide[c, pl.ds(b, patches, stride=PATCH), :]
            at = b * width + c * LANES
            out_ref[:, at : at + LANES] = (part * scale).astype(BF16)


def patch_norm(byte_embeds):
    rows, width = byte_embeds.shape
    return call(
        patch_norm_body,
        [((rows // PATCH, PATCH * width), BF16)],
        [pltpu.VMEM((width // LANES, rows, LANES), F32)],
        16,
    )(byte_embeds)[0]


def stack(refs):
    return jnp.concatenate([ref[...].astype(F32) for ref in refs], axis=0).astype(BF16)


def project_body(count, tp_count, info_ref, *refs):
    x_refs, refs = refs[:count], refs[count:]
    first_ref, pass_ref, w_ref, q, kv, passed, held, wide, sems = refs
    kinds, rows, _ = held.shape
    depth = math.gcd(rows, 1024)
    copies = {}
    for c in range(kinds):
        for k in range(0, rows, depth):
            at = pl.ds(k, depth)
            copies[c, k] = pltpu.make_async_copy(
                w_ref.at[c + 1, at], held.at[c, at], sems.at[len(copies)]
            )
            copies[c, k].start()
    x = stack(x_refs)
    count_rows = x.shape[0]
    passed.ref[...] = pass_ref[...]
    passed.send()
    for c in range(kinds + 1):
        total = None
        for k in range(0, rows, depth):
            if c:
                copies[c - 1, k].wait()
                w = held[c - 1, k : k + depth, :]
            else:
                w = first_ref[k : k + depth, :]
            term = dot(x[:, k : k + depth], w)
            total = term if total is None else total + term
        for h in range(total.shape[1] // HEAD_DIM):
            at = slice(h * HEAD_DIM, (h + 1) * HEAD_DIM)
            part = total[:, at]
            if c < 2:
                part = part * lax.rsqrt(jnp.mean(part * part, axis=-1, keepdims=True) + EPS)
            if c == 0:
                wide[:, at] = part
            else:
                kv.ref[(c - 1) * count_rows : c * count_rows, at] = part.astype(BF16)
        if c == 0:
            q.ref[...] = wide[...].astype(BF16)
            q.send()
            last = wide[pl.ds(last_row(info_ref, count_rows, tp_count), 1), :]
            spread = jnp.broadcast_to(last, (EDGE_ROWS, last.shape[1]))
            kv.ref[kinds * count_rows :, :] = spread.astype(BF16)


def project(info, pieces, first, weights, passed, tp_count):
    rows = sum(piece.shape[0] for piece in pieces)
    kinds, deep, width = weights.shape
    here, there = pl.BlockSpec(memory_space=pltpu.VMEM), pl.BlockSpec(memory_space=pltpu.HBM)
    outs = [((rows, width), BF16), (((kinds - 1) * rows + EDGE_ROWS, width), BF16)]
    outs.append((passed.shape, passed.dtype))
    count = len(pieces)

    def body(*refs):
        in_refs, refs = refs[: count + 4], refs[count + 4 :]
        far, near, (held, wide, sems, out_sems) = refs[:3], refs[3:6], refs[6:]
        outputs = [Sent(n, f, out_sems.at[i]) for i, (f, n) in enumerate(zip(far, near))]
        project_body(count, tp_count, *in_refs, *outputs, held, wide, sems)
        outputs[1].send()
        for output in outputs:
            output.copy.wait()

    return pl.pallas_call(
        body,
        in_specs=[pl.BlockSpec(memory_space=pltpu.SMEM)]
        + [here] * (count + 2)
        + [pl.BlockSpec(memory_space=pl.ANY)],
        out_specs=[there] * 3,
        out_shape=[pltpu.HBM(shape, dtype) for shape, dtype in outs],
        scratch_shapes=[pltpu.VMEM(shape, dtype) for shape, dtype in outs]
        + [
            pltpu.VMEM((kinds - 1, deep, width), BF16),
            pltpu.VMEM((rows, width), F32),
            pltpu.SemaphoreType.DMA(((kinds - 1) * deep // math.gcd(deep, 1024),)),
            pltpu.SemaphoreType.DMA((3,)),
        ],
        compiler_params=params(40),
    )(info, *pieces, first, passed, weights)


def heads_of(ref_width):
    return [slice(at, at + HEAD_DIM) for at in range(0, ref_width, HEAD_DIM)]


def last_row(info_ref, rows, tp_count):
    return block_place(info_ref[1] ^ (tp_count - 1), tp_count) * (rows // tp_count) + (
        rows // tp_count - 1
    )


def block_place(bits, size):
    return bits // 2 + (bits % 2) * (size // 2)


def split_den(dens, count):
    high = dens.astype(BF16).astype(F32)
    return high + pltpu.roll(dens - high, count, 1)


ROOT = 1.0 / math.sqrt(HEAD_DIM)


def weigh(q, k):
    expo = jnp.exp(dot(q, k, ((1,), (1,))) * ROOT)
    return expo, jnp.sum(expo, axis=-1, keepdims=True)


def den_lanes(rows):
    return -(-(rows + 1) // LANES) * LANES


def far_body(tp_count, info_ref, kv_in_ref, q3_ref, q2_ref, kv, *refs):
    back3, back2, token_ref, far_top, far_den = refs
    token_ref[...] = jnp.zeros_like(token_ref)
    kv_ref = kv()
    rows, width = q2_ref.shape
    heads = heads_of(width)
    count = len(heads)
    keys, values = slice(0, rows), slice(rows, 2 * rows)
    last = last_row(info_ref, rows, tp_count)
    spread = den_lanes(rows) - rows

    def sums(q_ref, at_rows, top_ref):
        size = at_rows.stop - at_rows.start
        lane = lax.broadcasted_iota(jnp.int32, (size, LANES), 1)
        dens = jnp.zeros((size, LANES), F32)
        for h, at in enumerate(heads):
            q = q_ref[at_rows, at]
            own, own_den = weigh(q, kv_ref[keys, at])
            other, other_den = weigh(q, kv_in_ref[keys, at])
            top_ref[:size, at] = dot(own.astype(BF16), kv_ref[values, at]) + dot(
                other.astype(BF16), kv_in_ref[values, at]
            )
            dens = jnp.where(lane == h, own_den + other_den, dens)
        return dens

    def fill(back, top, den, edge_top, edge_den):
        back.ref[:rows, :] = top.astype(BF16)
        back.ref[rows : rows + EDGE_ROWS, :] = edge_top.astype(BF16)
        den = jnp.concatenate([den, jnp.broadcast_to(edge_den, (spread, LANES))], axis=0)
        turned = split_den(den, count).T[:EDGE_ROWS].astype(BF16)
        back.ref[rows + EDGE_ROWS :, : turned.shape[1]] = turned
        if turned.shape[1] < width:
            rest = jnp.zeros((EDGE_ROWS, width - turned.shape[1]), BF16)
            back.ref[rows + EDGE_ROWS :, turned.shape[1] :] = rest
        back.send()

    everything = slice(0, rows)
    far_den[...] = sums(q2_ref, everything, far_top.at[0])
    den3 = sums(q3_ref, everything, far_top.at[1])
    row = jnp.broadcast_to(far_top[0, pl.ds(last, 1), :], (EDGE_ROWS, width))
    fill(back3, far_top[1], den3, row, far_den[pl.ds(last, 1), :])
    edge_den = sums(kv_ref, slice(2 * rows, 2 * rows + EDGE_ROWS), far_top.at[1])
    fill(back2, far_top[0], far_den[...], far_top[1, :EDGE_ROWS, :], edge_den[:1])


def near_body(info_ref, kv_in_ref, mask_ref, _, q, kv, top_ref, den_ref, edge_ref):
    q_ref, kv_ref = q(), kv()
    rows, width = q_ref.shape
    allowed = mask_ref[...] > 0
    linked = jnp.where(info_ref[3] % 2 == 1, 1.0, 0.0)
    lane = lax.broadcasted_iota(jnp.int32, (rows, LANES), 1)
    edge_lane = lax.broadcasted_iota(jnp.int32, (EDGE_ROWS, LANES), 1)
    dens = jnp.zeros((rows, LANES), F32)
    edge_dens = jnp.zeros((EDGE_ROWS, LANES), F32)
    keys, values = slice(0, rows), slice(rows, 2 * rows)
    for h, at in enumerate(heads_of(width)):
        k, v = kv_ref[keys, at], kv_ref[values, at]
        k_in, v_in = kv_in_ref[keys, at], kv_in_ref[values, at]
        q = q_ref[:, at]
        own = jnp.where(allowed, jnp.exp(dot(q, k, ((1,), (1,))) * ROOT), 0.0)
        own_den = jnp.sum(own, axis=-1, keepdims=True)
        other, other_den = weigh(q, k_in)
        top_ref[:, at] = dot(own.astype(BF16), v) + dot((other * linked).astype(BF16), v_in)
        dens = jnp.where(lane == h, own_den + other_den * linked, dens)
        edge, edge_den = weigh(kv_in_ref[2 * rows :, at], k_in)
        edge_ref[:, at] = dot((edge * linked).astype(BF16), v_in)
        edge_dens = jnp.where(edge_lane == h, edge_den * linked, edge_dens)
    den_ref[...] = dens
    edge_ref[:, width:] = edge_dens


def attend_paired(info, q, kv, mask, tp_count):
    kv_in = lax.ppermute(kv, "ctx", [(0, 1), (2, 3)])
    far = [lax.ppermute(q, "ctx", [(c, 1)]) for c in (3, 2)]
    rows, width = q.shape
    back = ((rows + 2 * EDGE_ROWS, width), BF16)
    back3, back2, done = staged(
        functools.partial(far_body, tp_count),
        [kv_in, *far],
        [back, back],
        [TOKEN],
        [pltpu.VMEM((2, rows, width), F32), pltpu.VMEM((rows, LANES), F32)],
        info,
        held=[kv],
    )
    back = [lax.ppermute(back3, "ctx", [(1, 3)]), lax.ppermute(back2, "ctx", [(1, 2)])]
    top, den, edge = staged(
        near_body,
        [kv_in, mask, done],
        [],
        [((rows, width), F32), ((rows, LANES), F32), ((EDGE_ROWS, width + LANES), F32)],
        info=info,
        held=[q, kv],
    )
    return top, den, edge, back


def attend_all_body(tp_count, info_ref, mask_ref, q_ref, k_ref, v_ref, top_ref, den_ref, edge_ref):
    rows, width = q_ref.shape
    allowed = mask_ref[...] > 0
    lane = lax.broadcasted_iota(jnp.int32, den_ref.shape, 1)
    dens = jnp.zeros(den_ref.shape, F32)
    heads = heads_of(width)
    for h, at in enumerate(heads):
        scores = dot(q_ref[:, at], k_ref[:, at], ((1,), (1,))) * (1.0 / math.sqrt(HEAD_DIM))
        expo = jnp.where(allowed, jnp.exp(scores), 0.0)
        top_ref[:, at] = dot(expo.astype(BF16), v_ref[:, at])
        dens = jnp.where(lane == h, jnp.sum(expo, axis=-1, keepdims=True), dens)
    den_ref[...] = dens
    last = last_row(info_ref, rows, tp_count)
    count = edge_ref.shape[0]
    top = jnp.broadcast_to(top_ref[pl.ds(last, 1), :], (count, width))
    den = jnp.broadcast_to(den_ref[pl.ds(last, 1), :], (count, LANES))
    edge_ref[:, :width] = top
    edge_ref[:, width:] = den


def attend_all(info, q, kv, mask, tp_count):
    planes = lax.axis_size("ctx")
    rows, width = q.shape
    keys = lax.all_gather(kv[:rows], "ctx", axis=0, tiled=True)
    values = lax.all_gather(kv[rows : 2 * rows], "ctx", axis=0, tiled=True)
    here = pl.BlockSpec(memory_space=pltpu.VMEM)
    outs = [((rows, width), F32), ((rows, LANES), F32), ((EDGE_ROWS, width + LANES), F32)]
    top, den, edge = pl.pallas_call(
        functools.partial(attend_all_body, tp_count),
        in_specs=[pl.BlockSpec(memory_space=pltpu.SMEM)] + [here] * 4,
        out_specs=[here] * 3,
        out_shape=[jax.ShapeDtypeStruct(shape, dtype) for shape, dtype in outs],
        compiler_params=params(48),
    )(info, mask, q, keys, values)
    edge = lax.ppermute(edge, "ctx", [(c, c + 1) for c in range(planes - 1)])
    return top, den, edge, []


def output_body(count, tp_count, info_ref, *refs):
    back_refs = refs[:count]
    top_ref, den_ref, edge_ref, w_ref, odd_out, even_ref, whole, odd_ref, out_sems = refs[count:]
    depth = w_ref.shape[0]
    blocks, _, step = odd_ref.shape
    rows = top_ref.shape[0]
    heads = heads_of(depth)
    edges = []

    back_dens = []
    for ref in back_refs:
        turned = ref[rows + EDGE_ROWS :, : den_lanes(rows)].astype(F32)
        rest = jnp.zeros((LANES - EDGE_ROWS, turned.shape[1]), F32)
        back_dens.append(jnp.concatenate([turned, rest], axis=0).T)

    for h, lanes in enumerate(heads):
        top, den = top_ref[:, lanes], den_ref[:, h : h + 1]
        edge, edge_den = edge_ref[:, lanes], edge_ref[:, depth + h : depth + h + 1]
        for ref in back_refs:
            top += ref[:rows, lanes].astype(F32)
            edge += ref[rows : rows + EDGE_ROWS, lanes].astype(F32)
        for value in back_dens:
            both = value[:, h : h + 1] + value[:, len(heads) + h : len(heads) + h + 1]
            den += both[:rows]
            edge_den += both[rows : rows + EDGE_ROWS]
        whole[:, lanes] = top / den
        edges.append(jnp.where(edge_den > 0, edge / jnp.where(edge_den > 0, edge_den, 1.0), 0.0))
    edge = jnp.concatenate(edges, axis=1)[:1]
    patches = rows // tp_count
    me = info_ref[1]
    before = []
    for bits in block_order(tp_count):
        peer = me ^ bits
        source = block_place(me ^ ((peer + tp_count - 1) % tp_count), tp_count)
        row = whole[pl.ds(source * patches + patches - 1, 1), :]
        before.append(jnp.where(peer == 0, edge, row))
    for index, row in enumerate(before):
        at = index * patches + patches - 1
        whole[at : at + 1, :] = row
    attended = whole[...].astype(BF16)
    half = rows // 2
    sends = []
    for n in range(blocks):
        at = pl.ds(n * step, step)
        out = dot(attended, w_ref[:, at])
        odd_ref[n] = out[half:].astype(BF16)
        sends.append(pltpu.make_async_copy(odd_ref.at[n], odd_out.at[:, at], out_sems.at[n]))
        sends[-1].start()
        even_ref[:, at] = out[:half].astype(BF16)
    for copy in sends:
        copy.wait()


def output_project(info, top, den, edge, back, weights, tp_count):
    rows, depth = top.shape
    width = weights.shape[1]
    step = min(width, 1024)
    here, there = pl.BlockSpec(memory_space=pltpu.VMEM), pl.BlockSpec(memory_space=pltpu.HBM)
    blocks = width // step
    odd, even = pl.pallas_call(
        functools.partial(output_body, len(back), tp_count),
        in_specs=[pl.BlockSpec(memory_space=pltpu.SMEM)] + [here] * (4 + len(back)),
        out_specs=[there, here],
        out_shape=[
            pltpu.HBM((rows // 2, width), BF16),
            jax.ShapeDtypeStruct((rows // 2, width), BF16),
        ],
        scratch_shapes=[
            pltpu.VMEM((rows, depth), F32),
            pltpu.VMEM((blocks, rows // 2, step), BF16),
            pltpu.SemaphoreType.DMA((blocks,)),
        ],
        compiler_params=params(16),
    )(info, *back, top, den, edge, weights)
    return even, odd


def pair_sum_body(mine_ref, other_ref, own_ref, *send_refs):
    patches = own_ref.shape[0]
    total = mine_ref[...].astype(F32) + other_ref[...].astype(F32)
    own_ref[...] = total[:patches]
    for index, ref in enumerate(send_refs):
        ref[...] = total[(index + 1) * patches : (index + 2) * patches].astype(BF16)


def scatter_sum(even, odd, patches):
    blocks = even.shape[0] // patches
    block = (patches, even.shape[1])
    pieces = call(pair_sum_body, [(block, F32)] + [(block, BF16)] * (blocks - 1))(
        even, swap(odd, 1)
    )
    return [pieces[0]] + [swap(piece, 2 * (index + 1)) for index, piece in enumerate(pieces[1:])]


def state_body(count, *refs):
    terms = refs[:count]
    local_ref, normed, state_out, normed_ref, wide = refs[count:]
    patches = terms[0].shape[0]
    width = normed_ref.shape[1]
    chunks = width // LANES
    for b in range(PATCH):
        at = slice(b * width, (b + 1) * width)
        total = terms[0][:, at]
        for term in terms[1:]:
            total += term[:, at].astype(F32)
        part = pltpu.roll(total.astype(BF16).astype(F32), 1, 0)
        for c in range(chunks):
            wide[c, pl.ds(b, patches, stride=PATCH), :] = part[:, c * LANES : (c + 1) * LANES]
    context = jnp.concatenate([wide[c] for c in range(chunks)], axis=1)
    state = local_ref[...].astype(F32) + context
    state_out.ref[...] = state
    state_out.send()
    mean = jnp.mean(state * state, axis=-1, keepdims=True)
    normed_ref[...] = (state * lax.rsqrt(mean + EPS)).astype(BF16)
    normed.ref[...] = normed_ref[...]


def byte_state(terms, local_embeds, after):
    rows, width = local_embeds.shape
    normed, state, normed_near = staged(
        functools.partial(state_body, len(terms)),
        [*terms, local_embeds],
        [((rows, width), BF16), ((rows, width), F32)],
        [((rows, width), BF16)],
        [pltpu.VMEM((width // LANES, rows, LANES), F32)],
        after=after,
    )
    return state, normed, normed_near


def unit(x):
    scale = lax.rsqrt(jnp.mean(x * x, axis=-1, keepdims=True) + EPS)
    return x * scale, scale


def unit_back(grad, y, scale):
    return scale * (grad - y * jnp.mean(grad * y, axis=-1, keepdims=True))


def prepare_body(parts, info_ref, gb_ref, wq_ref, wk_ref, wv_ref, wo_ref, token_ref, *refs):
    token_ref[...] = jnp.zeros_like(token_ref)
    weights_ref = refs[0]
    d = LOCAL_HEAD_DIM
    rows = refs[1].shape[0] // len(parts[0])
    for kind, ref in enumerate((wq_ref, wk_ref, wv_ref)):
        weights_ref[:, kind * d : (kind + 1) * d] = ref[0]
    for index, part in enumerate(parts):
        out_ref, core_ref = refs[1 + 2 * index : 3 + 2 * index]
        for place, bits in enumerate(part):
            at = pl.multiple_of((info_ref[1] ^ bits) * rows, rows)
            out_ref[place * rows : (place + 1) * rows, :] = gb_ref[pl.ds(at, rows), :]
        core_ref[...] = dot(out_ref[...], wo_ref[0], ((1,), (1,))).astype(BF16)


def prepare(info, gb_all, local_qkv, local_out, rows, parts):
    width = gb_all.shape[1]
    d = LOCAL_HEAD_DIM
    heads = LOCAL_HEADS

    def qkv_spec(kind):
        return pl.BlockSpec((1, width, d), lambda i, info: (0, 0, kind * heads + info[0]))

    outs = [(width, 3 * d)]
    for part in parts:
        outs += [(len(part) * rows, width), (len(part) * rows, d)]
    token, weights, *blocks = pl.pallas_call(
        functools.partial(prepare_body, parts),
        grid_spec=pltpu.PrefetchScalarGridSpec(
            num_scalar_prefetch=1,
            grid=(1,),
            in_specs=[
                pl.BlockSpec(gb_all.shape, lambda i, info: (0, 0)),
                qkv_spec(0),
                qkv_spec(1),
                qkv_spec(2),
                pl.BlockSpec((1, d, width), lambda i, info: (0, info[0], 0)),
            ],
            out_specs=[pl.BlockSpec(shape, lambda i, info: (0, 0)) for shape in [TOKEN.shape, *outs]],
        ),
        out_shape=[TOKEN] + [jax.ShapeDtypeStruct(shape, BF16) for shape in outs],
        compiler_params=params(LARGE),
    )(info, gb_all, local_qkv, local_qkv, local_qkv, local_out)
    return token, weights, blocks[0::2], blocks[1::2]


def window(rows):
    row = lax.broadcasted_iota(jnp.int32, (rows, rows), 0)
    column = lax.broadcasted_iota(jnp.int32, (rows, rows), 1)
    return (row // PATCH == column // PATCH) & (column <= row)


def core_weights(qkv, allowed):
    d = LOCAL_HEAD_DIM
    q, q_scale = unit(qkv[:, :d])
    k, k_scale = unit(qkv[:, d : 2 * d])
    qb, kb, vb = q.astype(BF16), k.astype(BF16), qkv[:, 2 * d :].astype(BF16)
    expo = jnp.where(allowed, jnp.exp(dot(qb, kb, ((1,), (1,))) * (1.0 / math.sqrt(d))), 0.0)
    weight = expo / jnp.sum(expo, axis=-1, keepdims=True)
    return (q, q_scale, qb), (k, k_scale, kb), vb, weight


def core_forward(weight, vb):
    return dot(weight.astype(BF16), vb).astype(BF16)


def core_backward(query, key, vb, weight, gradb):
    q, q_scale, qb = query
    k, k_scale, kb = key
    grad_v = dot(weight.astype(BF16), gradb, ((0,), (0,)))
    grad_w = dot(gradb, vb, ((1,), (1,)))
    mean = jnp.sum(weight * grad_w, axis=-1, keepdims=True)
    grad_s = (weight * (grad_w - mean) * (1.0 / math.sqrt(LOCAL_HEAD_DIM))).astype(BF16)
    grad_q = unit_back(dot(grad_s, kb), q, q_scale)
    grad_k = unit_back(dot(grad_s, qb, ((0,), (0,))), k, k_scale)
    return jnp.concatenate([grad_q, grad_k, grad_v], axis=1).astype(BF16)


def chunks_in(piece):
    return jnp.concatenate(
        [piece[:, at : at + LANES] for at in range(0, piece.shape[1], LANES)], axis=0
    )


def chunks_out(value, rows):
    return jnp.concatenate(
        [value[at : at + rows] for at in range(0, value.shape[0], rows)], axis=1
    )


def rows_of(refs):
    return jnp.concatenate([ref[...] for ref in refs], axis=0)


def local_body(count, *refs):
    x_refs, refs = refs[:count], refs[count:]
    (gb_ref, core_ref, w_ref), refs = refs[:3], refs[3:]
    carry, (gqkv_ref, gout_ref, ab_ref, token_ref) = refs[:-4], refs[-4:]
    token_ref[...] = jnp.zeros_like(token_ref)
    gqkv, gout, abs_ = local_grads(x_refs, gb_ref, core_ref, w_ref, carry)
    gqkv_ref[...] = gqkv
    gout_ref[...] = gout
    ab_ref[...] = jnp.concatenate(abs_, axis=0)


def local_grads(x_refs, gb_ref, core_ref, w_ref, carry):
    x = rows_of(x_refs)
    rows = x_refs[0].shape[0]
    allowed = window(rows)
    qkv = dot(x, w_ref[...])
    abs_, gqs = [], []
    for index in range(len(x_refs)):
        at = slice(index * rows, (index + 1) * rows)
        query, key, vb, weight = core_weights(qkv[at], allowed)
        abs_.append(core_forward(weight, vb))
        gqs.append(core_backward(query, key, vb, weight, core_ref[at, :]))
    gqkv = dot(jnp.concatenate(gqs, axis=0), x, ((0,), (0,)))
    gout = dot(jnp.concatenate(abs_, axis=0), gb_ref[...], ((0,), (0,)))
    if carry:
        gqkv += carry[0][...]
        gout += carry[1][...]
    return gqkv, gout, abs_


def local_last_body(count, info_ref, *refs):
    x_refs, refs = refs[:count], refs[count:]
    gb_ref, core_ref, w_ref, *carry, ab0_ref, gqkv_out, message, kept_ref, held = refs
    gqkv, gout, abs_ = local_grads(x_refs, gb_ref, core_ref, w_ref, carry)
    gqkv_out.ref[...] = gqkv.T.astype(BF16)
    gqkv_out.send()
    held[...] = gout
    rows = x_refs[0].shape[0]
    message.ref[:rows, :] = ab0_ref[rows:, :]
    for index, ab in enumerate(abs_):
        message.ref[(index + 1) * rows : (index + 2) * rows, :] = ab
    deep = kept_ref.shape[1]
    piece_rows = deep * LANES // held.shape[1]
    for k in range(held.shape[0] // piece_rows):
        at = pl.multiple_of((info_ref[2] ^ k) * piece_rows, piece_rows)
        piece = chunks_in(held[pl.ds(at, piece_rows), :]).astype(BF16)
        if k % 2:
            start = (count + 1) * rows + k // 2 * deep
            message.ref[start : start + deep, :] = piece
        else:
            kept_ref[k // 2] = piece


def relay_body(count, ab0_ref, ab1_ref, kept_ref, there_ref, *refs):
    rows = ab0_ref.shape[0] // 2
    deep = kept_ref.shape[1]
    *messages, own, token_ref = refs
    token_ref[...] = jnp.zeros_like(token_ref)
    for k, message in enumerate([own, *messages]):
        parts = []
        if k <= count:
            parts.append(ab0_ref[:rows, :] if k == 0 else ab1_ref[(k - 1) * rows : k * rows, :])
            parts.append(there_ref[k * rows : (k + 1) * rows, :])
        if k < kept_ref.shape[0]:
            start = (count + 1) * rows + k * deep
            parts.append(kept_ref[k])
            parts.append(there_ref[start : start + deep, :])
        at = 0
        target = message if k == 0 else message.ref
        for part in parts:
            target[at : at + part.shape[0], :] = part
            at += part.shape[0]
        if k:
            message.send()


def local_layer(normed, normed_near, info, parts, gbs, cores, weights, rounds, tp_count):
    rows, width = normed.shape
    d = LOCAL_HEAD_DIM
    near = [swap(normed, bits) for bits in parts[1]]
    count = len(near)
    totals = [((3 * d, width), F32), ((d, width), F32)]

    def step(index, xs, carry):
        return staged(
            functools.partial(local_body, len(xs)),
            [*xs, gbs[index], cores[index], weights, *carry],
            [],
            [*totals, ((len(xs) * rows, d), BF16), TOKEN],
            flops=1 << 34,
            mib=20,
        )

    *carry, ab0, done = step(0, [normed_near, swap(normed, 1)], [])
    near = [tie(block, done) for block in near]
    far = [swap(block, 1) for block in near]
    *carry, ab1, _ = step(1, near, carry)
    deep = d // rounds * width // LANES
    halves = rounds // 2
    length = (count + 1) * rows + halves * deep
    grad_qkv, message, kept = staged(
        functools.partial(local_last_body, count),
        [*far, gbs[2], cores[2], weights, *carry, ab0],
        [((width, 3 * d), BF16), ((length, d), BF16)],
        [((halves, deep, d), BF16)],
        [pltpu.VMEM((d, width), F32)],
        info,
        flops=1 << 34,
        mib=20,
    )
    sizes = [2 * rows * (k <= count) + 2 * deep * (k < halves) for k in range(max(count + 1, halves))]
    *messages, own, done = staged(
        functools.partial(relay_body, count),
        [ab0, ab1, kept, swap(message, 1)],
        [((size, d), BF16) for size in sizes[1:]],
        [((sizes[0], d), BF16), TOKEN],
    )
    messages = [own] + [swap(value, 2 * (k + 1)) for k, value in enumerate(messages)]
    return messages, tie(grad_qkv, done, mib=LARGE)


def hidden_body(heads, count, info_ref, state_ref, w_ref, *refs):
    *messages, out_ref, token_ref = refs
    token_ref[...] = jnp.zeros_like(token_ref)
    rows = state_ref.shape[0]
    d = LOCAL_HEAD_DIM
    total = state_ref[...]
    for bits in range(2 * count + 2):
        at = bits % 2 * rows
        head = heads(info_ref[1] ^ bits)
        weights = w_ref[0, pl.ds(pl.multiple_of(head * d, d), d), :]
        total += dot(messages[bits // 2][at : at + rows, :], weights)
    out_ref[...] = total.astype(BF16)


def planes_body(planes, count, rounds, rows, info_ref, *refs):
    half = rounds // 2
    messages, outs, held = refs[:half], refs[half:-1], refs[-1]
    deep = held.shape[1]
    for k in range(rounds):
        start = 2 * rows * (k // 2 <= count) + k % 2 * deep
        held[k] = messages[k // 2][start : start + deep, :].astype(F32)
    for z, out in enumerate(outs):
        total = None
        for outer in range(rounds // planes):
            term = held[info_ref[2] ^ ((info_ref[3] ^ z) + outer * planes)]
            total = term if total is None else total + term
        out.ref[...] = total.astype(BF16)
        out.send()


def final_body(heads, parts_ref, _, *refs):
    *terms, gqkv_ref, gout_ref = refs
    gout = sum(term[...].astype(F32) for term in terms)
    gout_ref[0] = chunks_out(gout, gout_ref.shape[1])
    d = LOCAL_HEAD_DIM
    tp_count = len(heads)
    for h in range(LOCAL_HEADS):
        total = None
        for source in range(parts_ref.shape[0]):
            if heads[source % tp_count] == h:
                term = parts_ref[source].astype(F32)
                total = term if total is None else total + term
        for kind in range(3):
            at = (kind * LOCAL_HEADS + h) * d
            gqkv_ref[0, :, at : at + d] = total[:, kind * d : (kind + 1) * d]


def swap_planes(pieces):
    count = len(pieces)
    return [pieces[0]] + [
        lax.ppermute(pieces[k], "ctx", [(c, c ^ k) for c in range(count)]) for k in range(1, count)
    ]


def per_device(byte_embeds, local_embeds, global_qkv, global_out, local_qkv, local_out, cotangent):
    byte_count, width = byte_embeds.shape
    patches = byte_count // PATCH
    planes, tp_count = lax.axis_size("ctx"), lax.axis_size("tp")
    plane, me = lax.axis_index("ctx"), lax.axis_index("tp")
    order = block_order(tp_count)
    shard_rows = tp_count * patches
    devices = planes * tp_count

    group = min(tp_count, LOCAL_HEADS)
    share = width // devices
    rounds = LOCAL_HEAD_DIM // share
    plane_heads = LOCAL_HEADS // planes

    def head_of(t):
        return (t % rounds) % planes * plane_heads + t // rounds

    heads = [head_of(t) for t in range(tp_count)]
    head_info = jnp.stack([head_of(me), me, me % rounds, plane]).astype(jnp.int32)

    patch_in = patch_norm(byte_embeds)
    mine = swap(patch_in, 1)
    weights_in, head_info = preload(global_qkv, head_info, mine)
    even = [tie(swap(patch_in, bits), head_info) for bits in range(2, tp_count, 2)]
    pieces = [patch_in, *even, mine, *(swap(piece, 1) for piece in even)]
    q, kv, gb = project(head_info, pieces, weights_in, global_qkv, cotangent, tp_count)

    place = (
        (me ^ jnp.array(order, jnp.int32))[:, None] * patches
        + jnp.arange(patches, dtype=jnp.int32)[None, :]
    ).reshape(-1)
    if planes == 4 and den_lanes(shard_rows) <= q.shape[1]:
        mask = (place[None, :] <= place[:, None]).astype(F32)
        top, den, edge, back = attend_paired(
            head_info, q, kv, mask, tp_count
        )
    else:
        key_place = (
            jnp.arange(planes, dtype=jnp.int32)[:, None] * shard_rows + place[None, :]
        ).reshape(-1)
        mask = (key_place[None, :] <= (plane * shard_rows + place)[:, None]).astype(F32)
        top, den, edge, back = attend_all(head_info, q, kv, mask, tp_count)

    weights_out, _ = preload(global_out, head_info, den)
    even, odd = output_project(head_info, top, den, edge, back, weights_out, tp_count)

    parts = [[0, 1], list(range(2, group, 2)), list(range(3, group, 2))]
    gb_all = lax.all_gather(gb, "tp", axis=0, tiled=True)
    prepared, weights, gbs, cores = prepare(head_info, gb_all, local_qkv, local_out, byte_count, parts)
    state, normed, normed_near = byte_state(
        scatter_sum(even, odd, patches), local_embeds, prepared
    )
    messages, grad_qkv = local_layer(
        normed, normed_near, head_info, parts, gbs, cores, weights, rounds, tp_count
    )
    grad_qkv = lax.all_to_all(grad_qkv, ("ctx", "tp"), 0, 0, tiled=True)
    flat = (share * width // LANES, LANES)
    count = group // 2 - 1
    out_pieces = staged(
        functools.partial(planes_body, planes, count, rounds, byte_count),
        messages[: rounds // 2],
        [(flat, BF16)] * planes,
        scratch=[pltpu.VMEM((rounds,) + flat, F32)],
        info=head_info,
    )
    out_pieces = swap_planes(out_pieces)
    here = pl.BlockSpec(memory_space=pltpu.VMEM)
    hidden, done = pl.pallas_call(
        functools.partial(hidden_body, head_of, count),
        in_specs=[pl.BlockSpec(memory_space=pltpu.SMEM)] + [here] * (3 + count),
        out_specs=[here, here],
        out_shape=[jax.ShapeDtypeStruct((byte_count, width), BF16), TOKEN],
        compiler_params=params(16),
    )(head_info, state, local_out, *messages[: count + 1])
    grad_qkv, grad_out = call(
        functools.partial(final_body, heads),
        [((1, share, 3 * width), F32), ((1, share, width), F32)],
        mib=16,
    )(grad_qkv.reshape(devices, share, 3 * LOCAL_HEAD_DIM), done, *out_pieces)
    return (hidden, grad_qkv, grad_out)


def solution(mesh):
    in_specs = (
        P(("ctx", "tp"), None),
        P(("ctx", "tp"), None),
        P(None, None, "tp"),
        P("tp", None),
        P(),
        P(),
        P(("ctx", "tp"), None),
    )
    out_specs = (P(("ctx", "tp"), None), P(None, ("ctx", "tp"), None), P(None, ("ctx", "tp"), None))
    return jax.shard_map(
        per_device, mesh=mesh, in_specs=in_specs, out_specs=out_specs, check_vma=False
    )
```

```python
import functools
import math

import jax
import jax.numpy as jnp
from jax import lax
from jax.experimental import pallas as pl
from jax.experimental.pallas import tpu as pltpu
from jax.sharding import PartitionSpec as P

PATCH = 8
HEAD_DIM = 128
LOCAL_HEADS = 8
LOCAL_HEAD_DIM = 128
EPS = 1e-06
F32 = jnp.float32
BF16 = jnp.bfloat16
MIB = 1 << 20
LARGE = 60
TOKEN = pltpu.VMEM((8, 128), jnp.float32)
LANES = 128
EDGE_ROWS = 16
BF16_ROWS = 16


def params(mib):
    return pltpu.CompilerParams(vmem_limit_bytes=mib * MIB)


def call(body, outs, scratch=(), mib=32):
    return pl.pallas_call(
        body,
        out_shape=[out if out is TOKEN else jax.ShapeDtypeStruct(*out) for out in outs],
        scratch_shapes=list(scratch),
        compiler_params=params(mib),
    )


class Held:
    def __init__(self, source, target, sem):
        self.ref, self.copy, self.waited = target, pltpu.make_async_copy(source, target, sem), False
        self.copy.start()

    def __call__(self):
        if not self.waited:
            self.copy.wait()
            self.waited = True
        return self.ref


class Sent:
    def __init__(self, source, target, sem):
        self.ref, self.copy, self.started = source, pltpu.make_async_copy(source, target, sem), False

    def send(self):
        self.copy.start()
        self.started = True


def staged(body, args, sent, outs=(), scratch=(), info=None, mib=16, flops=0, after=None, held=()):
    tokens = [] if after is None else [after]
    counts = [len(args), len(held), len(tokens), len(sent), len(outs)]
    counts += [len(held), len(sent), len(scratch)]

    def kernel(*refs):
        refs = list(refs)
        info_ref = [refs.pop(0)] if info is not None else []
        groups = []
        for count in counts:
            groups.append(refs[:count])
            del refs[:count]
        in_refs, held_far, _, sent_far, out_refs, held_near, sent_near, own = groups
        in_sems, out_sems = refs
        inputs = [Held(f, n, in_sems.at[i]) for i, (f, n) in enumerate(zip(held_far, held_near))]
        outputs = [Sent(n, f, out_sems.at[i]) for i, (f, n) in enumerate(zip(sent_far, sent_near))]
        body(*info_ref, *in_refs, *inputs, *outputs, *out_refs, *own)
        for output in outputs:
            if not output.started:
                output.send()
        for value in inputs:
            value()
        for output in outputs:
            output.copy.wait()

    here, there = pl.BlockSpec(memory_space=pltpu.VMEM), pl.BlockSpec(memory_space=pltpu.HBM)
    free = pl.BlockSpec(memory_space=pl.ANY)
    scalars = [] if info is None else [info]
    return pl.pallas_call(
        kernel,
        in_specs=[pl.BlockSpec(memory_space=pltpu.SMEM)] * len(scalars)
        + [here] * len(args)
        + [free] * (len(held) + len(tokens)),
        out_specs=[there] * len(sent) + [here] * len(outs),
        out_shape=[pltpu.HBM(shape, dtype) for shape, dtype in sent]
        + [out if out is TOKEN else jax.ShapeDtypeStruct(*out) for out in outs],
        scratch_shapes=[pltpu.VMEM(value.shape, value.dtype) for value in held]
        + [pltpu.VMEM(shape, dtype) for shape, dtype in sent]
        + list(scratch)
        + [pltpu.SemaphoreType.DMA((max(1, count),)) for count in (len(held), len(sent))],
        compiler_params=params(mib),
        cost_estimate=pl.CostEstimate(flops=flops, bytes_accessed=1 << 22, transcendentals=0),
    )(*scalars, *args, *held, *tokens)


def dot(a, b, dims=((1,), (0,))):
    return lax.dot_general(a, b, (dims, ((), ())), preferred_element_type=F32)


def swap(value, bits):
    count = lax.axis_size("tp")
    return lax.ppermute(value, "tp", [(source, source ^ bits) for source in range(count)])


def block_order(size):
    return list(range(0, size, 2)) + list(range(1, size, 2))


def gather(value, size):
    even = [value] + [swap(value, bits) for bits in range(2, size, 2)]
    return even + [swap(piece, 1) for piece in even]


def tie_body(*refs):
    pass


def tie(value, *after, mib=1):
    there = pl.BlockSpec(memory_space=pl.ANY)
    return pl.pallas_call(
        tie_body,
        in_specs=[there] * (1 + len(after)),
        out_specs=there,
        out_shape=jax.ShapeDtypeStruct(value.shape, value.dtype),
        input_output_aliases={0: 0},
        compiler_params=params(mib),
    )(value, *after)


def preload_body(parts, info_ref, w_ref, _, out_ref, info_out, sems):
    for index in range(info_ref.shape[0]):
        info_out[index] = info_ref[index]
    source = w_ref.at[0] if len(w_ref.shape) == 3 else w_ref
    size = source.shape[0] // parts
    copies = []
    for part in range(parts):
        at = pl.ds(part * size, size)
        copies.append(pltpu.make_async_copy(source.at[at], out_ref.at[at], sems.at[part]))
        copies[-1].start()
    for copy in copies:
        copy.wait()


def preload(weights, info, after, parts=8):
    there = pl.BlockSpec(memory_space=pl.ANY)
    scalar = pl.BlockSpec(memory_space=pltpu.SMEM)
    shape = weights.shape[-2:]
    return pl.pallas_call(
        functools.partial(preload_body, parts),
        in_specs=[scalar, there, there],
        out_specs=[pl.BlockSpec(memory_space=pltpu.VMEM), scalar],
        out_shape=[
            pltpu.VMEM(shape, weights.dtype),
            jax.ShapeDtypeStruct(info.shape, info.dtype),
        ],
        scratch_shapes=[pltpu.SemaphoreType.DMA((parts,))],
        compiler_params=params(50),
        cost_estimate=pl.CostEstimate(
            flops=0, bytes_accessed=2 * math.prod(shape), transcendentals=0
        ),
    )(info, weights, after)


def patch_norm_body(x_ref, out_ref, wide):
    patches = out_ref.shape[0]
    width = x_ref.shape[1]
    total = jnp.zeros((patches, LANES), F32)
    for c in range(width // LANES):
        wide[c] = x_ref[:, c * LANES : (c + 1) * LANES].astype(F32)
    for c in range(width // LANES):
        for b in range(PATCH):
            part = wide[c, pl.ds(b, patches, stride=PATCH), :]
            total += part * part
    scale = lax.rsqrt(jnp.sum(total, axis=-1, keepdims=True) / (PATCH * width) + EPS)
    for b in range(PATCH):
        for c in range(width // LANES):
            part = wide[c, pl.ds(b, patches, stride=PATCH), :]
            at = b * width + c * LANES
            out_ref[:, at : at + LANES] = (part * scale).astype(BF16)


def patch_norm(byte_embeds):
    rows, width = byte_embeds.shape
    return call(
        patch_norm_body,
        [((rows // PATCH, PATCH * width), BF16)],
        [pltpu.VMEM((width // LANES, rows, LANES), F32)],
        16,
    )(byte_embeds)[0]


def stack(refs):
    return jnp.concatenate([ref[...].astype(F32) for ref in refs], axis=0).astype(BF16)


def project_body(count, tp_count, info_ref, *refs):
    x_refs, refs = refs[:count], refs[count:]
    first_ref, pass_ref, w_ref, q, kv, passed, held, wide, sems = refs
    kinds, rows, _ = held.shape
    depth = math.gcd(rows, 1024)
    copies = {}
    for c in range(kinds):
        for k in range(0, rows, depth):
            at = pl.ds(k, depth)
            copies[c, k] = pltpu.make_async_copy(
                w_ref.at[c + 1, at], held.at[c, at], sems.at[len(copies)]
            )
            copies[c, k].start()
    x = stack(x_refs)
    count_rows = x.shape[0]
    passed.ref[...] = pass_ref[...]
    passed.send()
    for c in range(kinds + 1):
        total = None
        for k in range(0, rows, depth):
            if c:
                copies[c - 1, k].wait()
                w = held[c - 1, k : k + depth, :]
            else:
                w = first_ref[k : k + depth, :]
            term = dot(x[:, k : k + depth], w)
            total = term if total is None else total + term
        for h in range(total.shape[1] // HEAD_DIM):
            at = slice(h * HEAD_DIM, (h + 1) * HEAD_DIM)
            part = total[:, at]
            if c < 2:
                part = part * lax.rsqrt(jnp.mean(part * part, axis=-1, keepdims=True) + EPS)
            if c == 0:
                wide[:, at] = part
            else:
                kv.ref[(c - 1) * count_rows : c * count_rows, at] = part.astype(BF16)
        if c == 0:
            q.ref[...] = wide[...].astype(BF16)
            q.send()
            last = wide[pl.ds(last_row(info_ref, count_rows, tp_count), 1), :]
            spread = jnp.broadcast_to(last, (EDGE_ROWS, last.shape[1]))
            kv.ref[kinds * count_rows :, :] = spread.astype(BF16)


def project(info, pieces, first, weights, passed, tp_count):
    rows = sum(piece.shape[0] for piece in pieces)
    kinds, deep, width = weights.shape
    here, there = pl.BlockSpec(memory_space=pltpu.VMEM), pl.BlockSpec(memory_space=pltpu.HBM)
    outs = [((rows, width), BF16), (((kinds - 1) * rows + EDGE_ROWS, width), BF16)]
    outs.append((passed.shape, passed.dtype))
    count = len(pieces)

    def body(*refs):
        in_refs, refs = refs[: count + 4], refs[count + 4 :]
        far, near, (held, wide, sems, out_sems) = refs[:3], refs[3:6], refs[6:]
        outputs = [Sent(n, f, out_sems.at[i]) for i, (f, n) in enumerate(zip(far, near))]
        project_body(count, tp_count, *in_refs, *outputs, held, wide, sems)
        outputs[1].send()
        for output in outputs:
            output.copy.wait()

    return pl.pallas_call(
        body,
        in_specs=[pl.BlockSpec(memory_space=pltpu.SMEM)]
        + [here] * (count + 2)
        + [pl.BlockSpec(memory_space=pl.ANY)],
        out_specs=[there] * 3,
        out_shape=[pltpu.HBM(shape, dtype) for shape, dtype in outs],
        scratch_shapes=[pltpu.VMEM(shape, dtype) for shape, dtype in outs]
        + [
            pltpu.VMEM((kinds - 1, deep, width), BF16),
            pltpu.VMEM((rows, width), F32),
            pltpu.SemaphoreType.DMA(((kinds - 1) * deep // math.gcd(deep, 1024),)),
            pltpu.SemaphoreType.DMA((3,)),
        ],
        compiler_params=params(40),
    )(info, *pieces, first, passed, weights)


def heads_of(ref_width):
    return [slice(at, at + HEAD_DIM) for at in range(0, ref_width, HEAD_DIM)]


def last_row(info_ref, rows, tp_count):
    return block_place(info_ref[1] ^ (tp_count - 1), tp_count) * (rows // tp_count) + (
        rows // tp_count - 1
    )


def block_place(bits, size):
    return bits // 2 + (bits % 2) * (size // 2)


def split_den(dens, count):
    high = dens.astype(BF16).astype(F32)
    return high + pltpu.roll(dens - high, count, 1)


ROOT = 1.0 / math.sqrt(HEAD_DIM)


def weigh(q, k):
    expo = jnp.exp(dot(q, k, ((1,), (1,))) * ROOT)
    return expo, jnp.sum(expo, axis=-1, keepdims=True)


def den_lanes(rows):
    return -(-(rows + 1) // LANES) * LANES


def far_body(tp_count, info_ref, kv_in_ref, q_ref, *refs):
    first = len(refs) == 6
    if first:
        kv, back, given_ref, token_ref, top, dens_ref = refs
        token_ref[...] = jnp.zeros_like(token_ref)
    else:
        given_ref, kv, back, top = refs
    kv_ref = kv()
    rows, width = q_ref.shape
    heads = heads_of(width)
    count = len(heads)
    keys, values = slice(0, rows), slice(rows, 2 * rows)

    def sums(source_ref, at_rows):
        size = at_rows.stop - at_rows.start
        lane = lax.broadcasted_iota(jnp.int32, (size, LANES), 1)
        dens = jnp.zeros((size, LANES), F32)
        tops = []
        for h, at in enumerate(heads):
            q = source_ref[at_rows, at]
            own, own_den = weigh(q, kv_ref[keys, at])
            other, other_den = weigh(q, kv_in_ref[keys, at])
            tops.append(
                dot(own.astype(BF16), kv_ref[values, at])
                + dot(other.astype(BF16), kv_in_ref[values, at])
            )
            dens = jnp.where(lane == h, own_den + other_den, dens)
        return jnp.concatenate(tops, axis=1), dens

    top[...], dens = sums(q_ref, slice(0, rows))
    if first:
        dens_ref[...] = dens
        last = last_row(info_ref, rows, tp_count)
        given_ref[:, :width] = jnp.broadcast_to(top[pl.ds(last, 1), :], (EDGE_ROWS, width))
        given_ref[:, width:] = jnp.broadcast_to(dens_ref[pl.ds(last, 1), :], (EDGE_ROWS, LANES))
        edge_top, edge_den = sums(kv_ref, slice(2 * rows, 2 * rows + EDGE_ROWS))
    else:
        edge_top, edge_den = given_ref[:, :width], given_ref[:, width:]
    back.ref[:rows, :] = top[...].astype(BF16)
    back.ref[rows : rows + EDGE_ROWS, :] = edge_top.astype(BF16)
    spread = jnp.broadcast_to(edge_den[:1], (den_lanes(rows) - rows, LANES))
    turned = split_den(jnp.concatenate([dens, spread], axis=0), count).T[:EDGE_ROWS].astype(BF16)
    back.ref[rows + EDGE_ROWS :, : turned.shape[1]] = turned
    if turned.shape[1] < width:
        rest = jnp.zeros((EDGE_ROWS, width - turned.shape[1]), BF16)
        back.ref[rows + EDGE_ROWS :, turned.shape[1] :] = rest


def near_body(info_ref, kv_in_ref, mask_ref, _, q, kv, top_ref, den_ref, edge_ref):
    q_ref, kv_ref = q(), kv()
    rows, width = q_ref.shape
    allowed = mask_ref[...] > 0
    linked = jnp.where(info_ref[3] % 2 == 1, 1.0, 0.0)
    lane = lax.broadcasted_iota(jnp.int32, (rows, LANES), 1)
    edge_lane = lax.broadcasted_iota(jnp.int32, (EDGE_ROWS, LANES), 1)
    dens = jnp.zeros((rows, LANES), F32)
    edge_dens = jnp.zeros((EDGE_ROWS, LANES), F32)
    keys, values = slice(0, rows), slice(rows, 2 * rows)
    for h, at in enumerate(heads_of(width)):
        k, v = kv_ref[keys, at], kv_ref[values, at]
        k_in, v_in = kv_in_ref[keys, at], kv_in_ref[values, at]
        q = q_ref[:, at]
        own = jnp.where(allowed, jnp.exp(dot(q, k, ((1,), (1,))) * ROOT), 0.0)
        own_den = jnp.sum(own, axis=-1, keepdims=True)
        other, other_den = weigh(q, k_in)
        top_ref[:, at] = dot(own.astype(BF16), v) + dot((other * linked).astype(BF16), v_in)
        dens = jnp.where(lane == h, own_den + other_den * linked, dens)
        edge, edge_den = weigh(kv_in_ref[2 * rows :, at], k_in)
        edge_ref[:, at] = dot((edge * linked).astype(BF16), v_in)
        edge_dens = jnp.where(edge_lane == h, edge_den * linked, edge_dens)
    den_ref[...] = dens
    edge_ref[:, width:] = edge_dens


def attend_paired(info, q, kv, mask, tp_count):
    kv_in = lax.ppermute(kv, "ctx", [(0, 1), (2, 3)])
    q2, q3 = (lax.ppermute(q, "ctx", [(c, 1)]) for c in (2, 3))
    rows, width = q.shape
    back = ((rows + 2 * EDGE_ROWS, width), BF16)
    body = functools.partial(far_body, tp_count)
    tops = pltpu.VMEM((rows, width), F32)
    back2, given, done = staged(
        body,
        [kv_in, q2],
        [back],
        [((EDGE_ROWS, width + LANES), F32), TOKEN],
        [tops, pltpu.VMEM((rows, LANES), F32)],
        info,
        held=[kv],
    )
    back2 = lax.ppermute(back2, "ctx", [(1, 2)])
    back3 = staged(body, [kv_in, q3, given], [back], scratch=[tops], info=info, held=[kv])[0]
    back3 = lax.ppermute(back3, "ctx", [(1, 3)])
    back = [back2, back3]
    top, den, edge = staged(
        near_body,
        [kv_in, mask, done],
        [],
        [((rows, width), F32), ((rows, LANES), F32), ((EDGE_ROWS, width + LANES), F32)],
        info=info,
        held=[q, kv],
    )
    return top, den, edge, back


def attend_all_body(tp_count, info_ref, mask_ref, q_ref, k_ref, v_ref, top_ref, den_ref, edge_ref):
    rows, width = q_ref.shape
    allowed = mask_ref[...] > 0
    lane = lax.broadcasted_iota(jnp.int32, den_ref.shape, 1)
    dens = jnp.zeros(den_ref.shape, F32)
    heads = heads_of(width)
    for h, at in enumerate(heads):
        scores = dot(q_ref[:, at], k_ref[:, at], ((1,), (1,))) * (1.0 / math.sqrt(HEAD_DIM))
        expo = jnp.where(allowed, jnp.exp(scores), 0.0)
        top_ref[:, at] = dot(expo.astype(BF16), v_ref[:, at])
        dens = jnp.where(lane == h, jnp.sum(expo, axis=-1, keepdims=True), dens)
    den_ref[...] = dens
    last = last_row(info_ref, rows, tp_count)
    count = edge_ref.shape[0]
    top = jnp.broadcast_to(top_ref[pl.ds(last, 1), :], (count, width))
    den = jnp.broadcast_to(den_ref[pl.ds(last, 1), :], (count, LANES))
    edge_ref[:, :width] = top
    edge_ref[:, width:] = den


def attend_all(info, q, kv, mask, tp_count):
    planes = lax.axis_size("ctx")
    rows, width = q.shape
    keys = lax.all_gather(kv[:rows], "ctx", axis=0, tiled=True)
    values = lax.all_gather(kv[rows : 2 * rows], "ctx", axis=0, tiled=True)
    here = pl.BlockSpec(memory_space=pltpu.VMEM)
    outs = [((rows, width), F32), ((rows, LANES), F32), ((EDGE_ROWS, width + LANES), F32)]
    top, den, edge = pl.pallas_call(
        functools.partial(attend_all_body, tp_count),
        in_specs=[pl.BlockSpec(memory_space=pltpu.SMEM)] + [here] * 4,
        out_specs=[here] * 3,
        out_shape=[jax.ShapeDtypeStruct(shape, dtype) for shape, dtype in outs],
        compiler_params=params(48),
    )(info, mask, q, keys, values)
    edge = lax.ppermute(edge, "ctx", [(c, c + 1) for c in range(planes - 1)])
    return top, den, edge, []


def output_body(count, tp_count, info_ref, *refs):
    back_refs = refs[:count]
    top_ref, den_ref, edge_ref, w_ref, odd_out, even_ref, whole, odd_ref, out_sems = refs[count:]
    depth = w_ref.shape[0]
    blocks, _, step = odd_ref.shape
    rows = top_ref.shape[0]
    heads = heads_of(depth)
    edges = []

    back_dens = []
    for ref in back_refs:
        turned = ref[rows + EDGE_ROWS :, : den_lanes(rows)].astype(F32)
        rest = jnp.zeros((LANES - EDGE_ROWS, turned.shape[1]), F32)
        back_dens.append(jnp.concatenate([turned, rest], axis=0).T)

    for h, lanes in enumerate(heads):
        top, den = top_ref[:, lanes], den_ref[:, h : h + 1]
        edge, edge_den = edge_ref[:, lanes], edge_ref[:, depth + h : depth + h + 1]
        for ref in back_refs:
            top += ref[:rows, lanes].astype(F32)
            edge += ref[rows : rows + EDGE_ROWS, lanes].astype(F32)
        for value in back_dens:
            both = value[:, h : h + 1] + value[:, len(heads) + h : len(heads) + h + 1]
            den += both[:rows]
            edge_den += both[rows : rows + EDGE_ROWS]
        whole[:, lanes] = top / den
        edges.append(jnp.where(edge_den > 0, edge / jnp.where(edge_den > 0, edge_den, 1.0), 0.0))
    edge = jnp.concatenate(edges, axis=1)[:1]
    patches = rows // tp_count
    me = info_ref[1]
    before = []
    for bits in block_order(tp_count):
        peer = me ^ bits
        source = block_place(me ^ ((peer + tp_count - 1) % tp_count), tp_count)
        row = whole[pl.ds(source * patches + patches - 1, 1), :]
        before.append(jnp.where(peer == 0, edge, row))
    for index, row in enumerate(before):
        at = index * patches + patches - 1
        whole[at : at + 1, :] = row
    attended = whole[...].astype(BF16)
    half = rows // 2
    sends = []
    for n in range(blocks):
        at = pl.ds(n * step, step)
        out = dot(attended, w_ref[:, at])
        odd_ref[n] = out[half:].astype(BF16)
        sends.append(pltpu.make_async_copy(odd_ref.at[n], odd_out.at[:, at], out_sems.at[n]))
        sends[-1].start()
        even_ref[:, at] = out[:half].astype(BF16)
    for copy in sends:
        copy.wait()


def output_project(info, top, den, edge, back, weights, tp_count):
    rows, depth = top.shape
    width = weights.shape[1]
    step = min(width, 1024)
    here, there = pl.BlockSpec(memory_space=pltpu.VMEM), pl.BlockSpec(memory_space=pltpu.HBM)
    blocks = width // step
    odd, even = pl.pallas_call(
        functools.partial(output_body, len(back), tp_count),
        in_specs=[pl.BlockSpec(memory_space=pltpu.SMEM)] + [here] * (4 + len(back)),
        out_specs=[there, here],
        out_shape=[
            pltpu.HBM((rows // 2, width), BF16),
            jax.ShapeDtypeStruct((rows // 2, width), BF16),
        ],
        scratch_shapes=[
            pltpu.VMEM((rows, depth), F32),
            pltpu.VMEM((blocks, rows // 2, step), BF16),
            pltpu.SemaphoreType.DMA((blocks,)),
        ],
        compiler_params=params(16),
    )(info, *back, top, den, edge, weights)
    return even, odd


def pair_sum_body(mine_ref, other_ref, own_ref, *send_refs):
    patches = own_ref.shape[0]
    total = mine_ref[...].astype(F32) + other_ref[...].astype(F32)
    own_ref[...] = total[:patches]
    for index, ref in enumerate(send_refs):
        ref[...] = total[(index + 1) * patches : (index + 2) * patches].astype(BF16)


def scatter_sum(even, odd, patches):
    blocks = even.shape[0] // patches
    block = (patches, even.shape[1])
    pieces = call(pair_sum_body, [(block, F32)] + [(block, BF16)] * (blocks - 1))(
        even, swap(odd, 1)
    )
    return [pieces[0]] + [swap(piece, 2 * (index + 1)) for index, piece in enumerate(pieces[1:])]


def state_body(count, *refs):
    terms = refs[:count]
    local_ref, normed, state_out, normed_ref, wide = refs[count:]
    patches = terms[0].shape[0]
    width = normed_ref.shape[1]
    chunks = width // LANES
    for b in range(PATCH):
        at = slice(b * width, (b + 1) * width)
        total = terms[0][:, at]
        for term in terms[1:]:
            total += term[:, at].astype(F32)
        part = pltpu.roll(total.astype(BF16).astype(F32), 1, 0)
        for c in range(chunks):
            wide[c, pl.ds(b, patches, stride=PATCH), :] = part[:, c * LANES : (c + 1) * LANES]
    context = jnp.concatenate([wide[c] for c in range(chunks)], axis=1)
    state = local_ref[...].astype(F32) + context
    state_out.ref[...] = state
    state_out.send()
    mean = jnp.mean(state * state, axis=-1, keepdims=True)
    normed_ref[...] = (state * lax.rsqrt(mean + EPS)).astype(BF16)
    normed.ref[...] = normed_ref[...]


def byte_state(terms, local_embeds, after):
    rows, width = local_embeds.shape
    normed, state, normed_near = staged(
        functools.partial(state_body, len(terms)),
        [*terms, local_embeds],
        [((rows, width), BF16), ((rows, width), F32)],
        [((rows, width), BF16)],
        [pltpu.VMEM((width // LANES, rows, LANES), F32)],
        after=after,
    )
    return state, normed, normed_near


def unit(x):
    scale = lax.rsqrt(jnp.mean(x * x, axis=-1, keepdims=True) + EPS)
    return x * scale, scale


def unit_back(grad, y, scale):
    return scale * (grad - y * jnp.mean(grad * y, axis=-1, keepdims=True))


def prepare_body(parts, info_ref, gb_ref, wq_ref, wk_ref, wv_ref, wo_ref, token_ref, *refs):
    token_ref[...] = jnp.zeros_like(token_ref)
    weights_ref = refs[0]
    d = LOCAL_HEAD_DIM
    rows = refs[1].shape[0] // len(parts[0])
    for kind, ref in enumerate((wq_ref, wk_ref, wv_ref)):
        weights_ref[:, kind * d : (kind + 1) * d] = ref[0]
    for index, part in enumerate(parts):
        out_ref, core_ref = refs[1 + 2 * index : 3 + 2 * index]
        for place, bits in enumerate(part):
            at = pl.multiple_of((info_ref[1] ^ bits) * rows, rows)
            out_ref[place * rows : (place + 1) * rows, :] = gb_ref[pl.ds(at, rows), :]
        core_ref[...] = dot(out_ref[...], wo_ref[0], ((1,), (1,))).astype(BF16)


def prepare(info, gb_all, local_qkv, local_out, rows, parts):
    width = gb_all.shape[1]
    d = LOCAL_HEAD_DIM
    heads = LOCAL_HEADS

    def qkv_spec(kind):
        return pl.BlockSpec((1, width, d), lambda i, info: (0, 0, kind * heads + info[0]))

    outs = [(width, 3 * d)]
    for part in parts:
        outs += [(len(part) * rows, width), (len(part) * rows, d)]
    token, weights, *blocks = pl.pallas_call(
        functools.partial(prepare_body, parts),
        grid_spec=pltpu.PrefetchScalarGridSpec(
            num_scalar_prefetch=1,
            grid=(1,),
            in_specs=[
                pl.BlockSpec(gb_all.shape, lambda i, info: (0, 0)),
                qkv_spec(0),
                qkv_spec(1),
                qkv_spec(2),
                pl.BlockSpec((1, d, width), lambda i, info: (0, info[0], 0)),
            ],
            out_specs=[pl.BlockSpec(shape, lambda i, info: (0, 0)) for shape in [TOKEN.shape, *outs]],
        ),
        out_shape=[TOKEN] + [jax.ShapeDtypeStruct(shape, BF16) for shape in outs],
        compiler_params=params(LARGE),
    )(info, gb_all, local_qkv, local_qkv, local_qkv, local_out)
    return token, weights, blocks[0::2], blocks[1::2]


def window(rows):
    row = lax.broadcasted_iota(jnp.int32, (rows, rows), 0)
    column = lax.broadcasted_iota(jnp.int32, (rows, rows), 1)
    return (row // PATCH == column // PATCH) & (column <= row)


def core_weights(qkv, allowed):
    d = LOCAL_HEAD_DIM
    q, q_scale = unit(qkv[:, :d])
    k, k_scale = unit(qkv[:, d : 2 * d])
    qb, kb, vb = q.astype(BF16), k.astype(BF16), qkv[:, 2 * d :].astype(BF16)
    expo = jnp.where(allowed, jnp.exp(dot(qb, kb, ((1,), (1,))) * (1.0 / math.sqrt(d))), 0.0)
    weight = expo / jnp.sum(expo, axis=-1, keepdims=True)
    return (q, q_scale, qb), (k, k_scale, kb), vb, weight


def core_forward(weight, vb):
    return dot(weight.astype(BF16), vb).astype(BF16)


def core_backward(query, key, vb, weight, gradb):
    q, q_scale, qb = query
    k, k_scale, kb = key
    grad_v = dot(weight.astype(BF16), gradb, ((0,), (0,)))
    grad_w = dot(gradb, vb, ((1,), (1,)))
    mean = jnp.sum(weight * grad_w, axis=-1, keepdims=True)
    grad_s = (weight * (grad_w - mean) * (1.0 / math.sqrt(LOCAL_HEAD_DIM))).astype(BF16)
    grad_q = unit_back(dot(grad_s, kb), q, q_scale)
    grad_k = unit_back(dot(grad_s, qb, ((0,), (0,))), k, k_scale)
    return jnp.concatenate([grad_q, grad_k, grad_v], axis=1).astype(BF16)


def chunks_in(piece):
    return jnp.concatenate(
        [piece[:, at : at + LANES] for at in range(0, piece.shape[1], LANES)], axis=0
    )


def chunks_out(value, rows):
    return jnp.concatenate(
        [value[at : at + rows] for at in range(0, value.shape[0], rows)], axis=1
    )


def rows_of(refs):
    return jnp.concatenate([ref[...] for ref in refs], axis=0)


def local_body(count, *refs):
    x_refs, refs = refs[:count], refs[count:]
    (gb_ref, core_ref, w_ref), refs = refs[:3], refs[3:]
    carry, (gqkv_ref, gout_ref, ab_ref, token_ref) = refs[:-4], refs[-4:]
    token_ref[...] = jnp.zeros_like(token_ref)
    gqkv, gout, abs_ = local_grads(x_refs, gb_ref, core_ref, w_ref, carry)
    gqkv_ref[...] = gqkv
    gout_ref[...] = gout
    ab_ref[...] = jnp.concatenate(abs_, axis=0)


def local_grads(x_refs, gb_ref, core_ref, w_ref, carry):
    x = rows_of(x_refs)
    rows = x_refs[0].shape[0]
    tile = rows // 2 if rows % (2 * BF16_ROWS) == 0 else rows
    allowed = window(tile)
    qkv = dot(x, w_ref[...])
    abs_, gqs = [], []
    for start in range(0, x.shape[0], tile):
        at = slice(start, start + tile)
        query, key, vb, weight = core_weights(qkv[at], allowed)
        abs_.append(core_forward(weight, vb))
        gqs.append(core_backward(query, key, vb, weight, core_ref[at, :]))
    gqkv = dot(jnp.concatenate(gqs, axis=0), x, ((0,), (0,)))
    gout = dot(jnp.concatenate(abs_, axis=0), gb_ref[...], ((0,), (0,)))
    if carry:
        gqkv += carry[0][...]
        gout += carry[1][...]
    return gqkv, gout, abs_


def local_last_body(count, rounds, info_ref, *refs):
    x_refs, refs = refs[:count], refs[count:]
    gb_ref, core_ref, w_ref, *refs = refs
    *carry, ab0_ref = refs[:3]
    gqkv_out, message, *pieces = refs[3 : 4 + rounds]
    own_ref, held = refs[4 + rounds :]
    gqkv, gout, abs_ = local_grads(x_refs, gb_ref, core_ref, w_ref, carry)
    held[...] = gout
    deep = own_ref.shape[0]
    piece_rows = deep * LANES // held.shape[1]
    for k in range(rounds):
        at = pl.multiple_of((info_ref[2] ^ k) * piece_rows, piece_rows)
        piece = chunks_in(held[pl.ds(at, piece_rows), :]).astype(BF16)
        if k:
            pieces[k - 1].ref[...] = piece
            pieces[k - 1].send()
        else:
            own_ref[...] = piece
    gqkv_out.ref[...] = gqkv.T.astype(BF16)
    gqkv_out.send()
    rows = x_refs[0].shape[0]
    message.ref[:rows, :] = ab0_ref[rows:, :]
    message.ref[rows:, :] = jnp.concatenate(abs_, axis=0)


def relay_body(count, rounds, planes, info_ref, *refs):
    (ab0_ref, ab1_ref, there_ref), refs = refs[:3], refs[3:]
    pieces, refs = refs[:rounds], refs[rounds:]
    messages, outs, (own_ref, held) = refs[:count], refs[count : count + planes], refs[count + planes :]
    rows = ab0_ref.shape[0] // 2
    for k, piece in enumerate(pieces):
        held[k] = piece[...].astype(F32)
    for z, out in enumerate(outs):
        total = None
        for outer in range(rounds // planes):
            term = held[info_ref[2] ^ ((info_ref[3] ^ z) + outer * planes)]
            total = term if total is None else total + term
        out.ref[...] = total.astype(BF16)
        out.send()
    for k in range(count + 1):
        mine = ab0_ref[:rows, :] if k == 0 else ab1_ref[(k - 1) * rows : k * rows, :]
        target = messages[k - 1].ref if k else own_ref
        target[:rows, :] = mine
        target[rows:, :] = there_ref[k * rows : (k + 1) * rows, :]
        if k:
            messages[k - 1].send()


def local_layer(normed, normed_near, info, parts, gbs, cores, weights, rounds, planes):
    rows, width = normed.shape
    d = LOCAL_HEAD_DIM
    near = [swap(normed, bits) for bits in parts[1]]
    count = len(near)
    totals = [((3 * d, width), F32), ((d, width), F32)]

    def step(index, xs, carry):
        return staged(
            functools.partial(local_body, len(xs)),
            [*xs, gbs[index], cores[index], weights, *carry],
            [],
            [*totals, ((len(xs) * rows, d), BF16), TOKEN],
            flops=1 << 34,
            mib=20,
        )

    *carry, ab0, done = step(0, [normed_near, swap(normed, 1)], [])
    near = [tie(block, done) for block in near]
    far = [swap(block, 1) for block in near]
    *carry, ab1, _ = step(1, near, carry)
    deep = d // rounds * width // LANES
    piece = ((deep, d), BF16)
    grad_qkv, message, *pieces, own = staged(
        functools.partial(local_last_body, count, rounds),
        [*far, gbs[2], cores[2], weights, *carry, ab0],
        [((width, 3 * d), BF16), (((count + 1) * rows, d), BF16)] + [piece] * (rounds - 1),
        [piece],
        [pltpu.VMEM((d, width), F32)],
        info,
        flops=1 << 34,
        mib=20,
    )
    pieces = [own] + [swap(value, k + 1) for k, value in enumerate(pieces)]
    block = ((2 * rows, d), BF16)
    *sent, own = staged(
        functools.partial(relay_body, count, rounds, planes),
        [ab0, ab1, swap(message, 1), *pieces],
        [block] * count + [piece] * planes,
        [block],
        [pltpu.VMEM((rounds, deep, d), F32)],
        info,
    )
    messages = [own] + [swap(value, 2 * (k + 1)) for k, value in enumerate(sent[:count])]
    return messages, sent[count:], grad_qkv


def hidden_body(heads, count, info_ref, state_ref, w_ref, *refs):
    *messages, out_ref, token_ref = refs
    token_ref[...] = jnp.zeros_like(token_ref)
    rows = state_ref.shape[0]
    d = LOCAL_HEAD_DIM
    total = state_ref[...]
    for bits in range(2 * count + 2):
        at = bits % 2 * rows
        head = heads(info_ref[1] ^ bits)
        weights = w_ref[0, pl.ds(pl.multiple_of(head * d, d), d), :]
        total += dot(messages[bits // 2][at : at + rows, :], weights)
    out_ref[...] = total.astype(BF16)


def final_body(heads, parts_ref, _, *refs):
    *terms, gqkv_ref, gout_ref = refs
    gout = sum(term[...].astype(F32) for term in terms)
    gout_ref[0] = chunks_out(gout, gout_ref.shape[1])
    d = LOCAL_HEAD_DIM
    tp_count = len(heads)
    for h in range(LOCAL_HEADS):
        total = None
        for source in range(parts_ref.shape[0]):
            if heads[source % tp_count] == h:
                term = parts_ref[source].astype(F32)
                total = term if total is None else total + term
        for kind in range(3):
            at = (kind * LOCAL_HEADS + h) * d
            gqkv_ref[0, :, at : at + d] = total[:, kind * d : (kind + 1) * d]


def swap_planes(pieces):
    count = len(pieces)
    return [pieces[0]] + [
        lax.ppermute(pieces[k], "ctx", [(c, c ^ k) for c in range(count)]) for k in range(1, count)
    ]


def per_device(byte_embeds, local_embeds, global_qkv, global_out, local_qkv, local_out, cotangent):
    byte_count, width = byte_embeds.shape
    patches = byte_count // PATCH
    planes, tp_count = lax.axis_size("ctx"), lax.axis_size("tp")
    plane, me = lax.axis_index("ctx"), lax.axis_index("tp")
    order = block_order(tp_count)
    shard_rows = tp_count * patches
    devices = planes * tp_count

    group = min(tp_count, LOCAL_HEADS)
    share = width // devices
    rounds = LOCAL_HEAD_DIM // share
    plane_heads = LOCAL_HEADS // planes

    def head_of(t):
        return (t % rounds) % planes * plane_heads + t // rounds

    heads = [head_of(t) for t in range(tp_count)]
    head_info = jnp.stack([head_of(me), me, me % rounds, plane]).astype(jnp.int32)

    patch_in = patch_norm(byte_embeds)
    mine = swap(patch_in, 1)
    weights_in, head_info = preload(global_qkv, head_info, mine)
    even = [tie(swap(patch_in, bits), head_info) for bits in range(2, tp_count, 2)]
    pieces = [patch_in, *even, mine, *(swap(piece, 1) for piece in even)]
    q, kv, gb = project(head_info, pieces, weights_in, global_qkv, cotangent, tp_count)

    place = (
        (me ^ jnp.array(order, jnp.int32))[:, None] * patches
        + jnp.arange(patches, dtype=jnp.int32)[None, :]
    ).reshape(-1)
    if planes == 4 and den_lanes(shard_rows) <= q.shape[1]:
        mask = (place[None, :] <= place[:, None]).astype(F32)
        top, den, edge, back = attend_paired(
            head_info, q, kv, mask, tp_count
        )
    else:
        key_place = (
            jnp.arange(planes, dtype=jnp.int32)[:, None] * shard_rows + place[None, :]
        ).reshape(-1)
        mask = (key_place[None, :] <= (plane * shard_rows + place)[:, None]).astype(F32)
        top, den, edge, back = attend_all(head_info, q, kv, mask, tp_count)

    weights_out, _ = preload(global_out, head_info, den)
    even, odd = output_project(head_info, top, den, edge, back, weights_out, tp_count)

    parts = [[0, 1], list(range(2, group, 2)), list(range(3, group, 2))]
    gb_all = lax.all_gather(gb, "tp", axis=0, tiled=True)
    prepared, weights, gbs, cores = prepare(head_info, gb_all, local_qkv, local_out, byte_count, parts)
    state, normed, normed_near = byte_state(
        scatter_sum(even, odd, patches), local_embeds, prepared
    )
    messages, out_pieces, grad_qkv = local_layer(
        normed, normed_near, head_info, parts, gbs, cores, weights, rounds, planes
    )
    grad_qkv = lax.all_to_all(grad_qkv, ("ctx", "tp"), 0, 0, tiled=True)
    count = group // 2 - 1
    out_pieces = swap_planes(out_pieces)
    here = pl.BlockSpec(memory_space=pltpu.VMEM)
    hidden, done = pl.pallas_call(
        functools.partial(hidden_body, head_of, count),
        in_specs=[pl.BlockSpec(memory_space=pltpu.SMEM)] + [here] * (3 + count),
        out_specs=[here, here],
        out_shape=[jax.ShapeDtypeStruct((byte_count, width), BF16), TOKEN],
        compiler_params=params(16),
    )(head_info, state, local_out, *messages[: count + 1])
    grad_qkv, grad_out = call(
        functools.partial(final_body, heads),
        [((1, share, 3 * width), F32), ((1, share, width), F32)],
        mib=16,
    )(grad_qkv.reshape(devices, share, 3 * LOCAL_HEAD_DIM), done, *out_pieces)
    return (hidden, grad_qkv, grad_out)


def solution(mesh):
    in_specs = (
        P(("ctx", "tp"), None),
        P(("ctx", "tp"), None),
        P(None, None, "tp"),
        P("tp", None),
        P(),
        P(),
        P(("ctx", "tp"), None),
    )
    out_specs = (P(("ctx", "tp"), None), P(None, ("ctx", "tp"), None), P(None, ("ctx", "tp"), None))
    return jax.shard_map(
        per_device, mesh=mesh, in_specs=in_specs, out_specs=out_specs, check_vma=False
    )
```

```python
import functools
import math

import jax
import jax.numpy as jnp
from jax import lax
from jax.experimental import pallas as pl
from jax.experimental.pallas import tpu as pltpu
from jax.sharding import PartitionSpec as P

PATCH = 8
HEAD_DIM = 128
LOCAL_HEADS = 8
LOCAL_HEAD_DIM = 128
EPS = 1e-06
F32 = jnp.float32
BF16 = jnp.bfloat16
MIB = 1 << 20
LARGE = 60
TOKEN = pltpu.VMEM((8, 128), jnp.float32)
LANES = 128
EDGE_ROWS = 16
BF16_ROWS = 16


def params(mib):
    return pltpu.CompilerParams(vmem_limit_bytes=mib * MIB)


def call(body, outs, scratch=(), mib=32):
    return pl.pallas_call(
        body,
        out_shape=[out if out is TOKEN else jax.ShapeDtypeStruct(*out) for out in outs],
        scratch_shapes=list(scratch),
        compiler_params=params(mib),
    )


class Held:
    def __init__(self, source, target, sem):
        self.ref, self.copy, self.waited = target, pltpu.make_async_copy(source, target, sem), False
        self.copy.start()

    def __call__(self):
        if not self.waited:
            self.copy.wait()
            self.waited = True
        return self.ref


class Sent:
    def __init__(self, source, target, sem):
        self.ref, self.copy, self.started = source, pltpu.make_async_copy(source, target, sem), False

    def send(self):
        self.copy.start()
        self.started = True


def staged(body, args, sent, outs=(), scratch=(), info=None, mib=16, flops=0, after=None, held=()):
    tokens = [] if after is None else [after]
    counts = [len(args), len(held), len(tokens), len(sent), len(outs)]
    counts += [len(held), len(sent), len(scratch)]

    def kernel(*refs):
        refs = list(refs)
        info_ref = [refs.pop(0)] if info is not None else []
        groups = []
        for count in counts:
            groups.append(refs[:count])
            del refs[:count]
        in_refs, held_far, _, sent_far, out_refs, held_near, sent_near, own = groups
        in_sems, out_sems = refs
        inputs = [Held(f, n, in_sems.at[i]) for i, (f, n) in enumerate(zip(held_far, held_near))]
        outputs = [Sent(n, f, out_sems.at[i]) for i, (f, n) in enumerate(zip(sent_far, sent_near))]
        body(*info_ref, *in_refs, *inputs, *outputs, *out_refs, *own)
        for output in outputs:
            if not output.started:
                output.send()
        for value in inputs:
            value()
        for output in outputs:
            output.copy.wait()

    here, there = pl.BlockSpec(memory_space=pltpu.VMEM), pl.BlockSpec(memory_space=pltpu.HBM)
    free = pl.BlockSpec(memory_space=pl.ANY)
    scalars = [] if info is None else [info]
    return pl.pallas_call(
        kernel,
        in_specs=[pl.BlockSpec(memory_space=pltpu.SMEM)] * len(scalars)
        + [here] * len(args)
        + [free] * (len(held) + len(tokens)),
        out_specs=[there] * len(sent) + [here] * len(outs),
        out_shape=[pltpu.HBM(shape, dtype) for shape, dtype in sent]
        + [out if out is TOKEN else jax.ShapeDtypeStruct(*out) for out in outs],
        scratch_shapes=[pltpu.VMEM(value.shape, value.dtype) for value in held]
        + [pltpu.VMEM(shape, dtype) for shape, dtype in sent]
        + list(scratch)
        + [pltpu.SemaphoreType.DMA((max(1, count),)) for count in (len(held), len(sent))],
        compiler_params=params(mib),
        cost_estimate=pl.CostEstimate(flops=flops, bytes_accessed=1 << 22, transcendentals=0),
    )(*scalars, *args, *held, *tokens)


def dot(a, b, dims=((1,), (0,))):
    return lax.dot_general(a, b, (dims, ((), ())), preferred_element_type=F32)


def swap(value, bits):
    count = lax.axis_size("tp")
    return lax.ppermute(value, "tp", [(source, source ^ bits) for source in range(count)])


def block_order(size):
    return list(range(0, size, 2)) + list(range(1, size, 2))


def gather(value, size):
    even = [value] + [swap(value, bits) for bits in range(2, size, 2)]
    return even + [swap(piece, 1) for piece in even]


def tie_body(*refs):
    pass


def tie(value, *after, mib=1):
    there = pl.BlockSpec(memory_space=pl.ANY)
    return pl.pallas_call(
        tie_body,
        in_specs=[there] * (1 + len(after)),
        out_specs=there,
        out_shape=jax.ShapeDtypeStruct(value.shape, value.dtype),
        input_output_aliases={0: 0},
        compiler_params=params(mib),
    )(value, *after)


def preload_body(parts, info_ref, w_ref, _, out_ref, info_out, sems):
    for index in range(info_ref.shape[0]):
        info_out[index] = info_ref[index]
    source = w_ref.at[0] if len(w_ref.shape) == 3 else w_ref
    size = source.shape[0] // parts
    copies = []
    for part in range(parts):
        at = pl.ds(part * size, size)
        copies.append(pltpu.make_async_copy(source.at[at], out_ref.at[at], sems.at[part]))
        copies[-1].start()
    for copy in copies:
        copy.wait()


def preload(weights, info, after, parts=8):
    there = pl.BlockSpec(memory_space=pl.ANY)
    scalar = pl.BlockSpec(memory_space=pltpu.SMEM)
    shape = weights.shape[-2:]
    return pl.pallas_call(
        functools.partial(preload_body, parts),
        in_specs=[scalar, there, there],
        out_specs=[pl.BlockSpec(memory_space=pltpu.VMEM), scalar],
        out_shape=[
            pltpu.VMEM(shape, weights.dtype),
            jax.ShapeDtypeStruct(info.shape, info.dtype),
        ],
        scratch_shapes=[pltpu.SemaphoreType.DMA((parts,))],
        compiler_params=params(50),
        cost_estimate=pl.CostEstimate(
            flops=0, bytes_accessed=2 * math.prod(shape), transcendentals=0
        ),
    )(info, weights, after)


def patch_norm_body(x_ref, out_ref, wide):
    patches = out_ref.shape[0]
    width = x_ref.shape[1]
    total = jnp.zeros((patches, LANES), F32)
    for c in range(width // LANES):
        wide[c] = x_ref[:, c * LANES : (c + 1) * LANES].astype(F32)
    for c in range(width // LANES):
        for b in range(PATCH):
            part = wide[c, pl.ds(b, patches, stride=PATCH), :]
            total += part * part
    scale = lax.rsqrt(jnp.sum(total, axis=-1, keepdims=True) / (PATCH * width) + EPS)
    for b in range(PATCH):
        for c in range(width // LANES):
            part = wide[c, pl.ds(b, patches, stride=PATCH), :]
            at = b * width + c * LANES
            out_ref[:, at : at + LANES] = (part * scale).astype(BF16)


def patch_norm(byte_embeds):
    rows, width = byte_embeds.shape
    return call(
        patch_norm_body,
        [((rows // PATCH, PATCH * width), BF16)],
        [pltpu.VMEM((width // LANES, rows, LANES), F32)],
        16,
    )(byte_embeds)[0]


def stack(refs):
    return jnp.concatenate([ref[...].astype(F32) for ref in refs], axis=0).astype(BF16)


def project_body(count, tp_count, info_ref, *refs):
    x_refs, refs = refs[:count], refs[count:]
    first_ref, pass_ref, w_ref, q, kv, passed, kv_ref, held, wide, sems = refs
    kinds, rows, _ = held.shape
    depth = math.gcd(rows, 1024)
    copies = {}
    for c in range(kinds):
        for k in range(0, rows, depth):
            at = pl.ds(k, depth)
            copies[c, k] = pltpu.make_async_copy(
                w_ref.at[c + 1, at], held.at[c, at], sems.at[len(copies)]
            )
            copies[c, k].start()
    x = stack(x_refs)
    count_rows = x.shape[0]
    passed.ref[...] = pass_ref[...]
    passed.send()
    for c in range(kinds + 1):
        total = None
        for k in range(0, rows, depth):
            if c:
                copies[c - 1, k].wait()
                w = held[c - 1, k : k + depth, :]
            else:
                w = first_ref[k : k + depth, :]
            term = dot(x[:, k : k + depth], w)
            total = term if total is None else total + term
        for h in range(total.shape[1] // HEAD_DIM):
            at = slice(h * HEAD_DIM, (h + 1) * HEAD_DIM)
            part = total[:, at]
            if c < 2:
                part = part * lax.rsqrt(jnp.mean(part * part, axis=-1, keepdims=True) + EPS)
            if c == 0:
                wide[:, at] = part
            else:
                kv_ref[(c - 1) * count_rows : c * count_rows, at] = part.astype(BF16)
        if c == 0:
            q.ref[...] = wide[...].astype(BF16)
            q.send()
            last = wide[pl.ds(last_row(info_ref, count_rows, tp_count), 1), :]
            spread = jnp.broadcast_to(last, (EDGE_ROWS, last.shape[1]))
            kv_ref[kinds * count_rows :, :] = spread.astype(BF16)


def project(info, pieces, first, weights, passed, tp_count):
    rows = sum(piece.shape[0] for piece in pieces)
    kinds, deep, width = weights.shape
    here, there = pl.BlockSpec(memory_space=pltpu.VMEM), pl.BlockSpec(memory_space=pltpu.HBM)
    outs = [((rows, width), BF16), (((kinds - 1) * rows + EDGE_ROWS, width), BF16)]
    outs.append((passed.shape, passed.dtype))
    count = len(pieces)

    def body(*refs):
        in_refs, refs = refs[: count + 4], refs[count + 4 :]
        far, kv_near, near, (held, wide, sems, out_sems) = refs[:3], refs[3], refs[4:7], refs[7:]
        outputs = [Sent(n, f, out_sems.at[i]) for i, (f, n) in enumerate(zip(far, near))]
        project_body(count, tp_count, *in_refs, *outputs, kv_near, held, wide, sems)
        near[1][...] = kv_near[...]
        outputs[1].send()
        for output in outputs:
            output.copy.wait()

    return pl.pallas_call(
        body,
        in_specs=[pl.BlockSpec(memory_space=pltpu.SMEM)]
        + [here] * (count + 2)
        + [pl.BlockSpec(memory_space=pl.ANY)],
        out_specs=[there] * 3 + [here],
        out_shape=[pltpu.HBM(shape, dtype) for shape, dtype in outs]
        + [jax.ShapeDtypeStruct(*outs[1])],
        scratch_shapes=[pltpu.VMEM(shape, dtype) for shape, dtype in outs]
        + [
            pltpu.VMEM((kinds - 1, deep, width), BF16),
            pltpu.VMEM((rows, width), F32),
            pltpu.SemaphoreType.DMA(((kinds - 1) * deep // math.gcd(deep, 1024),)),
            pltpu.SemaphoreType.DMA((3,)),
        ],
        compiler_params=params(40),
    )(info, *pieces, first, passed, weights)


def heads_of(ref_width):
    return [slice(at, at + HEAD_DIM) for at in range(0, ref_width, HEAD_DIM)]


def last_row(info_ref, rows, tp_count):
    return block_place(info_ref[1] ^ (tp_count - 1), tp_count) * (rows // tp_count) + (
        rows // tp_count - 1
    )


def block_place(bits, size):
    return bits // 2 + (bits % 2) * (size // 2)


def split_den(dens, count):
    high = dens.astype(BF16).astype(F32)
    return high + pltpu.roll(dens - high, count, 1)


ROOT = 1.0 / math.sqrt(HEAD_DIM)


def weigh(q, k):
    expo = jnp.exp(dot(q, k, ((1,), (1,))) * ROOT)
    return expo, jnp.sum(expo, axis=-1, keepdims=True)


def den_lanes(rows):
    return -(-(rows + 1) // LANES) * LANES


def far_body(tp_count, info_ref, kv_ref, kv_in_ref, q3_ref, q2_ref, *refs):
    back3, back2, token_ref, far_top, far_den = refs
    token_ref[...] = jnp.zeros_like(token_ref)
    rows, width = q2_ref.shape
    heads = heads_of(width)
    count = len(heads)
    keys, values = slice(0, rows), slice(rows, 2 * rows)
    last = last_row(info_ref, rows, tp_count)
    spread = den_lanes(rows) - rows

    def sums(q_ref, at_rows, top_ref):
        size = at_rows.stop - at_rows.start
        lane = lax.broadcasted_iota(jnp.int32, (size, LANES), 1)
        dens = jnp.zeros((size, LANES), F32)
        for h, at in enumerate(heads):
            q = q_ref[at_rows, at]
            own, own_den = weigh(q, kv_ref[keys, at])
            other, other_den = weigh(q, kv_in_ref[keys, at])
            top_ref[:size, at] = dot(own.astype(BF16), kv_ref[values, at]) + dot(
                other.astype(BF16), kv_in_ref[values, at]
            )
            dens = jnp.where(lane == h, own_den + other_den, dens)
        return dens

    def fill(back, top, den, edge_top, edge_den):
        back.ref[:rows, :] = top.astype(BF16)
        back.ref[rows : rows + EDGE_ROWS, :] = edge_top.astype(BF16)
        den = jnp.concatenate([den, jnp.broadcast_to(edge_den, (spread, LANES))], axis=0)
        turned = split_den(den, count).T[:EDGE_ROWS].astype(BF16)
        back.ref[rows + EDGE_ROWS :, : turned.shape[1]] = turned
        if turned.shape[1] < width:
            rest = jnp.zeros((EDGE_ROWS, width - turned.shape[1]), BF16)
            back.ref[rows + EDGE_ROWS :, turned.shape[1] :] = rest
        back.send()

    everything = slice(0, rows)
    far_den[...] = sums(q2_ref, everything, far_top.at[0])
    den3 = sums(q3_ref, everything, far_top.at[1])
    row = jnp.broadcast_to(far_top[0, pl.ds(last, 1), :], (EDGE_ROWS, width))
    fill(back3, far_top[1], den3, row, far_den[pl.ds(last, 1), :])
    edge_den = sums(kv_ref, slice(2 * rows, 2 * rows + EDGE_ROWS), far_top.at[1])
    fill(back2, far_top[0], far_den[...], far_top[1, :EDGE_ROWS, :], edge_den[:1])


def near_body(info_ref, kv_ref, kv_in_ref, mask_ref, _, q, top_ref, den_ref, edge_ref):
    q_ref = q()
    rows, width = q_ref.shape
    allowed = mask_ref[...] > 0
    linked = jnp.where(info_ref[3] % 2 == 1, 1.0, 0.0)
    lane = lax.broadcasted_iota(jnp.int32, (rows, LANES), 1)
    edge_lane = lax.broadcasted_iota(jnp.int32, (EDGE_ROWS, LANES), 1)
    dens = jnp.zeros((rows, LANES), F32)
    edge_dens = jnp.zeros((EDGE_ROWS, LANES), F32)
    keys, values = slice(0, rows), slice(rows, 2 * rows)
    for h, at in enumerate(heads_of(width)):
        k, v = kv_ref[keys, at], kv_ref[values, at]
        k_in, v_in = kv_in_ref[keys, at], kv_in_ref[values, at]
        q = q_ref[:, at]
        own = jnp.where(allowed, jnp.exp(dot(q, k, ((1,), (1,))) * ROOT), 0.0)
        own_den = jnp.sum(own, axis=-1, keepdims=True)
        other, other_den = weigh(q, k_in)
        top_ref[:, at] = dot(own.astype(BF16), v) + dot((other * linked).astype(BF16), v_in)
        dens = jnp.where(lane == h, own_den + other_den * linked, dens)
        edge, edge_den = weigh(kv_in_ref[2 * rows :, at], k_in)
        edge_ref[:, at] = dot((edge * linked).astype(BF16), v_in)
        edge_dens = jnp.where(edge_lane == h, edge_den * linked, edge_dens)
    den_ref[...] = dens
    edge_ref[:, width:] = edge_dens


def attend_paired(info, q, kv, kv_near, mask, tp_count):
    kv_in = lax.ppermute(kv, "ctx", [(0, 1), (2, 3)])
    far = [lax.ppermute(q, "ctx", [(c, 1)]) for c in (3, 2)]
    rows, width = q.shape
    back = ((rows + 2 * EDGE_ROWS, width), BF16)
    back3, back2, done = staged(
        functools.partial(far_body, tp_count),
        [kv_near, kv_in, *far],
        [back, back],
        [TOKEN],
        [pltpu.VMEM((2, rows, width), F32), pltpu.VMEM((rows, LANES), F32)],
        info,
    )
    back = [lax.ppermute(back3, "ctx", [(1, 3)]), lax.ppermute(back2, "ctx", [(1, 2)])]
    top, den, edge = staged(
        near_body,
        [kv_near, kv_in, mask, done],
        [],
        [((rows, width), F32), ((rows, LANES), F32), ((EDGE_ROWS, width + LANES), F32)],
        info=info,
        held=[q],
    )
    return top, den, edge, back


def attend_all_body(tp_count, info_ref, mask_ref, q_ref, k_ref, v_ref, top_ref, den_ref, edge_ref):
    rows, width = q_ref.shape
    allowed = mask_ref[...] > 0
    lane = lax.broadcasted_iota(jnp.int32, den_ref.shape, 1)
    dens = jnp.zeros(den_ref.shape, F32)
    heads = heads_of(width)
    for h, at in enumerate(heads):
        scores = dot(q_ref[:, at], k_ref[:, at], ((1,), (1,))) * (1.0 / math.sqrt(HEAD_DIM))
        expo = jnp.where(allowed, jnp.exp(scores), 0.0)
        top_ref[:, at] = dot(expo.astype(BF16), v_ref[:, at])
        dens = jnp.where(lane == h, jnp.sum(expo, axis=-1, keepdims=True), dens)
    den_ref[...] = dens
    last = last_row(info_ref, rows, tp_count)
    count = edge_ref.shape[0]
    top = jnp.broadcast_to(top_ref[pl.ds(last, 1), :], (count, width))
    den = jnp.broadcast_to(den_ref[pl.ds(last, 1), :], (count, LANES))
    edge_ref[:, :width] = top
    edge_ref[:, width:] = den


def attend_all(info, q, kv, mask, tp_count):
    planes = lax.axis_size("ctx")
    rows, width = q.shape
    keys = lax.all_gather(kv[:rows], "ctx", axis=0, tiled=True)
    values = lax.all_gather(kv[rows : 2 * rows], "ctx", axis=0, tiled=True)
    here = pl.BlockSpec(memory_space=pltpu.VMEM)
    outs = [((rows, width), F32), ((rows, LANES), F32), ((EDGE_ROWS, width + LANES), F32)]
    top, den, edge = pl.pallas_call(
        functools.partial(attend_all_body, tp_count),
        in_specs=[pl.BlockSpec(memory_space=pltpu.SMEM)] + [here] * 4,
        out_specs=[here] * 3,
        out_shape=[jax.ShapeDtypeStruct(shape, dtype) for shape, dtype in outs],
        compiler_params=params(48),
    )(info, mask, q, keys, values)
    edge = lax.ppermute(edge, "ctx", [(c, c + 1) for c in range(planes - 1)])
    return top, den, edge, []


def output_body(count, tp_count, info_ref, *refs):
    back_refs = refs[:count]
    top_ref, den_ref, edge_ref, w_ref, odd_out, even_ref, whole, odd_ref, out_sems = refs[count:]
    depth = w_ref.shape[0]
    blocks, _, step = odd_ref.shape
    rows = top_ref.shape[0]
    heads = heads_of(depth)
    edges = []

    back_dens = []
    for ref in back_refs:
        turned = ref[rows + EDGE_ROWS :, : den_lanes(rows)].astype(F32)
        rest = jnp.zeros((LANES - EDGE_ROWS, turned.shape[1]), F32)
        back_dens.append(jnp.concatenate([turned, rest], axis=0).T)

    for h, lanes in enumerate(heads):
        top, den = top_ref[:, lanes], den_ref[:, h : h + 1]
        edge, edge_den = edge_ref[:, lanes], edge_ref[:, depth + h : depth + h + 1]
        for ref in back_refs:
            top += ref[:rows, lanes].astype(F32)
            edge += ref[rows : rows + EDGE_ROWS, lanes].astype(F32)
        for value in back_dens:
            both = value[:, h : h + 1] + value[:, len(heads) + h : len(heads) + h + 1]
            den += both[:rows]
            edge_den += both[rows : rows + EDGE_ROWS]
        whole[:, lanes] = top / den
        edges.append(jnp.where(edge_den > 0, edge / jnp.where(edge_den > 0, edge_den, 1.0), 0.0))
    edge = jnp.concatenate(edges, axis=1)[:1]
    patches = rows // tp_count
    me = info_ref[1]
    before = []
    for bits in block_order(tp_count):
        peer = me ^ bits
        source = block_place(me ^ ((peer + tp_count - 1) % tp_count), tp_count)
        row = whole[pl.ds(source * patches + patches - 1, 1), :]
        before.append(jnp.where(peer == 0, edge, row))
    for index, row in enumerate(before):
        at = index * patches + patches - 1
        whole[at : at + 1, :] = row
    attended = whole[...].astype(BF16)
    half = rows // 2
    sends = []
    for n in range(blocks):
        at = pl.ds(n * step, step)
        out = dot(attended, w_ref[:, at])
        odd_ref[n] = out[half:].astype(BF16)
        sends.append(pltpu.make_async_copy(odd_ref.at[n], odd_out.at[:, at], out_sems.at[n]))
        sends[-1].start()
        even_ref[:, at] = out[:half].astype(BF16)
    for copy in sends:
        copy.wait()


def output_project(info, top, den, edge, back, weights, tp_count):
    rows, depth = top.shape
    width = weights.shape[1]
    step = min(width, 1024)
    here, there = pl.BlockSpec(memory_space=pltpu.VMEM), pl.BlockSpec(memory_space=pltpu.HBM)
    blocks = width // step
    odd, even = pl.pallas_call(
        functools.partial(output_body, len(back), tp_count),
        in_specs=[pl.BlockSpec(memory_space=pltpu.SMEM)] + [here] * (4 + len(back)),
        out_specs=[there, here],
        out_shape=[
            pltpu.HBM((rows // 2, width), BF16),
            jax.ShapeDtypeStruct((rows // 2, width), BF16),
        ],
        scratch_shapes=[
            pltpu.VMEM((rows, depth), F32),
            pltpu.VMEM((blocks, rows // 2, step), BF16),
            pltpu.SemaphoreType.DMA((blocks,)),
        ],
        compiler_params=params(16),
    )(info, *back, top, den, edge, weights)
    return even, odd


def pair_sum_body(mine_ref, other_ref, own_ref, *send_refs):
    patches = own_ref.shape[0]
    total = mine_ref[...].astype(F32) + other_ref[...].astype(F32)
    own_ref[...] = total[:patches]
    for index, ref in enumerate(send_refs):
        ref[...] = total[(index + 1) * patches : (index + 2) * patches].astype(BF16)


def scatter_sum(even, odd, patches):
    blocks = even.shape[0] // patches
    block = (patches, even.shape[1])
    pieces = call(pair_sum_body, [(block, F32)] + [(block, BF16)] * (blocks - 1))(
        even, swap(odd, 1)
    )
    return [pieces[0]] + [swap(piece, 2 * (index + 1)) for index, piece in enumerate(pieces[1:])]


def state_body(count, *refs):
    terms = refs[:count]
    local_ref, normed, state_out, normed_ref, wide = refs[count:]
    patches = terms[0].shape[0]
    width = normed_ref.shape[1]
    chunks = width // LANES
    for b in range(PATCH):
        at = slice(b * width, (b + 1) * width)
        total = terms[0][:, at]
        for term in terms[1:]:
            total += term[:, at].astype(F32)
        part = pltpu.roll(total.astype(BF16).astype(F32), 1, 0)
        for c in range(chunks):
            wide[c, pl.ds(b, patches, stride=PATCH), :] = part[:, c * LANES : (c + 1) * LANES]
    context = jnp.concatenate([wide[c] for c in range(chunks)], axis=1)
    state = local_ref[...].astype(F32) + context
    state_out.ref[...] = state
    state_out.send()
    mean = jnp.mean(state * state, axis=-1, keepdims=True)
    normed_ref[...] = (state * lax.rsqrt(mean + EPS)).astype(BF16)
    normed.ref[...] = normed_ref[...]


def byte_state(terms, local_embeds, after):
    rows, width = local_embeds.shape
    normed, state, normed_near = staged(
        functools.partial(state_body, len(terms)),
        [*terms, local_embeds],
        [((rows, width), BF16), ((rows, width), F32)],
        [((rows, width), BF16)],
        [pltpu.VMEM((width // LANES, rows, LANES), F32)],
        after=after,
    )
    return state, normed, normed_near


def unit(x):
    scale = lax.rsqrt(jnp.mean(x * x, axis=-1, keepdims=True) + EPS)
    return x * scale, scale


def unit_back(grad, y, scale):
    return scale * (grad - y * jnp.mean(grad * y, axis=-1, keepdims=True))


def prepare_body(parts, info_ref, gb_ref, wq_ref, wk_ref, wv_ref, wo_ref, token_ref, *refs):
    token_ref[...] = jnp.zeros_like(token_ref)
    weights_ref = refs[0]
    d = LOCAL_HEAD_DIM
    rows = refs[1].shape[0] // len(parts[0])
    for kind, ref in enumerate((wq_ref, wk_ref, wv_ref)):
        weights_ref[:, kind * d : (kind + 1) * d] = ref[0]
    for index, part in enumerate(parts):
        out_ref, core_ref = refs[1 + 2 * index : 3 + 2 * index]
        for place, bits in enumerate(part):
            at = pl.multiple_of((info_ref[1] ^ bits) * rows, rows)
            out_ref[place * rows : (place + 1) * rows, :] = gb_ref[pl.ds(at, rows), :]
        core_ref[...] = dot(out_ref[...], wo_ref[0], ((1,), (1,))).astype(BF16)


def prepare(info, gb_all, local_qkv, local_out, rows, parts):
    width = gb_all.shape[1]
    d = LOCAL_HEAD_DIM
    heads = LOCAL_HEADS

    def qkv_spec(kind):
        return pl.BlockSpec((1, width, d), lambda i, info: (0, 0, kind * heads + info[0]))

    outs = [(width, 3 * d)]
    for part in parts:
        outs += [(len(part) * rows, width), (len(part) * rows, d)]
    token, weights, *blocks = pl.pallas_call(
        functools.partial(prepare_body, parts),
        grid_spec=pltpu.PrefetchScalarGridSpec(
            num_scalar_prefetch=1,
            grid=(1,),
            in_specs=[
                pl.BlockSpec(gb_all.shape, lambda i, info: (0, 0)),
                qkv_spec(0),
                qkv_spec(1),
                qkv_spec(2),
                pl.BlockSpec((1, d, width), lambda i, info: (0, info[0], 0)),
            ],
            out_specs=[pl.BlockSpec(shape, lambda i, info: (0, 0)) for shape in [TOKEN.shape, *outs]],
        ),
        out_shape=[TOKEN] + [jax.ShapeDtypeStruct(shape, BF16) for shape in outs],
        compiler_params=params(LARGE),
    )(info, gb_all, local_qkv, local_qkv, local_qkv, local_out)
    return token, weights, blocks[0::2], blocks[1::2]


def window(rows):
    row = lax.broadcasted_iota(jnp.int32, (rows, rows), 0)
    column = lax.broadcasted_iota(jnp.int32, (rows, rows), 1)
    return (row // PATCH == column // PATCH) & (column <= row)


def core_weights(qkv, allowed):
    d = LOCAL_HEAD_DIM
    q, q_scale = unit(qkv[:, :d])
    k, k_scale = unit(qkv[:, d : 2 * d])
    qb, kb, vb = q.astype(BF16), k.astype(BF16), qkv[:, 2 * d :].astype(BF16)
    expo = jnp.where(allowed, jnp.exp(dot(qb, kb, ((1,), (1,))) * (1.0 / math.sqrt(d))), 0.0)
    weight = expo / jnp.sum(expo, axis=-1, keepdims=True)
    return (q, q_scale, qb), (k, k_scale, kb), vb, weight


def core_forward(weight, vb):
    return dot(weight.astype(BF16), vb).astype(BF16)


def core_backward(query, key, vb, weight, gradb):
    q, q_scale, qb = query
    k, k_scale, kb = key
    grad_v = dot(weight.astype(BF16), gradb, ((0,), (0,)))
    grad_w = dot(gradb, vb, ((1,), (1,)))
    mean = jnp.sum(weight * grad_w, axis=-1, keepdims=True)
    grad_s = (weight * (grad_w - mean) * (1.0 / math.sqrt(LOCAL_HEAD_DIM))).astype(BF16)
    grad_q = unit_back(dot(grad_s, kb), q, q_scale)
    grad_k = unit_back(dot(grad_s, qb, ((0,), (0,))), k, k_scale)
    return jnp.concatenate([grad_q, grad_k, grad_v], axis=1).astype(BF16)


def chunks_in(piece):
    return jnp.concatenate(
        [piece[:, at : at + LANES] for at in range(0, piece.shape[1], LANES)], axis=0
    )


def chunks_out(value, rows):
    return jnp.concatenate(
        [value[at : at + rows] for at in range(0, value.shape[0], rows)], axis=1
    )


def rows_of(refs):
    return jnp.concatenate([ref[...] for ref in refs], axis=0)


def local_body(count, *refs):
    x_refs, refs = refs[:count], refs[count:]
    (gb_ref, core_ref, w_ref), refs = refs[:3], refs[3:]
    carry, (gqkv_ref, gout_ref, ab_ref, token_ref) = refs[:-4], refs[-4:]
    token_ref[...] = jnp.zeros_like(token_ref)
    gqkv, gout, abs_ = local_grads(x_refs, gb_ref, core_ref, w_ref, carry)
    gqkv_ref[...] = gqkv
    gout_ref[...] = gout
    ab_ref[...] = jnp.concatenate(abs_, axis=0)


def local_grads(x_refs, gb_ref, core_ref, w_ref, carry):
    x = rows_of(x_refs)
    rows = x_refs[0].shape[0]
    tile = rows // 2 if rows % (2 * BF16_ROWS) == 0 else rows
    allowed = window(tile)
    qkv = dot(x, w_ref[...])
    abs_, gqs = [], []
    for start in range(0, x.shape[0], tile):
        at = slice(start, start + tile)
        query, key, vb, weight = core_weights(qkv[at], allowed)
        abs_.append(core_forward(weight, vb))
        gqs.append(core_backward(query, key, vb, weight, core_ref[at, :]))
    gqkv = dot(jnp.concatenate(gqs, axis=0), x, ((0,), (0,)))
    gout = dot(jnp.concatenate(abs_, axis=0), gb_ref[...], ((0,), (0,)))
    if carry:
        gqkv += carry[0][...]
        gout += carry[1][...]
    return gqkv, gout, abs_


def local_last_body(count, rounds, info_ref, *refs):
    x_refs, refs = refs[:count], refs[count:]
    gb_ref, core_ref, w_ref, *refs = refs
    *carry, ab0_ref = refs[:3]
    gqkv_out, message, *pieces = refs[3 : 4 + rounds]
    own_ref, held = refs[4 + rounds :]
    gqkv, gout, abs_ = local_grads(x_refs, gb_ref, core_ref, w_ref, carry)
    held[...] = gout
    deep = own_ref.shape[0]
    piece_rows = deep * LANES // held.shape[1]
    for k in range(rounds):
        at = pl.multiple_of((info_ref[2] ^ k) * piece_rows, piece_rows)
        piece = chunks_in(held[pl.ds(at, piece_rows), :]).astype(BF16)
        if k:
            pieces[k - 1].ref[...] = piece
            pieces[k - 1].send()
        else:
            own_ref[...] = piece
    gqkv_out.ref[...] = gqkv.T.astype(BF16)
    gqkv_out.send()
    rows = x_refs[0].shape[0]
    message.ref[:rows, :] = ab0_ref[rows:, :]
    message.ref[rows:, :] = jnp.concatenate(abs_, axis=0)


def relay_body(heads, count, rounds, planes, info_ref, state_ref, w_ref, *refs):
    (ab0_ref, ab1_ref, there_ref), refs = refs[:3], refs[3:]
    pieces, refs = refs[:rounds], refs[rounds:]
    messages, outs, (total_ref, held) = refs[:count], refs[count : count + planes], refs[count + planes :]
    rows = ab0_ref.shape[0] // 2
    for k, piece in enumerate(pieces):
        held[k] = piece[...].astype(F32)
    for z, out in enumerate(outs):
        total = None
        for outer in range(rounds // planes):
            term = held[info_ref[2] ^ ((info_ref[3] ^ z) + outer * planes)]
            total = term if total is None else total + term
        out.ref[...] = total.astype(BF16)
        out.send()
    for k, message in enumerate(messages):
        message.ref[:rows, :] = ab1_ref[k * rows : (k + 1) * rows, :]
        message.ref[rows:, :] = there_ref[(k + 1) * rows : (k + 2) * rows, :]
        message.send()
    total = add_heads(heads, info_ref, state_ref[...], w_ref, 0, [ab0_ref[:rows, :]])
    total_ref[...] = add_heads(heads, info_ref, total, w_ref, 1, [there_ref[:rows, :]])


def add_heads(heads, info_ref, total, w_ref, first, values):
    d = LOCAL_HEAD_DIM
    for index, value in enumerate(values):
        head = heads(info_ref[1] ^ (first + index))
        total += dot(value, w_ref[0, pl.ds(pl.multiple_of(head * d, d), d), :])
    return total


def local_layer(
    normed, normed_near, info, parts, gbs, cores, weights, rounds, planes, heads, state, local_out
):
    rows, width = normed.shape
    d = LOCAL_HEAD_DIM
    near = [swap(normed, bits) for bits in parts[1]]
    count = len(near)
    totals = [((3 * d, width), F32), ((d, width), F32)]

    def step(index, xs, carry):
        return staged(
            functools.partial(local_body, len(xs)),
            [*xs, gbs[index], cores[index], weights, *carry],
            [],
            [*totals, ((len(xs) * rows, d), BF16), TOKEN],
            flops=1 << 34,
            mib=20,
        )

    *carry, ab0, done = step(0, [normed_near, swap(normed, 1)], [])
    near = [tie(block, done) for block in near]
    far = [swap(block, 1) for block in near]
    *carry, ab1, _ = step(1, near, carry)
    deep = d // rounds * width // LANES
    piece = ((deep, d), BF16)
    grad_qkv, message, *pieces, own = staged(
        functools.partial(local_last_body, count, rounds),
        [*far, gbs[2], cores[2], weights, *carry, ab0],
        [((width, 3 * d), BF16), (((count + 1) * rows, d), BF16)] + [piece] * (rounds - 1),
        [piece],
        [pltpu.VMEM((d, width), F32)],
        info,
        flops=1 << 34,
        mib=20,
    )
    pieces = [own] + [swap(value, k + 1) for k, value in enumerate(pieces)]
    *sent, total = staged(
        functools.partial(relay_body, heads, count, rounds, planes),
        [state, local_out, ab0, ab1, swap(message, 1), *pieces],
        [((2 * rows, d), BF16)] * count + [piece] * planes,
        [((rows, width), F32)],
        [pltpu.VMEM((rounds, deep, d), F32)],
        info,
    )
    messages = [swap(value, 2 * (k + 1)) for k, value in enumerate(sent[:count])]
    return total, messages, sent[count:], grad_qkv


def hidden_body(heads, info_ref, total_ref, w_ref, *refs):
    *messages, out_ref, token_ref = refs
    token_ref[...] = jnp.zeros_like(token_ref)
    rows = total_ref.shape[0]
    values = [message[at : at + rows, :] for message in messages for at in (0, rows)]
    out_ref[...] = add_heads(heads, info_ref, total_ref[...], w_ref, 2, values).astype(BF16)


def final_body(heads, parts_ref, _, *refs):
    *terms, gqkv_ref, gout_ref = refs
    gout = sum(term[...].astype(F32) for term in terms)
    gout_ref[0] = chunks_out(gout, gout_ref.shape[1])
    d = LOCAL_HEAD_DIM
    tp_count = len(heads)
    for h in range(LOCAL_HEADS):
        total = None
        for source in range(parts_ref.shape[0]):
            if heads[source % tp_count] == h:
                term = parts_ref[source].astype(F32)
                total = term if total is None else total + term
        for kind in range(3):
            at = (kind * LOCAL_HEADS + h) * d
            gqkv_ref[0, :, at : at + d] = total[:, kind * d : (kind + 1) * d]


def swap_planes(pieces):
    count = len(pieces)
    return [pieces[0]] + [
        lax.ppermute(pieces[k], "ctx", [(c, c ^ k) for c in range(count)]) for k in range(1, count)
    ]


def per_device(byte_embeds, local_embeds, global_qkv, global_out, local_qkv, local_out, cotangent):
    byte_count, width = byte_embeds.shape
    patches = byte_count // PATCH
    planes, tp_count = lax.axis_size("ctx"), lax.axis_size("tp")
    plane, me = lax.axis_index("ctx"), lax.axis_index("tp")
    order = block_order(tp_count)
    shard_rows = tp_count * patches
    devices = planes * tp_count

    group = min(tp_count, LOCAL_HEADS)
    share = width // devices
    rounds = LOCAL_HEAD_DIM // share
    plane_heads = LOCAL_HEADS // planes

    def head_of(t):
        return (t % rounds) % planes * plane_heads + t // rounds

    heads = [head_of(t) for t in range(tp_count)]
    head_info = jnp.stack([head_of(me), me, me % rounds, plane]).astype(jnp.int32)

    patch_in = patch_norm(byte_embeds)
    mine = swap(patch_in, 1)
    weights_in, head_info = preload(global_qkv, head_info, mine)
    even = [tie(swap(patch_in, bits), head_info) for bits in range(2, tp_count, 2)]
    pieces = [patch_in, *even, mine, *(swap(piece, 1) for piece in even)]
    q, kv, gb, kv_near = project(head_info, pieces, weights_in, global_qkv, cotangent, tp_count)

    place = (
        (me ^ jnp.array(order, jnp.int32))[:, None] * patches
        + jnp.arange(patches, dtype=jnp.int32)[None, :]
    ).reshape(-1)
    if planes == 4 and den_lanes(shard_rows) <= q.shape[1]:
        mask = (place[None, :] <= place[:, None]).astype(F32)
        top, den, edge, back = attend_paired(
            head_info, q, kv, kv_near, mask, tp_count
        )
    else:
        key_place = (
            jnp.arange(planes, dtype=jnp.int32)[:, None] * shard_rows + place[None, :]
        ).reshape(-1)
        mask = (key_place[None, :] <= (plane * shard_rows + place)[:, None]).astype(F32)
        top, den, edge, back = attend_all(head_info, q, kv, mask, tp_count)

    weights_out, _ = preload(global_out, head_info, den)
    even, odd = output_project(head_info, top, den, edge, back, weights_out, tp_count)

    parts = [[0, 1], list(range(2, group, 2)), list(range(3, group, 2))]
    gb_all = lax.all_gather(gb, "tp", axis=0, tiled=True)
    prepared, weights, gbs, cores = prepare(head_info, gb_all, local_qkv, local_out, byte_count, parts)
    state, normed, normed_near = byte_state(
        scatter_sum(even, odd, patches), local_embeds, prepared
    )
    total, messages, out_pieces, grad_qkv = local_layer(
        normed, normed_near, head_info, parts, gbs, cores, weights, rounds, planes, head_of, state, local_out
    )
    grad_qkv = lax.all_to_all(grad_qkv, ("ctx", "tp"), 0, 0, tiled=True)
    out_pieces = swap_planes(out_pieces)
    here = pl.BlockSpec(memory_space=pltpu.VMEM)
    hidden, done = pl.pallas_call(
        functools.partial(hidden_body, head_of),
        in_specs=[pl.BlockSpec(memory_space=pltpu.SMEM)] + [here] * (2 + len(messages)),
        out_specs=[here, here],
        out_shape=[jax.ShapeDtypeStruct((byte_count, width), BF16), TOKEN],
        compiler_params=params(16),
    )(head_info, total, local_out, *messages)
    grad_qkv, grad_out = call(
        functools.partial(final_body, heads),
        [((1, share, 3 * width), F32), ((1, share, width), F32)],
        mib=16,
    )(grad_qkv.reshape(devices, share, 3 * LOCAL_HEAD_DIM), done, *out_pieces)
    return (hidden, grad_qkv, grad_out)


def solution(mesh):
    in_specs = (
        P(("ctx", "tp"), None),
        P(("ctx", "tp"), None),
        P(None, None, "tp"),
        P("tp", None),
        P(),
        P(),
        P(("ctx", "tp"), None),
    )
    out_specs = (P(("ctx", "tp"), None), P(None, ("ctx", "tp"), None), P(None, ("ctx", "tp"), None))
    return jax.shard_map(
        per_device, mesh=mesh, in_specs=in_specs, out_specs=out_specs, check_vma=False
    )
```

```python
import functools
import math

import jax
import jax.numpy as jnp
from jax import lax
from jax.experimental import pallas as pl
from jax.experimental.pallas import tpu as pltpu
from jax.sharding import PartitionSpec as P

PATCH = 8
HEAD_DIM = 128
LOCAL_HEADS = 8
LOCAL_HEAD_DIM = 128
EPS = 1e-06
F32 = jnp.float32
BF16 = jnp.bfloat16
MIB = 1 << 20
LARGE = 60
TOKEN = pltpu.VMEM((8, 128), jnp.float32)
LANES = 128
EDGE_ROWS = 16
BF16_ROWS = 16


def params(mib):
    return pltpu.CompilerParams(vmem_limit_bytes=mib * MIB)


def call(body, outs, scratch=(), mib=32):
    return pl.pallas_call(
        body,
        out_shape=[out if out is TOKEN else jax.ShapeDtypeStruct(*out) for out in outs],
        scratch_shapes=list(scratch),
        compiler_params=params(mib),
    )


class Held:
    def __init__(self, source, target, sem):
        self.ref, self.copy, self.waited = target, pltpu.make_async_copy(source, target, sem), False
        self.copy.start()

    def __call__(self):
        if not self.waited:
            self.copy.wait()
            self.waited = True
        return self.ref


class Sent:
    def __init__(self, source, target, sem):
        self.ref, self.copy, self.started = source, pltpu.make_async_copy(source, target, sem), False

    def send(self):
        self.copy.start()
        self.started = True


def staged(body, args, sent, outs=(), scratch=(), info=None, mib=16, flops=0, after=None, held=()):
    tokens = [] if after is None else [after]
    counts = [len(args), len(held), len(tokens), len(sent), len(outs)]
    counts += [len(held), len(sent), len(scratch)]

    def kernel(*refs):
        refs = list(refs)
        info_ref = [refs.pop(0)] if info is not None else []
        groups = []
        for count in counts:
            groups.append(refs[:count])
            del refs[:count]
        in_refs, held_far, _, sent_far, out_refs, held_near, sent_near, own = groups
        in_sems, out_sems = refs
        inputs = [Held(f, n, in_sems.at[i]) for i, (f, n) in enumerate(zip(held_far, held_near))]
        outputs = [Sent(n, f, out_sems.at[i]) for i, (f, n) in enumerate(zip(sent_far, sent_near))]
        body(*info_ref, *in_refs, *inputs, *outputs, *out_refs, *own)
        for output in outputs:
            if not output.started:
                output.send()
        for value in inputs:
            value()
        for output in outputs:
            output.copy.wait()

    here, there = pl.BlockSpec(memory_space=pltpu.VMEM), pl.BlockSpec(memory_space=pltpu.HBM)
    free = pl.BlockSpec(memory_space=pl.ANY)
    scalars = [] if info is None else [info]
    return pl.pallas_call(
        kernel,
        in_specs=[pl.BlockSpec(memory_space=pltpu.SMEM)] * len(scalars)
        + [here] * len(args)
        + [free] * (len(held) + len(tokens)),
        out_specs=[there] * len(sent) + [here] * len(outs),
        out_shape=[pltpu.HBM(shape, dtype) for shape, dtype in sent]
        + [out if out is TOKEN else jax.ShapeDtypeStruct(*out) for out in outs],
        scratch_shapes=[pltpu.VMEM(value.shape, value.dtype) for value in held]
        + [pltpu.VMEM(shape, dtype) for shape, dtype in sent]
        + list(scratch)
        + [pltpu.SemaphoreType.DMA((max(1, count),)) for count in (len(held), len(sent))],
        compiler_params=params(mib),
        cost_estimate=pl.CostEstimate(flops=flops, bytes_accessed=1 << 22, transcendentals=0),
    )(*scalars, *args, *held, *tokens)


def dot(a, b, dims=((1,), (0,))):
    return lax.dot_general(a, b, (dims, ((), ())), preferred_element_type=F32)


def swap(value, bits):
    count = lax.axis_size("tp")
    return lax.ppermute(value, "tp", [(source, source ^ bits) for source in range(count)])


def block_order(size):
    return list(range(0, size, 2)) + list(range(1, size, 2))


def gather(value, size):
    even = [value] + [swap(value, bits) for bits in range(2, size, 2)]
    return even + [swap(piece, 1) for piece in even]


def tie_body(*refs):
    pass


def tie(value, *after, mib=1):
    there = pl.BlockSpec(memory_space=pl.ANY)
    return pl.pallas_call(
        tie_body,
        in_specs=[there] * (1 + len(after)),
        out_specs=there,
        out_shape=jax.ShapeDtypeStruct(value.shape, value.dtype),
        input_output_aliases={0: 0},
        compiler_params=params(mib),
    )(value, *after)


def preload_body(parts, info_ref, w_ref, _, out_ref, info_out, sems):
    for index in range(info_ref.shape[0]):
        info_out[index] = info_ref[index]
    source = w_ref.at[0] if len(w_ref.shape) == 3 else w_ref
    size = source.shape[0] // parts
    copies = []
    for part in range(parts):
        at = pl.ds(part * size, size)
        copies.append(pltpu.make_async_copy(source.at[at], out_ref.at[at], sems.at[part]))
        copies[-1].start()
    for copy in copies:
        copy.wait()


def preload(weights, info, after, parts=8):
    there = pl.BlockSpec(memory_space=pl.ANY)
    scalar = pl.BlockSpec(memory_space=pltpu.SMEM)
    shape = weights.shape[-2:]
    return pl.pallas_call(
        functools.partial(preload_body, parts),
        in_specs=[scalar, there, there],
        out_specs=[pl.BlockSpec(memory_space=pltpu.VMEM), scalar],
        out_shape=[
            pltpu.VMEM(shape, weights.dtype),
            jax.ShapeDtypeStruct(info.shape, info.dtype),
        ],
        scratch_shapes=[pltpu.SemaphoreType.DMA((parts,))],
        compiler_params=params(50),
        cost_estimate=pl.CostEstimate(
            flops=0, bytes_accessed=2 * math.prod(shape), transcendentals=0
        ),
    )(info, weights, after)


def patch_norm_body(x_ref, out_ref, wide):
    patches = out_ref.shape[0]
    width = x_ref.shape[1]
    total = jnp.zeros((patches, LANES), F32)
    for c in range(width // LANES):
        wide[c] = x_ref[:, c * LANES : (c + 1) * LANES].astype(F32)
    for c in range(width // LANES):
        for b in range(PATCH):
            part = wide[c, pl.ds(b, patches, stride=PATCH), :]
            total += part * part
    scale = lax.rsqrt(jnp.sum(total, axis=-1, keepdims=True) / (PATCH * width) + EPS)
    for b in range(PATCH):
        for c in range(width // LANES):
            part = wide[c, pl.ds(b, patches, stride=PATCH), :]
            at = b * width + c * LANES
            out_ref[:, at : at + LANES] = (part * scale).astype(BF16)


def patch_norm(byte_embeds):
    rows, width = byte_embeds.shape
    return call(
        patch_norm_body,
        [((rows // PATCH, PATCH * width), BF16)],
        [pltpu.VMEM((width // LANES, rows, LANES), F32)],
        16,
    )(byte_embeds)[0]


def stack(refs):
    return jnp.concatenate([ref[...].astype(F32) for ref in refs], axis=0).astype(BF16)


def project_body(count, tp_count, info_ref, *refs):
    x_refs, refs = refs[:count], refs[count:]
    first_ref, pass_ref, w_ref, q, kv, passed, kv_ref, held, wide, sems = refs
    kinds, rows, _ = held.shape
    depth = math.gcd(rows, 1024)
    copies = {}
    for c in range(kinds):
        for k in range(0, rows, depth):
            at = pl.ds(k, depth)
            copies[c, k] = pltpu.make_async_copy(
                w_ref.at[c + 1, at], held.at[c, at], sems.at[len(copies)]
            )
            copies[c, k].start()
    x = stack(x_refs)
    count_rows = x.shape[0]
    passed.ref[...] = pass_ref[...]
    passed.send()
    for c in range(kinds + 1):
        total = None
        for k in range(0, rows, depth):
            if c:
                copies[c - 1, k].wait()
                w = held[c - 1, k : k + depth, :]
            else:
                w = first_ref[k : k + depth, :]
            term = dot(x[:, k : k + depth], w)
            total = term if total is None else total + term
        for h in range(total.shape[1] // HEAD_DIM):
            at = slice(h * HEAD_DIM, (h + 1) * HEAD_DIM)
            part = total[:, at]
            if c < 2:
                part = part * lax.rsqrt(jnp.mean(part * part, axis=-1, keepdims=True) + EPS)
            if c == 0:
                wide[:, at] = part
            else:
                kv_ref[(c - 1) * count_rows : c * count_rows, at] = part.astype(BF16)
        if c == 0:
            q.ref[...] = wide[...].astype(BF16)
            q.send()
            last = wide[pl.ds(last_row(info_ref, count_rows, tp_count), 1), :]
            spread = jnp.broadcast_to(last, (EDGE_ROWS, last.shape[1]))
            kv_ref[kinds * count_rows :, :] = spread.astype(BF16)


def project(info, pieces, first, weights, passed, tp_count):
    rows = sum(piece.shape[0] for piece in pieces)
    kinds, deep, width = weights.shape
    here, there = pl.BlockSpec(memory_space=pltpu.VMEM), pl.BlockSpec(memory_space=pltpu.HBM)
    outs = [((rows, width), BF16), (((kinds - 1) * rows + EDGE_ROWS, width), BF16)]
    outs.append((passed.shape, passed.dtype))
    count = len(pieces)

    def body(*refs):
        in_refs, refs = refs[: count + 4], refs[count + 4 :]
        far, kv_near, near, (held, wide, sems, out_sems) = refs[:3], refs[3], refs[4:7], refs[7:]
        outputs = [Sent(n, f, out_sems.at[i]) for i, (f, n) in enumerate(zip(far, near))]
        project_body(count, tp_count, *in_refs, *outputs, kv_near, held, wide, sems)
        near[1][...] = kv_near[...]
        outputs[1].send()
        for output in outputs:
            output.copy.wait()

    return pl.pallas_call(
        body,
        in_specs=[pl.BlockSpec(memory_space=pltpu.SMEM)]
        + [here] * (count + 2)
        + [pl.BlockSpec(memory_space=pl.ANY)],
        out_specs=[there] * 3 + [here],
        out_shape=[pltpu.HBM(shape, dtype) for shape, dtype in outs]
        + [jax.ShapeDtypeStruct(*outs[1])],
        scratch_shapes=[pltpu.VMEM(shape, dtype) for shape, dtype in outs]
        + [
            pltpu.VMEM((kinds - 1, deep, width), BF16),
            pltpu.VMEM((rows, width), F32),
            pltpu.SemaphoreType.DMA(((kinds - 1) * deep // math.gcd(deep, 1024),)),
            pltpu.SemaphoreType.DMA((3,)),
        ],
        compiler_params=params(40),
    )(info, *pieces, first, passed, weights)


def heads_of(ref_width):
    return [slice(at, at + HEAD_DIM) for at in range(0, ref_width, HEAD_DIM)]


def last_row(info_ref, rows, tp_count):
    return block_place(info_ref[1] ^ (tp_count - 1), tp_count) * (rows // tp_count) + (
        rows // tp_count - 1
    )


def block_place(bits, size):
    return bits // 2 + (bits % 2) * (size // 2)


def split_den(dens, count):
    high = dens.astype(BF16).astype(F32)
    return high + pltpu.roll(dens - high, count, 1)


ROOT = 1.0 / math.sqrt(HEAD_DIM)


def weigh(q, k):
    expo = jnp.exp(dot(q, k, ((1,), (1,))) * ROOT)
    return expo, jnp.sum(expo, axis=-1, keepdims=True)


def den_lanes(rows):
    return -(-(rows + 1) // LANES) * LANES


def far_body(tp_count, info_ref, kv_ref, kv_in_ref, q3_ref, q2_ref, *refs):
    back3, back2, token_ref, far_top, far_den = refs
    token_ref[...] = jnp.zeros_like(token_ref)
    rows, width = q2_ref.shape
    heads = heads_of(width)
    count = len(heads)
    keys, values = slice(0, rows), slice(rows, 2 * rows)
    last = last_row(info_ref, rows, tp_count)
    spread = den_lanes(rows) - rows

    def sums(q_ref, at_rows, top_ref):
        size = at_rows.stop - at_rows.start
        lane = lax.broadcasted_iota(jnp.int32, (size, LANES), 1)
        dens = jnp.zeros((size, LANES), F32)
        for h, at in enumerate(heads):
            q = q_ref[at_rows, at]
            own, own_den = weigh(q, kv_ref[keys, at])
            other, other_den = weigh(q, kv_in_ref[keys, at])
            top_ref[:size, at] = dot(own.astype(BF16), kv_ref[values, at]) + dot(
                other.astype(BF16), kv_in_ref[values, at]
            )
            dens = jnp.where(lane == h, own_den + other_den, dens)
        return dens

    def fill(back, top, den, edge_top, edge_den):
        back.ref[:rows, :] = top.astype(BF16)
        back.ref[rows : rows + EDGE_ROWS, :] = edge_top.astype(BF16)
        den = jnp.concatenate([den, jnp.broadcast_to(edge_den, (spread, LANES))], axis=0)
        turned = split_den(den, count).T[:EDGE_ROWS].astype(BF16)
        back.ref[rows + EDGE_ROWS :, : turned.shape[1]] = turned
        if turned.shape[1] < width:
            rest = jnp.zeros((EDGE_ROWS, width - turned.shape[1]), BF16)
            back.ref[rows + EDGE_ROWS :, turned.shape[1] :] = rest
        back.send()

    everything = slice(0, rows)
    far_den[...] = sums(q2_ref, everything, far_top.at[0])
    den3 = sums(q3_ref, everything, far_top.at[1])
    row = jnp.broadcast_to(far_top[0, pl.ds(last, 1), :], (EDGE_ROWS, width))
    fill(back3, far_top[1], den3, row, far_den[pl.ds(last, 1), :])
    edge_den = sums(kv_ref, slice(2 * rows, 2 * rows + EDGE_ROWS), far_top.at[1])
    fill(back2, far_top[0], far_den[...], far_top[1, :EDGE_ROWS, :], edge_den[:1])


def near_body(info_ref, kv_ref, kv_in_ref, mask_ref, _, q, top_ref, den_ref, edge_ref):
    q_ref = q()
    rows, width = q_ref.shape
    allowed = mask_ref[...] > 0
    linked = jnp.where(info_ref[3] % 2 == 1, 1.0, 0.0)
    lane = lax.broadcasted_iota(jnp.int32, (rows, LANES), 1)
    edge_lane = lax.broadcasted_iota(jnp.int32, (EDGE_ROWS, LANES), 1)
    dens = jnp.zeros((rows, LANES), F32)
    edge_dens = jnp.zeros((EDGE_ROWS, LANES), F32)
    keys, values = slice(0, rows), slice(rows, 2 * rows)
    for h, at in enumerate(heads_of(width)):
        k, v = kv_ref[keys, at], kv_ref[values, at]
        k_in, v_in = kv_in_ref[keys, at], kv_in_ref[values, at]
        q = q_ref[:, at]
        own = jnp.where(allowed, jnp.exp(dot(q, k, ((1,), (1,))) * ROOT), 0.0)
        own_den = jnp.sum(own, axis=-1, keepdims=True)
        other, other_den = weigh(q, k_in)
        top_ref[:, at] = dot(own.astype(BF16), v) + dot((other * linked).astype(BF16), v_in)
        dens = jnp.where(lane == h, own_den + other_den * linked, dens)
        edge, edge_den = weigh(kv_in_ref[2 * rows :, at], k_in)
        edge_ref[:, at] = dot((edge * linked).astype(BF16), v_in)
        edge_dens = jnp.where(edge_lane == h, edge_den * linked, edge_dens)
    den_ref[...] = dens
    edge_ref[:, width:] = edge_dens


def attend_paired(info, q, kv, kv_near, mask, tp_count):
    kv_in = lax.ppermute(kv, "ctx", [(0, 1), (2, 3)])
    far = [lax.ppermute(q, "ctx", [(c, 1)]) for c in (3, 2)]
    rows, width = q.shape
    back = ((rows + 2 * EDGE_ROWS, width), BF16)
    back3, back2, done = staged(
        functools.partial(far_body, tp_count),
        [kv_near, kv_in, *far],
        [back, back],
        [TOKEN],
        [pltpu.VMEM((2, rows, width), F32), pltpu.VMEM((rows, LANES), F32)],
        info,
    )
    back = [lax.ppermute(back2, "ctx", [(1, 2)]), lax.ppermute(back3, "ctx", [(1, 3)])]
    top, den, edge = staged(
        near_body,
        [kv_near, kv_in, mask, done],
        [],
        [((rows, width), F32), ((rows, LANES), F32), ((EDGE_ROWS, width + LANES), F32)],
        info=info,
        held=[q],
    )
    return top, den, edge, back


def attend_all_body(tp_count, info_ref, mask_ref, q_ref, k_ref, v_ref, top_ref, den_ref, edge_ref):
    rows, width = q_ref.shape
    allowed = mask_ref[...] > 0
    lane = lax.broadcasted_iota(jnp.int32, den_ref.shape, 1)
    dens = jnp.zeros(den_ref.shape, F32)
    heads = heads_of(width)
    for h, at in enumerate(heads):
        scores = dot(q_ref[:, at], k_ref[:, at], ((1,), (1,))) * (1.0 / math.sqrt(HEAD_DIM))
        expo = jnp.where(allowed, jnp.exp(scores), 0.0)
        top_ref[:, at] = dot(expo.astype(BF16), v_ref[:, at])
        dens = jnp.where(lane == h, jnp.sum(expo, axis=-1, keepdims=True), dens)
    den_ref[...] = dens
    last = last_row(info_ref, rows, tp_count)
    count = edge_ref.shape[0]
    top = jnp.broadcast_to(top_ref[pl.ds(last, 1), :], (count, width))
    den = jnp.broadcast_to(den_ref[pl.ds(last, 1), :], (count, LANES))
    edge_ref[:, :width] = top
    edge_ref[:, width:] = den


def attend_all(info, q, kv, mask, tp_count):
    planes = lax.axis_size("ctx")
    rows, width = q.shape
    keys = lax.all_gather(kv[:rows], "ctx", axis=0, tiled=True)
    values = lax.all_gather(kv[rows : 2 * rows], "ctx", axis=0, tiled=True)
    here = pl.BlockSpec(memory_space=pltpu.VMEM)
    outs = [((rows, width), F32), ((rows, LANES), F32), ((EDGE_ROWS, width + LANES), F32)]
    top, den, edge = pl.pallas_call(
        functools.partial(attend_all_body, tp_count),
        in_specs=[pl.BlockSpec(memory_space=pltpu.SMEM)] + [here] * 4,
        out_specs=[here] * 3,
        out_shape=[jax.ShapeDtypeStruct(shape, dtype) for shape, dtype in outs],
        compiler_params=params(48),
    )(info, mask, q, keys, values)
    edge = lax.ppermute(edge, "ctx", [(c, c + 1) for c in range(planes - 1)])
    return top, den, edge, []


def output_body(count, tp_count, info_ref, *refs):
    back_refs = refs[:count]
    top_ref, den_ref, edge_ref, w_ref, odd_out, even_ref, whole, odd_ref, out_sems = refs[count:]
    depth = w_ref.shape[0]
    blocks, _, step = odd_ref.shape
    rows = top_ref.shape[0]
    heads = heads_of(depth)
    edges = []

    back_dens = []
    for ref in back_refs:
        turned = ref[rows + EDGE_ROWS :, : den_lanes(rows)].astype(F32)
        rest = jnp.zeros((LANES - EDGE_ROWS, turned.shape[1]), F32)
        back_dens.append(jnp.concatenate([turned, rest], axis=0).T)

    for h, lanes in enumerate(heads):
        top, den = top_ref[:, lanes], den_ref[:, h : h + 1]
        edge, edge_den = edge_ref[:, lanes], edge_ref[:, depth + h : depth + h + 1]
        for ref in back_refs:
            top += ref[:rows, lanes].astype(F32)
            edge += ref[rows : rows + EDGE_ROWS, lanes].astype(F32)
        for value in back_dens:
            both = value[:, h : h + 1] + value[:, len(heads) + h : len(heads) + h + 1]
            den += both[:rows]
            edge_den += both[rows : rows + EDGE_ROWS]
        whole[:, lanes] = top / den
        edges.append(jnp.where(edge_den > 0, edge / jnp.where(edge_den > 0, edge_den, 1.0), 0.0))
    edge = jnp.concatenate(edges, axis=1)[:1]
    patches = rows // tp_count
    me = info_ref[1]
    before = []
    for bits in block_order(tp_count):
        peer = me ^ bits
        source = block_place(me ^ ((peer + tp_count - 1) % tp_count), tp_count)
        row = whole[pl.ds(source * patches + patches - 1, 1), :]
        before.append(jnp.where(peer == 0, edge, row))
    for index, row in enumerate(before):
        at = index * patches + patches - 1
        whole[at : at + 1, :] = row
    attended = whole[...].astype(BF16)
    half = rows // 2
    sends = []
    for n in range(blocks):
        at = pl.ds(n * step, step)
        out = dot(attended, w_ref[:, at])
        odd_ref[n] = out[half:].astype(BF16)
        sends.append(pltpu.make_async_copy(odd_ref.at[n], odd_out.at[:, at], out_sems.at[n]))
        sends[-1].start()
        even_ref[:, at] = out[:half].astype(BF16)
    for copy in sends:
        copy.wait()


def output_project(info, top, den, edge, back, weights, tp_count):
    rows, depth = top.shape
    width = weights.shape[1]
    step = min(width, 1024)
    here, there = pl.BlockSpec(memory_space=pltpu.VMEM), pl.BlockSpec(memory_space=pltpu.HBM)
    blocks = width // step
    odd, even = pl.pallas_call(
        functools.partial(output_body, len(back), tp_count),
        in_specs=[pl.BlockSpec(memory_space=pltpu.SMEM)] + [here] * (4 + len(back)),
        out_specs=[there, here],
        out_shape=[
            pltpu.HBM((rows // 2, width), BF16),
            jax.ShapeDtypeStruct((rows // 2, width), BF16),
        ],
        scratch_shapes=[
            pltpu.VMEM((rows, depth), F32),
            pltpu.VMEM((blocks, rows // 2, step), BF16),
            pltpu.SemaphoreType.DMA((blocks,)),
        ],
        compiler_params=params(16),
    )(info, *back, top, den, edge, weights)
    return even, odd


def pair_sum_body(mine_ref, other_ref, own_ref, *send_refs):
    patches = own_ref.shape[0]
    total = mine_ref[...].astype(F32) + other_ref[...].astype(F32)
    own_ref[...] = total[:patches]
    for index, ref in enumerate(send_refs):
        ref[...] = total[(index + 1) * patches : (index + 2) * patches].astype(BF16)


def scatter_sum(even, odd, patches):
    blocks = even.shape[0] // patches
    block = (patches, even.shape[1])
    pieces = call(pair_sum_body, [(block, F32)] + [(block, BF16)] * (blocks - 1))(
        even, swap(odd, 1)
    )
    return [pieces[0]] + [swap(pieces[k], 2 * k) for k in range(blocks - 1, 0, -1)]


def state_body(count, *refs):
    terms = refs[:count]
    local_ref, normed, state_out, normed_ref, wide = refs[count:]
    patches = terms[0].shape[0]
    width = normed_ref.shape[1]
    chunks = width // LANES
    for b in range(PATCH):
        at = slice(b * width, (b + 1) * width)
        total = terms[0][:, at]
        for term in terms[1:]:
            total += term[:, at].astype(F32)
        part = pltpu.roll(total.astype(BF16).astype(F32), 1, 0)
        for c in range(chunks):
            wide[c, pl.ds(b, patches, stride=PATCH), :] = part[:, c * LANES : (c + 1) * LANES]
    context = jnp.concatenate([wide[c] for c in range(chunks)], axis=1)
    state = local_ref[...].astype(F32) + context
    state_out.ref[...] = state
    state_out.send()
    mean = jnp.mean(state * state, axis=-1, keepdims=True)
    normed_ref[...] = (state * lax.rsqrt(mean + EPS)).astype(BF16)
    normed.ref[...] = normed_ref[...]


def byte_state(terms, local_embeds, after):
    rows, width = local_embeds.shape
    normed, state, normed_near = staged(
        functools.partial(state_body, len(terms)),
        [*terms, local_embeds],
        [((rows, width), BF16), ((rows, width), F32)],
        [((rows, width), BF16)],
        [pltpu.VMEM((width // LANES, rows, LANES), F32)],
        after=after,
    )
    return state, normed, normed_near


def unit(x):
    scale = lax.rsqrt(jnp.mean(x * x, axis=-1, keepdims=True) + EPS)
    return x * scale, scale


def unit_back(grad, y, scale):
    return scale * (grad - y * jnp.mean(grad * y, axis=-1, keepdims=True))


def prepare_body(parts, info_ref, gb_ref, wq_ref, wk_ref, wv_ref, wo_ref, token_ref, *refs):
    token_ref[...] = jnp.zeros_like(token_ref)
    weights_ref = refs[0]
    d = LOCAL_HEAD_DIM
    rows = refs[1].shape[0] // len(parts[0])
    for kind, ref in enumerate((wq_ref, wk_ref, wv_ref)):
        weights_ref[:, kind * d : (kind + 1) * d] = ref[0]
    for index, part in enumerate(parts):
        out_ref, core_ref = refs[1 + 2 * index : 3 + 2 * index]
        for place, bits in enumerate(part):
            at = pl.multiple_of((info_ref[1] ^ bits) * rows, rows)
            out_ref[place * rows : (place + 1) * rows, :] = gb_ref[pl.ds(at, rows), :]
        core_ref[...] = dot(out_ref[...], wo_ref[0], ((1,), (1,))).astype(BF16)


def prepare(info, gb_all, local_qkv, local_out, rows, parts):
    width = gb_all.shape[1]
    d = LOCAL_HEAD_DIM
    heads = LOCAL_HEADS

    def qkv_spec(kind):
        return pl.BlockSpec((1, width, d), lambda i, info: (0, 0, kind * heads + info[0]))

    outs = [(width, 3 * d)]
    for part in parts:
        outs += [(len(part) * rows, width), (len(part) * rows, d)]
    token, weights, *blocks = pl.pallas_call(
        functools.partial(prepare_body, parts),
        grid_spec=pltpu.PrefetchScalarGridSpec(
            num_scalar_prefetch=1,
            grid=(1,),
            in_specs=[
                pl.BlockSpec(gb_all.shape, lambda i, info: (0, 0)),
                qkv_spec(0),
                qkv_spec(1),
                qkv_spec(2),
                pl.BlockSpec((1, d, width), lambda i, info: (0, info[0], 0)),
            ],
            out_specs=[pl.BlockSpec(shape, lambda i, info: (0, 0)) for shape in [TOKEN.shape, *outs]],
        ),
        out_shape=[TOKEN] + [jax.ShapeDtypeStruct(shape, BF16) for shape in outs],
        compiler_params=params(LARGE),
    )(info, gb_all, local_qkv, local_qkv, local_qkv, local_out)
    return token, weights, blocks[0::2], blocks[1::2]


def window(rows):
    row = lax.broadcasted_iota(jnp.int32, (rows, rows), 0)
    column = lax.broadcasted_iota(jnp.int32, (rows, rows), 1)
    return (row // PATCH == column // PATCH) & (column <= row)


def core_weights(qkv, allowed):
    d = LOCAL_HEAD_DIM
    q, q_scale = unit(qkv[:, :d])
    k, k_scale = unit(qkv[:, d : 2 * d])
    qb, kb, vb = q.astype(BF16), k.astype(BF16), qkv[:, 2 * d :].astype(BF16)
    expo = jnp.where(allowed, jnp.exp(dot(qb, kb, ((1,), (1,))) * (1.0 / math.sqrt(d))), 0.0)
    weight = expo / jnp.sum(expo, axis=-1, keepdims=True)
    return (q, q_scale, qb), (k, k_scale, kb), vb, weight


def core_forward(weight, vb):
    return dot(weight.astype(BF16), vb).astype(BF16)


def core_backward(query, key, vb, weight, gradb):
    q, q_scale, qb = query
    k, k_scale, kb = key
    grad_v = dot(weight.astype(BF16), gradb, ((0,), (0,)))
    grad_w = dot(gradb, vb, ((1,), (1,)))
    mean = jnp.sum(weight * grad_w, axis=-1, keepdims=True)
    grad_s = (weight * (grad_w - mean) * (1.0 / math.sqrt(LOCAL_HEAD_DIM))).astype(BF16)
    grad_q = unit_back(dot(grad_s, kb), q, q_scale)
    grad_k = unit_back(dot(grad_s, qb, ((0,), (0,))), k, k_scale)
    return jnp.concatenate([grad_q, grad_k, grad_v], axis=1).astype(BF16)


def chunks_in(piece):
    return jnp.concatenate(
        [piece[:, at : at + LANES] for at in range(0, piece.shape[1], LANES)], axis=0
    )


def chunks_out(value, rows):
    return jnp.concatenate(
        [value[at : at + rows] for at in range(0, value.shape[0], rows)], axis=1
    )


def rows_of(refs):
    return jnp.concatenate([ref[...] for ref in refs], axis=0)


def local_body(count, *refs):
    x_refs, refs = refs[:count], refs[count:]
    (gb_ref, core_ref, w_ref), refs = refs[:3], refs[3:]
    carry, (gqkv_ref, gout_ref, ab_ref, token_ref) = refs[:-4], refs[-4:]
    token_ref[...] = jnp.zeros_like(token_ref)
    gqkv, gout, abs_ = local_grads(x_refs, gb_ref, core_ref, w_ref, carry)
    gqkv_ref[...] = gqkv
    gout_ref[...] = gout
    ab_ref[...] = jnp.concatenate(abs_, axis=0)


def local_grads(x_refs, gb_ref, core_ref, w_ref, carry):
    x = rows_of(x_refs)
    rows = x_refs[0].shape[0]
    tile = rows // 2 if rows % (2 * BF16_ROWS) == 0 else rows
    allowed = window(tile)
    qkv = dot(x, w_ref[...])
    abs_, gqs = [], []
    for start in range(0, x.shape[0], tile):
        at = slice(start, start + tile)
        query, key, vb, weight = core_weights(qkv[at], allowed)
        abs_.append(core_forward(weight, vb))
        gqs.append(core_backward(query, key, vb, weight, core_ref[at, :]))
    gqkv = dot(jnp.concatenate(gqs, axis=0), x, ((0,), (0,)))
    gout = dot(jnp.concatenate(abs_, axis=0), gb_ref[...], ((0,), (0,)))
    if carry:
        gqkv += carry[0][...]
        gout += carry[1][...]
    return gqkv, gout, abs_


def local_last_body(count, rounds, info_ref, *refs):
    x_refs, refs = refs[:count], refs[count:]
    gb_ref, core_ref, w_ref, *refs = refs
    *carry, ab0_ref = refs[:3]
    gqkv_out, message, *pieces = refs[3 : 4 + rounds]
    own_ref, held = refs[4 + rounds :]
    gqkv, gout, abs_ = local_grads(x_refs, gb_ref, core_ref, w_ref, carry)
    held[...] = gout
    deep = own_ref.shape[0]
    piece_rows = deep * LANES // held.shape[1]
    for k in range(rounds):
        at = pl.multiple_of((info_ref[2] ^ k) * piece_rows, piece_rows)
        piece = chunks_in(held[pl.ds(at, piece_rows), :]).astype(BF16)
        if k:
            pieces[k - 1].ref[...] = piece
            pieces[k - 1].send()
        else:
            own_ref[...] = piece
    gqkv_out.ref[...] = gqkv.T.astype(BF16)
    gqkv_out.send()
    rows = x_refs[0].shape[0]
    message.ref[:rows, :] = ab0_ref[rows:, :]
    message.ref[rows:, :] = jnp.concatenate(abs_, axis=0)


def relay_body(*refs):
    ab0_ref, ab1_ref, there_ref, *messages, own_ref = refs
    rows = ab0_ref.shape[0] // 2
    for k, message in enumerate(messages):
        message.ref[:rows, :] = ab1_ref[k * rows : (k + 1) * rows, :]
        message.ref[rows:, :] = there_ref[(k + 1) * rows : (k + 2) * rows, :]
        message.send()
    own_ref[:rows, :] = ab0_ref[:rows, :]
    own_ref[rows:, :] = there_ref[:rows, :]


def planes_body(rounds, planes, info_ref, *refs):
    pieces, outs, held = refs[:rounds], refs[rounds:-1], refs[-1]
    for k, piece in enumerate(pieces):
        held[k] = piece[...].astype(F32)
    for z, out in enumerate(outs):
        total = None
        for outer in range(rounds // planes):
            term = held[info_ref[2] ^ ((info_ref[3] ^ z) + outer * planes)]
            total = term if total is None else total + term
        out.ref[...] = total.astype(BF16)
        out.send()


def local_layer(normed, normed_near, info, parts, gbs, cores, weights, rounds, planes):
    rows, width = normed.shape
    d = LOCAL_HEAD_DIM
    near = [swap(normed, bits) for bits in parts[1]]
    count = len(near)
    totals = [((3 * d, width), F32), ((d, width), F32)]

    def step(index, xs, carry):
        return staged(
            functools.partial(local_body, len(xs)),
            [*xs, gbs[index], cores[index], weights, *carry],
            [],
            [*totals, ((len(xs) * rows, d), BF16), TOKEN],
            flops=1 << 34,
            mib=20,
        )

    *carry, ab0, done = step(0, [normed_near, swap(normed, 1)], [])
    near = [tie(block, done) for block in near]
    far = [swap(block, 1) for block in near]
    *carry, ab1, _ = step(1, near, carry)
    deep = d // rounds * width // LANES
    piece = ((deep, d), BF16)
    grad_qkv, message, *pieces, own = staged(
        functools.partial(local_last_body, count, rounds),
        [*far, gbs[2], cores[2], weights, *carry, ab0],
        [((width, 3 * d), BF16), (((count + 1) * rows, d), BF16)] + [piece] * (rounds - 1),
        [piece],
        [pltpu.VMEM((d, width), F32)],
        info,
        flops=1 << 34,
        mib=20,
    )
    pieces = [own] + [swap(value, k + 1) for k, value in enumerate(pieces)]
    block = ((2 * rows, d), BF16)
    *sent, own = staged(
        relay_body, [ab0, ab1, swap(message, 1)], [block] * count, [block]
    )
    messages = [own] + [swap(value, 2 * (k + 1)) for k, value in enumerate(sent)]
    pieces = staged(
        functools.partial(planes_body, rounds, planes),
        pieces,
        [piece] * planes,
        scratch=[pltpu.VMEM((rounds, deep, d), F32)],
        info=info,
    )
    return messages, pieces, grad_qkv


def hidden_body(heads, info_ref, state_ref, w_ref, *refs):
    *messages, out_ref, token_ref = refs
    token_ref[...] = jnp.zeros_like(token_ref)
    rows = state_ref.shape[0]
    d = LOCAL_HEAD_DIM
    total = state_ref[...]
    for bits in range(2 * len(messages)):
        at = bits % 2 * rows
        head = heads(info_ref[1] ^ bits)
        weights = w_ref[0, pl.ds(pl.multiple_of(head * d, d), d), :]
        total += dot(messages[bits // 2][at : at + rows, :], weights)
    out_ref[...] = total.astype(BF16)


def final_body(heads, parts_ref, _, *refs):
    *terms, gqkv_ref, gout_ref = refs
    gout = sum(term[...].astype(F32) for term in terms)
    gout_ref[0] = chunks_out(gout, gout_ref.shape[1])
    d = LOCAL_HEAD_DIM
    tp_count = len(heads)
    for h in range(LOCAL_HEADS):
        total = None
        for source in range(parts_ref.shape[0]):
            if heads[source % tp_count] == h:
                term = parts_ref[source].astype(F32)
                total = term if total is None else total + term
        for kind in range(3):
            at = (kind * LOCAL_HEADS + h) * d
            gqkv_ref[0, :, at : at + d] = total[:, kind * d : (kind + 1) * d]


def swap_planes(pieces):
    count = len(pieces)
    return [pieces[0]] + [
        lax.ppermute(pieces[k], "ctx", [(c, c ^ k) for c in range(count)]) for k in range(1, count)
    ]


def per_device(byte_embeds, local_embeds, global_qkv, global_out, local_qkv, local_out, cotangent):
    byte_count, width = byte_embeds.shape
    patches = byte_count // PATCH
    planes, tp_count = lax.axis_size("ctx"), lax.axis_size("tp")
    plane, me = lax.axis_index("ctx"), lax.axis_index("tp")
    order = block_order(tp_count)
    shard_rows = tp_count * patches
    devices = planes * tp_count

    group = min(tp_count, LOCAL_HEADS)
    share = width // devices
    rounds = LOCAL_HEAD_DIM // share
    plane_heads = LOCAL_HEADS // planes

    def head_of(t):
        return (t % rounds) % planes * plane_heads + t // rounds

    heads = [head_of(t) for t in range(tp_count)]
    head_info = jnp.stack([head_of(me), me, me % rounds, plane]).astype(jnp.int32)

    patch_in = patch_norm(byte_embeds)
    mine = swap(patch_in, 1)
    weights_in, head_info = preload(global_qkv, head_info, mine)
    even = [tie(swap(patch_in, bits), head_info) for bits in range(2, tp_count, 2)]
    pieces = [patch_in, *even, mine, *(swap(piece, 1) for piece in even)]
    q, kv, gb, kv_near = project(head_info, pieces, weights_in, global_qkv, cotangent, tp_count)

    place = (
        (me ^ jnp.array(order, jnp.int32))[:, None] * patches
        + jnp.arange(patches, dtype=jnp.int32)[None, :]
    ).reshape(-1)
    if planes == 4 and den_lanes(shard_rows) <= q.shape[1]:
        mask = (place[None, :] <= place[:, None]).astype(F32)
        top, den, edge, back = attend_paired(
            head_info, q, kv, kv_near, mask, tp_count
        )
    else:
        key_place = (
            jnp.arange(planes, dtype=jnp.int32)[:, None] * shard_rows + place[None, :]
        ).reshape(-1)
        mask = (key_place[None, :] <= (plane * shard_rows + place)[:, None]).astype(F32)
        top, den, edge, back = attend_all(head_info, q, kv, mask, tp_count)

    weights_out, _ = preload(global_out, head_info, den)
    even, odd = output_project(head_info, top, den, edge, back, weights_out, tp_count)

    parts = [[0, 1], list(range(2, group, 2)), list(range(3, group, 2))]
    gb_all = lax.all_gather(gb, "tp", axis=0, tiled=True)
    prepared, weights, gbs, cores = prepare(head_info, gb_all, local_qkv, local_out, byte_count, parts)
    state, normed, normed_near = byte_state(
        scatter_sum(even, odd, patches), local_embeds, prepared
    )
    messages, out_pieces, grad_qkv = local_layer(
        normed, normed_near, head_info, parts, gbs, cores, weights, rounds, planes
    )
    grad_qkv = lax.all_to_all(grad_qkv, ("ctx", "tp"), 0, 0, tiled=True)
    out_pieces = swap_planes(out_pieces)
    here = pl.BlockSpec(memory_space=pltpu.VMEM)
    hidden, done = pl.pallas_call(
        functools.partial(hidden_body, head_of),
        in_specs=[pl.BlockSpec(memory_space=pltpu.SMEM)] + [here] * (2 + len(messages)),
        out_specs=[here, here],
        out_shape=[jax.ShapeDtypeStruct((byte_count, width), BF16), TOKEN],
        compiler_params=params(16),
    )(head_info, state, local_out, *messages)
    grad_qkv, grad_out = call(
        functools.partial(final_body, heads),
        [((1, share, 3 * width), F32), ((1, share, width), F32)],
        mib=16,
    )(grad_qkv.reshape(devices, share, 3 * LOCAL_HEAD_DIM), done, *out_pieces)
    return (hidden, grad_qkv, grad_out)


def solution(mesh):
    in_specs = (
        P(("ctx", "tp"), None),
        P(("ctx", "tp"), None),
        P(None, None, "tp"),
        P("tp", None),
        P(),
        P(),
        P(("ctx", "tp"), None),
    )
    out_specs = (P(("ctx", "tp"), None), P(None, ("ctx", "tp"), None), P(None, ("ctx", "tp"), None))
    return jax.shard_map(
        per_device, mesh=mesh, in_specs=in_specs, out_specs=out_specs, check_vma=False
    )
```

```python
import functools
import math

import jax
import jax.numpy as jnp
from jax import lax
from jax.experimental import pallas as pl
from jax.experimental.pallas import tpu as pltpu
from jax.sharding import PartitionSpec as P

PATCH = 8
HEAD_DIM = 128
LOCAL_HEADS = 8
LOCAL_HEAD_DIM = 128
EPS = 1e-06
F32 = jnp.float32
BF16 = jnp.bfloat16
MIB = 1 << 20
LARGE = 60
TOKEN = pltpu.VMEM((8, 128), jnp.float32)
LANES = 128
EDGE_ROWS = 16
DEN_ROWS = 8
BF16_ROWS = 16


def params(mib):
    return pltpu.CompilerParams(vmem_limit_bytes=mib * MIB)


def call(body, outs, scratch=(), mib=32):
    return pl.pallas_call(
        body,
        out_shape=[out if out is TOKEN else jax.ShapeDtypeStruct(*out) for out in outs],
        scratch_shapes=list(scratch),
        compiler_params=params(mib),
    )


class Held:
    def __init__(self, source, target, sem):
        self.ref, self.copy, self.waited = target, pltpu.make_async_copy(source, target, sem), False
        self.copy.start()

    def __call__(self):
        if not self.waited:
            self.copy.wait()
            self.waited = True
        return self.ref


class Sent:
    def __init__(self, source, target, sem):
        self.ref, self.copy, self.started = source, pltpu.make_async_copy(source, target, sem), False

    def send(self):
        self.copy.start()
        self.started = True


def staged(body, args, sent, outs=(), scratch=(), info=None, mib=16, flops=0, after=None, held=()):
    tokens = [] if after is None else [after]
    counts = [len(args), len(held), len(tokens), len(sent), len(outs)]
    counts += [len(held), len(sent), len(scratch)]

    def kernel(*refs):
        refs = list(refs)
        info_ref = [refs.pop(0)] if info is not None else []
        groups = []
        for count in counts:
            groups.append(refs[:count])
            del refs[:count]
        in_refs, held_far, _, sent_far, out_refs, held_near, sent_near, own = groups
        in_sems, out_sems = refs
        inputs = [Held(f, n, in_sems.at[i]) for i, (f, n) in enumerate(zip(held_far, held_near))]
        outputs = [Sent(n, f, out_sems.at[i]) for i, (f, n) in enumerate(zip(sent_far, sent_near))]
        body(*info_ref, *in_refs, *inputs, *outputs, *out_refs, *own)
        for output in outputs:
            if not output.started:
                output.send()
        for value in inputs:
            value()
        for output in outputs:
            output.copy.wait()

    here, there = pl.BlockSpec(memory_space=pltpu.VMEM), pl.BlockSpec(memory_space=pltpu.HBM)
    free = pl.BlockSpec(memory_space=pl.ANY)
    scalars = [] if info is None else [info]
    return pl.pallas_call(
        kernel,
        in_specs=[pl.BlockSpec(memory_space=pltpu.SMEM)] * len(scalars)
        + [here] * len(args)
        + [free] * (len(held) + len(tokens)),
        out_specs=[there] * len(sent) + [here] * len(outs),
        out_shape=[pltpu.HBM(shape, dtype) for shape, dtype in sent]
        + [out if out is TOKEN else jax.ShapeDtypeStruct(*out) for out in outs],
        scratch_shapes=[pltpu.VMEM(value.shape, value.dtype) for value in held]
        + [pltpu.VMEM(shape, dtype) for shape, dtype in sent]
        + list(scratch)
        + [pltpu.SemaphoreType.DMA((max(1, count),)) for count in (len(held), len(sent))],
        compiler_params=params(mib),
        cost_estimate=pl.CostEstimate(flops=flops, bytes_accessed=1 << 22, transcendentals=0),
    )(*scalars, *args, *held, *tokens)


def dot(a, b, dims=((1,), (0,))):
    return lax.dot_general(a, b, (dims, ((), ())), preferred_element_type=F32)


def swap(value, bits):
    count = lax.axis_size("tp")
    return lax.ppermute(value, "tp", [(source, source ^ bits) for source in range(count)])


def block_order(size):
    return list(range(0, size, 2)) + list(range(1, size, 2))


def gather(value, size):
    even = [value] + [swap(value, bits) for bits in range(2, size, 2)]
    return even + [swap(piece, 1) for piece in even]


def tie_body(*refs):
    pass


def tie(value, *after, mib=1):
    there = pl.BlockSpec(memory_space=pl.ANY)
    return pl.pallas_call(
        tie_body,
        in_specs=[there] * (1 + len(after)),
        out_specs=there,
        out_shape=jax.ShapeDtypeStruct(value.shape, value.dtype),
        input_output_aliases={0: 0},
        compiler_params=params(mib),
    )(value, *after)


def preload_body(parts, info_ref, w_ref, _, out_ref, info_out, sems):
    for index in range(info_ref.shape[0]):
        info_out[index] = info_ref[index]
    source = w_ref.at[0] if len(w_ref.shape) == 3 else w_ref
    size = source.shape[0] // parts
    copies = []
    for part in range(parts):
        at = pl.ds(part * size, size)
        copies.append(pltpu.make_async_copy(source.at[at], out_ref.at[at], sems.at[part]))
        copies[-1].start()
    for copy in copies:
        copy.wait()


def preload(weights, info, after, parts=8):
    there = pl.BlockSpec(memory_space=pl.ANY)
    scalar = pl.BlockSpec(memory_space=pltpu.SMEM)
    shape = weights.shape[-2:]
    return pl.pallas_call(
        functools.partial(preload_body, parts),
        in_specs=[scalar, there, there],
        out_specs=[pl.BlockSpec(memory_space=pltpu.VMEM), scalar],
        out_shape=[
            pltpu.VMEM(shape, weights.dtype),
            jax.ShapeDtypeStruct(info.shape, info.dtype),
        ],
        scratch_shapes=[pltpu.SemaphoreType.DMA((parts,))],
        compiler_params=params(50),
        cost_estimate=pl.CostEstimate(
            flops=0, bytes_accessed=2 * math.prod(shape), transcendentals=0
        ),
    )(info, weights, after)


def patch_norm_body(x_ref, out_ref, wide):
    patches = out_ref.shape[0]
    width = x_ref.shape[1]
    total = jnp.zeros((patches, LANES), F32)
    for c in range(width // LANES):
        wide[c] = x_ref[:, c * LANES : (c + 1) * LANES].astype(F32)
    for c in range(width // LANES):
        for b in range(PATCH):
            part = wide[c, pl.ds(b, patches, stride=PATCH), :]
            total += part * part
    scale = lax.rsqrt(jnp.sum(total, axis=-1, keepdims=True) / (PATCH * width) + EPS)
    for b in range(PATCH):
        for c in range(width // LANES):
            part = wide[c, pl.ds(b, patches, stride=PATCH), :]
            at = b * width + c * LANES
            out_ref[:, at : at + LANES] = (part * scale).astype(BF16)


def patch_norm(byte_embeds):
    rows, width = byte_embeds.shape
    return call(
        patch_norm_body,
        [((rows // PATCH, PATCH * width), BF16)],
        [pltpu.VMEM((width // LANES, rows, LANES), F32)],
        16,
    )(byte_embeds)[0]


def stack(refs):
    return jnp.concatenate([ref[...].astype(F32) for ref in refs], axis=0).astype(BF16)


def project_body(count, tp_count, info_ref, *refs):
    x_refs, refs = refs[:count], refs[count:]
    first_ref, pass_ref, w_ref, q, kv, passed, kv_ref, held, wide, sems = refs
    kinds, rows, _ = held.shape
    depth = math.gcd(rows, 1024)
    copies = {}
    for c in range(kinds):
        for k in range(0, rows, depth):
            at = pl.ds(k, depth)
            copies[c, k] = pltpu.make_async_copy(
                w_ref.at[c + 1, at], held.at[c, at], sems.at[len(copies)]
            )
            copies[c, k].start()
    x = stack(x_refs)
    count_rows = x.shape[0]
    passed.ref[...] = pass_ref[...]
    passed.send()
    for c in range(kinds + 1):
        total = None
        for k in range(0, rows, depth):
            if c:
                copies[c - 1, k].wait()
                w = held[c - 1, k : k + depth, :]
            else:
                w = first_ref[k : k + depth, :]
            term = dot(x[:, k : k + depth], w)
            total = term if total is None else total + term
        for h in range(total.shape[1] // HEAD_DIM):
            at = slice(h * HEAD_DIM, (h + 1) * HEAD_DIM)
            part = total[:, at]
            if c < 2:
                part = part * lax.rsqrt(jnp.mean(part * part, axis=-1, keepdims=True) + EPS)
            if c == 0:
                wide[:, at] = part
            else:
                kv_ref[(c - 1) * count_rows : c * count_rows, at] = part.astype(BF16)
        if c == 0:
            q.ref[...] = wide[...].astype(BF16)
            q.send()
            last = wide[pl.ds(last_row(info_ref, count_rows, tp_count), 1), :]
            spread = jnp.broadcast_to(last, (EDGE_ROWS, last.shape[1]))
            kv_ref[kinds * count_rows :, :] = spread.astype(BF16)


def project(info, pieces, first, weights, passed, tp_count):
    rows = sum(piece.shape[0] for piece in pieces)
    kinds, deep, width = weights.shape
    here, there = pl.BlockSpec(memory_space=pltpu.VMEM), pl.BlockSpec(memory_space=pltpu.HBM)
    outs = [((rows, width), BF16), (((kinds - 1) * rows + EDGE_ROWS, width), BF16)]
    outs.append((passed.shape, passed.dtype))
    count = len(pieces)

    def body(*refs):
        in_refs, refs = refs[: count + 4], refs[count + 4 :]
        far, kv_near, near, (held, wide, sems, out_sems) = refs[:3], refs[3], refs[4:7], refs[7:]
        outputs = [Sent(n, f, out_sems.at[i]) for i, (f, n) in enumerate(zip(far, near))]
        project_body(count, tp_count, *in_refs, *outputs, kv_near, held, wide, sems)
        near[1][...] = kv_near[...]
        outputs[1].send()
        for output in outputs:
            output.copy.wait()

    return pl.pallas_call(
        body,
        in_specs=[pl.BlockSpec(memory_space=pltpu.SMEM)]
        + [here] * (count + 2)
        + [pl.BlockSpec(memory_space=pl.ANY)],
        out_specs=[there] * 3 + [here],
        out_shape=[pltpu.HBM(shape, dtype) for shape, dtype in outs]
        + [jax.ShapeDtypeStruct(*outs[1])],
        scratch_shapes=[pltpu.VMEM(shape, dtype) for shape, dtype in outs]
        + [
            pltpu.VMEM((kinds - 1, deep, width), BF16),
            pltpu.VMEM((rows, width), F32),
            pltpu.SemaphoreType.DMA(((kinds - 1) * deep // math.gcd(deep, 1024),)),
            pltpu.SemaphoreType.DMA((3,)),
        ],
        compiler_params=params(40),
    )(info, *pieces, first, passed, weights)


def heads_of(ref_width):
    return [slice(at, at + HEAD_DIM) for at in range(0, ref_width, HEAD_DIM)]


def last_row(info_ref, rows, tp_count):
    return block_place(info_ref[1] ^ (tp_count - 1), tp_count) * (rows // tp_count) + (
        rows // tp_count - 1
    )


def block_place(bits, size):
    return bits // 2 + (bits % 2) * (size // 2)


def split_den(dens, count):
    high = dens.astype(BF16).astype(F32)
    return high + pltpu.roll(dens - high, count, 1)


ROOT = 1.0 / math.sqrt(HEAD_DIM)


def weigh(q, k):
    expo = jnp.exp(dot(q, k, ((1,), (1,))) * ROOT)
    return expo, jnp.sum(expo, axis=-1, keepdims=True)


def den_lanes(rows):
    return -(-(rows + 1) // LANES) * LANES


def far_body(tp_count, info_ref, kv_ref, kv_in_ref, q3_ref, q2_ref, *refs):
    back3, back2, token_ref, far_top, far_den = refs
    token_ref[...] = jnp.zeros_like(token_ref)
    rows, width = q2_ref.shape
    heads = heads_of(width)
    count = len(heads)
    keys, values = slice(0, rows), slice(rows, 2 * rows)
    queries = jnp.concatenate([q3_ref[...], q2_ref[...], kv_ref[2 * rows :, :]], axis=0)
    lane = lax.broadcasted_iota(jnp.int32, far_den.shape, 1)
    dens = jnp.zeros(far_den.shape, F32)
    for h, at in enumerate(heads):
        k = jnp.concatenate([kv_ref[keys, at], kv_in_ref[keys, at]], axis=0)
        v = jnp.concatenate([kv_ref[values, at], kv_in_ref[values, at]], axis=0)
        expo, den = weigh(queries[:, at], k)
        far_top[:, at] = dot(expo.astype(BF16), v)
        dens = jnp.where(lane == h, den, dens)
    far_den[...] = dens

    def fill(back, start, edge_row):
        back.ref[:rows, :] = far_top[start : start + rows, :].astype(BF16)
        edge_den = jnp.broadcast_to(far_den[pl.ds(edge_row, 1), :], (den_lanes(rows) - rows, LANES))
        den = jnp.concatenate([far_den[start : start + rows, :], edge_den], axis=0)
        turned = split_den(den, count).T[:DEN_ROWS]
        rest = jnp.zeros((DEN_ROWS, width - turned.shape[1]), F32)
        edge = jnp.broadcast_to(far_top[pl.ds(edge_row, 1), :], (EDGE_ROWS - DEN_ROWS, width))
        tail = jnp.concatenate([jnp.concatenate([turned, rest], axis=1), edge], axis=0)
        back.ref[rows:, :] = tail.astype(BF16)
        back.send()

    fill(back2, rows, 2 * rows)
    fill(back3, 0, rows + last_row(info_ref, rows, tp_count))


def near_body(info_ref, kv_ref, kv_in_ref, mask_ref, _, q, top_ref, den_ref, edge_ref):
    q_ref = q()
    rows, width = q_ref.shape
    allowed = mask_ref[...] > 0
    linked = jnp.where(info_ref[3] % 2 == 1, 1.0, 0.0)
    lane = lax.broadcasted_iota(jnp.int32, (rows, LANES), 1)
    edge_lane = lax.broadcasted_iota(jnp.int32, (EDGE_ROWS, LANES), 1)
    dens = jnp.zeros((rows, LANES), F32)
    edge_dens = jnp.zeros((EDGE_ROWS, LANES), F32)
    keys, values = slice(0, rows), slice(rows, 2 * rows)
    for h, at in enumerate(heads_of(width)):
        k, v = kv_ref[keys, at], kv_ref[values, at]
        k_in, v_in = kv_in_ref[keys, at], kv_in_ref[values, at]
        q = q_ref[:, at]
        own = jnp.where(allowed, jnp.exp(dot(q, k, ((1,), (1,))) * ROOT), 0.0)
        own_den = jnp.sum(own, axis=-1, keepdims=True)
        other, other_den = weigh(q, k_in)
        top_ref[:, at] = dot(own.astype(BF16), v) + dot((other * linked).astype(BF16), v_in)
        dens = jnp.where(lane == h, own_den + other_den * linked, dens)
        edge, edge_den = weigh(kv_in_ref[2 * rows :, at], k_in)
        edge_ref[:, at] = dot((edge * linked).astype(BF16), v_in)
        edge_dens = jnp.where(edge_lane == h, edge_den * linked, edge_dens)
    den_ref[...] = dens
    edge_ref[:, width:] = edge_dens


def attend_paired(info, q, kv, kv_near, mask, tp_count):
    kv_in = lax.ppermute(kv, "ctx", [(0, 1), (2, 3)])
    far = [lax.ppermute(q, "ctx", [(c, 1)]) for c in (3, 2)]
    rows, width = q.shape
    back = ((rows + EDGE_ROWS, width), BF16)
    total = 2 * rows + EDGE_ROWS
    back3, back2, done = staged(
        functools.partial(far_body, tp_count),
        [kv_near, kv_in, *far],
        [back, back],
        [TOKEN],
        [pltpu.VMEM((total, width), F32), pltpu.VMEM((total, LANES), F32)],
        info,
    )
    back = [lax.ppermute(back2, "ctx", [(1, 2)]), lax.ppermute(back3, "ctx", [(1, 3)])]
    top, den, edge = staged(
        near_body,
        [kv_near, kv_in, mask, done],
        [],
        [((rows, width), F32), ((rows, LANES), F32), ((EDGE_ROWS, width + LANES), F32)],
        info=info,
        held=[q],
    )
    return top, den, edge, back


def attend_all_body(tp_count, info_ref, mask_ref, q_ref, k_ref, v_ref, top_ref, den_ref, edge_ref):
    rows, width = q_ref.shape
    allowed = mask_ref[...] > 0
    lane = lax.broadcasted_iota(jnp.int32, den_ref.shape, 1)
    dens = jnp.zeros(den_ref.shape, F32)
    heads = heads_of(width)
    for h, at in enumerate(heads):
        scores = dot(q_ref[:, at], k_ref[:, at], ((1,), (1,))) * (1.0 / math.sqrt(HEAD_DIM))
        expo = jnp.where(allowed, jnp.exp(scores), 0.0)
        top_ref[:, at] = dot(expo.astype(BF16), v_ref[:, at])
        dens = jnp.where(lane == h, jnp.sum(expo, axis=-1, keepdims=True), dens)
    den_ref[...] = dens
    last = last_row(info_ref, rows, tp_count)
    count = edge_ref.shape[0]
    top = jnp.broadcast_to(top_ref[pl.ds(last, 1), :], (count, width))
    den = jnp.broadcast_to(den_ref[pl.ds(last, 1), :], (count, LANES))
    edge_ref[:, :width] = top
    edge_ref[:, width:] = den


def attend_all(info, q, kv, mask, tp_count):
    planes = lax.axis_size("ctx")
    rows, width = q.shape
    keys = lax.all_gather(kv[:rows], "ctx", axis=0, tiled=True)
    values = lax.all_gather(kv[rows : 2 * rows], "ctx", axis=0, tiled=True)
    here = pl.BlockSpec(memory_space=pltpu.VMEM)
    outs = [((rows, width), F32), ((rows, LANES), F32), ((EDGE_ROWS, width + LANES), F32)]
    top, den, edge = pl.pallas_call(
        functools.partial(attend_all_body, tp_count),
        in_specs=[pl.BlockSpec(memory_space=pltpu.SMEM)] + [here] * 4,
        out_specs=[here] * 3,
        out_shape=[jax.ShapeDtypeStruct(shape, dtype) for shape, dtype in outs],
        compiler_params=params(48),
    )(info, mask, q, keys, values)
    edge = lax.ppermute(edge, "ctx", [(c, c + 1) for c in range(planes - 1)])
    return top, den, edge, []


def output_body(count, tp_count, info_ref, *refs):
    back_refs = refs[:count]
    top_ref, den_ref, edge_ref, w_ref, odd_out, even_ref, whole, odd_ref, out_sems = refs[count:]
    depth = w_ref.shape[0]
    blocks, _, step = odd_ref.shape
    rows = top_ref.shape[0]
    heads = heads_of(depth)
    edges = []

    tails = [ref[rows:, :].astype(F32) for ref in back_refs]
    back_dens = []
    for tail in tails:
        turned = tail[:DEN_ROWS, : den_lanes(rows)]
        rest = jnp.zeros((LANES - DEN_ROWS, turned.shape[1]), F32)
        back_dens.append(jnp.concatenate([turned, rest], axis=0).T)

    some = EDGE_ROWS - DEN_ROWS
    for h, lanes in enumerate(heads):
        top, den = top_ref[:, lanes], den_ref[:, h : h + 1]
        edge, edge_den = edge_ref[:some, lanes], edge_ref[:some, depth + h : depth + h + 1]
        for ref, tail, value in zip(back_refs, tails, back_dens):
            both = value[:, h : h + 1] + value[:, len(heads) + h : len(heads) + h + 1]
            top += ref[:rows, lanes].astype(F32)
            edge += tail[DEN_ROWS:, lanes]
            den += both[:rows]
            edge_den += both[rows : rows + some]
        whole[:, lanes] = top / den
        edges.append(jnp.where(edge_den > 0, edge / jnp.where(edge_den > 0, edge_den, 1.0), 0.0))
    edge = jnp.concatenate(edges, axis=1)[:1]
    patches = rows // tp_count
    me = info_ref[1]
    before = []
    for bits in block_order(tp_count):
        peer = me ^ bits
        source = block_place(me ^ ((peer + tp_count - 1) % tp_count), tp_count)
        row = whole[pl.ds(source * patches + patches - 1, 1), :]
        before.append(jnp.where(peer == 0, edge, row))
    for index, row in enumerate(before):
        at = index * patches + patches - 1
        whole[at : at + 1, :] = row
    attended = whole[...].astype(BF16)
    half = rows // 2
    sends = []
    for n in range(blocks):
        at = pl.ds(n * step, step)
        out = dot(attended, w_ref[:, at])
        odd_ref[n] = out[half:].astype(BF16)
        sends.append(pltpu.make_async_copy(odd_ref.at[n], odd_out.at[:, at], out_sems.at[n]))
        sends[-1].start()
        even_ref[:, at] = out[:half].astype(BF16)
    for copy in sends:
        copy.wait()


def output_project(info, top, den, edge, back, weights, tp_count):
    rows, depth = top.shape
    width = weights.shape[1]
    step = min(width, 1024)
    here, there = pl.BlockSpec(memory_space=pltpu.VMEM), pl.BlockSpec(memory_space=pltpu.HBM)
    blocks = width // step
    odd, even = pl.pallas_call(
        functools.partial(output_body, len(back), tp_count),
        in_specs=[pl.BlockSpec(memory_space=pltpu.SMEM)] + [here] * (4 + len(back)),
        out_specs=[there, here],
        out_shape=[
            pltpu.HBM((rows // 2, width), BF16),
            jax.ShapeDtypeStruct((rows // 2, width), BF16),
        ],
        scratch_shapes=[
            pltpu.VMEM((rows, depth), F32),
            pltpu.VMEM((blocks, rows // 2, step), BF16),
            pltpu.SemaphoreType.DMA((blocks,)),
        ],
        compiler_params=params(16),
    )(info, *back, top, den, edge, weights)
    return even, odd


def pair_sum_body(mine_ref, other_ref, own_ref, *send_refs):
    patches = own_ref.shape[0]
    total = mine_ref[...].astype(F32) + other_ref[...].astype(F32)
    own_ref[...] = total[:patches]
    for index, ref in enumerate(send_refs):
        ref[...] = total[(index + 1) * patches : (index + 2) * patches].astype(BF16)


def scatter_sum(even, odd, patches):
    blocks = even.shape[0] // patches
    block = (patches, even.shape[1])
    pieces = call(pair_sum_body, [(block, F32)] + [(block, BF16)] * (blocks - 1))(
        even, swap(odd, 1)
    )
    return [pieces[0]] + [swap(pieces[k], 2 * k) for k in range(blocks - 1, 0, -1)]


def state_body(count, *refs):
    terms = refs[:count]
    local_ref, normed, state_out, normed_ref, wide = refs[count:]
    patches = terms[0].shape[0]
    width = normed_ref.shape[1]
    chunks = width // LANES
    for b in range(PATCH):
        at = slice(b * width, (b + 1) * width)
        total = terms[0][:, at]
        for term in terms[1:]:
            total += term[:, at].astype(F32)
        part = pltpu.roll(total.astype(BF16).astype(F32), 1, 0)
        for c in range(chunks):
            wide[c, pl.ds(b, patches, stride=PATCH), :] = part[:, c * LANES : (c + 1) * LANES]
    context = jnp.concatenate([wide[c] for c in range(chunks)], axis=1)
    state = local_ref[...].astype(F32) + context
    state_out.ref[...] = state
    state_out.send()
    mean = jnp.mean(state * state, axis=-1, keepdims=True)
    normed_ref[...] = (state * lax.rsqrt(mean + EPS)).astype(BF16)
    normed.ref[...] = normed_ref[...]


def byte_state(terms, local_embeds, after):
    rows, width = local_embeds.shape
    normed, state, normed_near = staged(
        functools.partial(state_body, len(terms)),
        [*terms, local_embeds],
        [((rows, width), BF16), ((rows, width), F32)],
        [((rows, width), BF16)],
        [pltpu.VMEM((width // LANES, rows, LANES), F32)],
        after=after,
    )
    return state, normed, normed_near


def unit(x):
    scale = lax.rsqrt(jnp.mean(x * x, axis=-1, keepdims=True) + EPS)
    return x * scale, scale


def unit_back(grad, y, scale):
    return scale * (grad - y * jnp.mean(grad * y, axis=-1, keepdims=True))


def prepare_body(parts, info_ref, gb_ref, wq_ref, wk_ref, wv_ref, wo_ref, token_ref, *refs):
    token_ref[...] = jnp.zeros_like(token_ref)
    weights_ref = refs[0]
    d = LOCAL_HEAD_DIM
    rows = refs[1].shape[0] // len(parts[0])
    for kind, ref in enumerate((wq_ref, wk_ref, wv_ref)):
        weights_ref[:, kind * d : (kind + 1) * d] = ref[0]
    for index, part in enumerate(parts):
        out_ref, core_ref = refs[1 + 2 * index : 3 + 2 * index]
        for place, bits in enumerate(part):
            at = pl.multiple_of((info_ref[1] ^ bits) * rows, rows)
            out_ref[place * rows : (place + 1) * rows, :] = gb_ref[pl.ds(at, rows), :]
        core_ref[...] = dot(out_ref[...], wo_ref[0], ((1,), (1,))).astype(BF16)


def prepare(info, gb_all, local_qkv, local_out, rows, parts):
    width = gb_all.shape[1]
    d = LOCAL_HEAD_DIM
    heads = LOCAL_HEADS

    def qkv_spec(kind):
        return pl.BlockSpec((1, width, d), lambda i, info: (0, 0, kind * heads + info[0]))

    outs = [(width, 3 * d)]
    for part in parts:
        outs += [(len(part) * rows, width), (len(part) * rows, d)]
    token, weights, *blocks = pl.pallas_call(
        functools.partial(prepare_body, parts),
        grid_spec=pltpu.PrefetchScalarGridSpec(
            num_scalar_prefetch=1,
            grid=(1,),
            in_specs=[
                pl.BlockSpec(gb_all.shape, lambda i, info: (0, 0)),
                qkv_spec(0),
                qkv_spec(1),
                qkv_spec(2),
                pl.BlockSpec((1, d, width), lambda i, info: (0, info[0], 0)),
            ],
            out_specs=[pl.BlockSpec(shape, lambda i, info: (0, 0)) for shape in [TOKEN.shape, *outs]],
        ),
        out_shape=[TOKEN] + [jax.ShapeDtypeStruct(shape, BF16) for shape in outs],
        compiler_params=params(LARGE),
    )(info, gb_all, local_qkv, local_qkv, local_qkv, local_out)
    return token, weights, blocks[0::2], blocks[1::2]


def window(rows):
    row = lax.broadcasted_iota(jnp.int32, (rows, rows), 0)
    column = lax.broadcasted_iota(jnp.int32, (rows, rows), 1)
    return (row // PATCH == column // PATCH) & (column <= row)


def core_weights(qkv, allowed):
    d = LOCAL_HEAD_DIM
    q, q_scale = unit(qkv[:, :d])
    k, k_scale = unit(qkv[:, d : 2 * d])
    qb, kb, vb = q.astype(BF16), k.astype(BF16), qkv[:, 2 * d :].astype(BF16)
    expo = jnp.where(allowed, jnp.exp(dot(qb, kb, ((1,), (1,))) * (1.0 / math.sqrt(d))), 0.0)
    weight = expo / jnp.sum(expo, axis=-1, keepdims=True)
    return (q, q_scale, qb), (k, k_scale, kb), vb, weight


def core_forward(weight, vb):
    return dot(weight.astype(BF16), vb).astype(BF16)


def core_backward(query, key, vb, weight, gradb):
    q, q_scale, qb = query
    k, k_scale, kb = key
    grad_v = dot(weight.astype(BF16), gradb, ((0,), (0,)))
    grad_w = dot(gradb, vb, ((1,), (1,)))
    mean = jnp.sum(weight * grad_w, axis=-1, keepdims=True)
    grad_s = (weight * (grad_w - mean) * (1.0 / math.sqrt(LOCAL_HEAD_DIM))).astype(BF16)
    grad_q = unit_back(dot(grad_s, kb), q, q_scale)
    grad_k = unit_back(dot(grad_s, qb, ((0,), (0,))), k, k_scale)
    return jnp.concatenate([grad_q, grad_k, grad_v], axis=1).astype(BF16)


def chunks_in(piece):
    return jnp.concatenate(
        [piece[:, at : at + LANES] for at in range(0, piece.shape[1], LANES)], axis=0
    )


def chunks_out(value, rows):
    return jnp.concatenate(
        [value[at : at + rows] for at in range(0, value.shape[0], rows)], axis=1
    )


def rows_of(refs):
    return jnp.concatenate([ref[...] for ref in refs], axis=0)


def local_body(count, *refs):
    x_refs, refs = refs[:count], refs[count:]
    (gb_ref, core_ref, w_ref), refs = refs[:3], refs[3:]
    carry, (gqkv_ref, gout_ref, ab_ref, token_ref) = refs[:-4], refs[-4:]
    token_ref[...] = jnp.zeros_like(token_ref)
    gqkv, gout, abs_ = local_grads(x_refs, gb_ref, core_ref, w_ref, carry)
    gqkv_ref[...] = gqkv
    gout_ref[...] = gout
    ab_ref[...] = jnp.concatenate(abs_, axis=0)


def local_grads(x_refs, gb_ref, core_ref, w_ref, carry):
    x = rows_of(x_refs)
    rows = x_refs[0].shape[0]
    tile = rows // 2 if rows % (2 * BF16_ROWS) == 0 else rows
    allowed = window(tile)
    qkv = dot(x, w_ref[...])
    abs_, gqs = [], []
    for start in range(0, x.shape[0], tile):
        at = slice(start, start + tile)
        query, key, vb, weight = core_weights(qkv[at], allowed)
        abs_.append(core_forward(weight, vb))
        gqs.append(core_backward(query, key, vb, weight, core_ref[at, :]))
    gqkv = dot(jnp.concatenate(gqs, axis=0), x, ((0,), (0,)))
    gout = dot(jnp.concatenate(abs_, axis=0), gb_ref[...], ((0,), (0,)))
    if carry:
        gqkv += carry[0][...]
        gout += carry[1][...]
    return gqkv, gout, abs_


def local_last_body(count, rounds, info_ref, *refs):
    x_refs, refs = refs[:count], refs[count:]
    gb_ref, core_ref, w_ref, *refs = refs
    *carry, ab0_ref = refs[:3]
    gqkv_out, message, *pieces = refs[3 : 4 + rounds]
    own_ref, held = refs[4 + rounds :]
    gqkv, gout, abs_ = local_grads(x_refs, gb_ref, core_ref, w_ref, carry)
    held[...] = gout
    deep = own_ref.shape[0]
    piece_rows = deep * LANES // held.shape[1]
    for k in range(rounds):
        at = pl.multiple_of((info_ref[2] ^ k) * piece_rows, piece_rows)
        piece = chunks_in(held[pl.ds(at, piece_rows), :]).astype(BF16)
        if k:
            pieces[k - 1].ref[...] = piece
            pieces[k - 1].send()
        else:
            own_ref[...] = piece
    gqkv_out.ref[...] = gqkv.T.astype(BF16)
    gqkv_out.send()
    rows = x_refs[0].shape[0]
    message.ref[:rows, :] = ab0_ref[rows:, :]
    message.ref[rows:, :] = jnp.concatenate(abs_, axis=0)


def relay_body(*refs):
    ab0_ref, ab1_ref, there_ref, *messages, own_ref = refs
    rows = ab0_ref.shape[0] // 2
    for k, message in enumerate(messages):
        message.ref[:rows, :] = ab1_ref[k * rows : (k + 1) * rows, :]
        message.ref[rows:, :] = there_ref[(k + 1) * rows : (k + 2) * rows, :]
        message.send()
    own_ref[:rows, :] = ab0_ref[:rows, :]
    own_ref[rows:, :] = there_ref[:rows, :]


def planes_body(rounds, planes, info_ref, *refs):
    pieces, outs, held = refs[:rounds], refs[rounds:-1], refs[-1]
    for k, piece in enumerate(pieces):
        held[k] = piece[...].astype(F32)
    for z, out in enumerate(outs):
        total = None
        for outer in range(rounds // planes):
            term = held[info_ref[2] ^ ((info_ref[3] ^ z) + outer * planes)]
            total = term if total is None else total + term
        out.ref[...] = total.astype(BF16)
        out.send()


def local_layer(normed, normed_near, info, parts, gbs, cores, weights, rounds, planes):
    rows, width = normed.shape
    d = LOCAL_HEAD_DIM
    near = [swap(normed, bits) for bits in parts[1]]
    count = len(near)
    totals = [((3 * d, width), F32), ((d, width), F32)]

    def step(index, xs, carry):
        return staged(
            functools.partial(local_body, len(xs)),
            [*xs, gbs[index], cores[index], weights, *carry],
            [],
            [*totals, ((len(xs) * rows, d), BF16), TOKEN],
            flops=1 << 34,
            mib=20,
        )

    *carry, ab0, done = step(0, [normed_near, swap(normed, 1)], [])
    near = [tie(block, done) for block in near]
    far = [swap(block, 1) for block in near]
    *carry, ab1, _ = step(1, near, carry)
    deep = d // rounds * width // LANES
    piece = ((deep, d), BF16)
    grad_qkv, message, *pieces, own = staged(
        functools.partial(local_last_body, count, rounds),
        [*far, gbs[2], cores[2], weights, *carry, ab0],
        [((width, 3 * d), BF16), (((count + 1) * rows, d), BF16)] + [piece] * (rounds - 1),
        [piece],
        [pltpu.VMEM((d, width), F32)],
        info,
        flops=1 << 34,
        mib=20,
    )
    pieces = [own] + [swap(value, k + 1) for k, value in enumerate(pieces)]
    block = ((2 * rows, d), BF16)
    *sent, own = staged(
        relay_body, [ab0, ab1, swap(message, 1)], [block] * count, [block]
    )
    messages = [own] + [swap(value, 2 * (k + 1)) for k, value in enumerate(sent)]
    pieces = staged(
        functools.partial(planes_body, rounds, planes),
        pieces,
        [piece] * planes,
        scratch=[pltpu.VMEM((rounds, deep, d), F32)],
        info=info,
    )
    return messages, pieces, grad_qkv


def hidden_body(heads, info_ref, state_ref, w_ref, *refs):
    *messages, out_ref, token_ref = refs
    token_ref[...] = jnp.zeros_like(token_ref)
    rows = state_ref.shape[0]
    d = LOCAL_HEAD_DIM
    total = state_ref[...]
    for bits in range(2 * len(messages)):
        at = bits % 2 * rows
        head = heads(info_ref[1] ^ bits)
        weights = w_ref[0, pl.ds(pl.multiple_of(head * d, d), d), :]
        total += dot(messages[bits // 2][at : at + rows, :], weights)
    out_ref[...] = total.astype(BF16)


def final_body(heads, parts_ref, _, *refs):
    *terms, gqkv_ref, gout_ref = refs
    gout = sum(term[...].astype(F32) for term in terms)
    gout_ref[0] = chunks_out(gout, gout_ref.shape[1])
    d = LOCAL_HEAD_DIM
    tp_count = len(heads)
    for h in range(LOCAL_HEADS):
        total = None
        for source in range(parts_ref.shape[0]):
            if heads[source % tp_count] == h:
                term = parts_ref[source].astype(F32)
                total = term if total is None else total + term
        for kind in range(3):
            at = (kind * LOCAL_HEADS + h) * d
            gqkv_ref[0, :, at : at + d] = total[:, kind * d : (kind + 1) * d]


def swap_planes(pieces):
    count = len(pieces)
    return [pieces[0]] + [
        lax.ppermute(pieces[k], "ctx", [(c, c ^ k) for c in range(count)]) for k in range(1, count)
    ]


def per_device(byte_embeds, local_embeds, global_qkv, global_out, local_qkv, local_out, cotangent):
    byte_count, width = byte_embeds.shape
    patches = byte_count // PATCH
    planes, tp_count = lax.axis_size("ctx"), lax.axis_size("tp")
    plane, me = lax.axis_index("ctx"), lax.axis_index("tp")
    order = block_order(tp_count)
    shard_rows = tp_count * patches
    devices = planes * tp_count

    group = min(tp_count, LOCAL_HEADS)
    share = width // devices
    rounds = LOCAL_HEAD_DIM // share
    plane_heads = LOCAL_HEADS // planes

    def head_of(t):
        return (t % rounds) % planes * plane_heads + t // rounds

    heads = [head_of(t) for t in range(tp_count)]
    head_info = jnp.stack([head_of(me), me, me % rounds, plane]).astype(jnp.int32)

    patch_in = patch_norm(byte_embeds)
    mine = swap(patch_in, 1)
    weights_in, head_info = preload(global_qkv, head_info, mine)
    even = [tie(swap(patch_in, bits), head_info) for bits in range(2, tp_count, 2)]
    pieces = [patch_in, *even, mine, *(swap(piece, 1) for piece in even)]
    q, kv, gb, kv_near = project(head_info, pieces, weights_in, global_qkv, cotangent, tp_count)

    place = (
        (me ^ jnp.array(order, jnp.int32))[:, None] * patches
        + jnp.arange(patches, dtype=jnp.int32)[None, :]
    ).reshape(-1)
    fits = den_lanes(shard_rows) < q.shape[1] and 2 * q.shape[1] // HEAD_DIM <= DEN_ROWS
    if planes == 4 and fits:
        mask = (place[None, :] <= place[:, None]).astype(F32)
        top, den, edge, back = attend_paired(
            head_info, q, kv, kv_near, mask, tp_count
        )
    else:
        key_place = (
            jnp.arange(planes, dtype=jnp.int32)[:, None] * shard_rows + place[None, :]
        ).reshape(-1)
        mask = (key_place[None, :] <= (plane * shard_rows + place)[:, None]).astype(F32)
        top, den, edge, back = attend_all(head_info, q, kv, mask, tp_count)

    weights_out, _ = preload(global_out, head_info, den)
    even, odd = output_project(head_info, top, den, edge, back, weights_out, tp_count)

    parts = [[0, 1], list(range(2, group, 2)), list(range(3, group, 2))]
    gb_all = lax.all_gather(gb, "tp", axis=0, tiled=True)
    prepared, weights, gbs, cores = prepare(head_info, gb_all, local_qkv, local_out, byte_count, parts)
    state, normed, normed_near = byte_state(
        scatter_sum(even, odd, patches), local_embeds, prepared
    )
    messages, out_pieces, grad_qkv = local_layer(
        normed, normed_near, head_info, parts, gbs, cores, weights, rounds, planes
    )
    grad_qkv = lax.all_to_all(grad_qkv, ("ctx", "tp"), 0, 0, tiled=True)
    out_pieces = swap_planes(out_pieces)
    here = pl.BlockSpec(memory_space=pltpu.VMEM)
    hidden, done = pl.pallas_call(
        functools.partial(hidden_body, head_of),
        in_specs=[pl.BlockSpec(memory_space=pltpu.SMEM)] + [here] * (2 + len(messages)),
        out_specs=[here, here],
        out_shape=[jax.ShapeDtypeStruct((byte_count, width), BF16), TOKEN],
        compiler_params=params(16),
    )(head_info, state, local_out, *messages)
    grad_qkv, grad_out = call(
        functools.partial(final_body, heads),
        [((1, share, 3 * width), F32), ((1, share, width), F32)],
        mib=16,
    )(grad_qkv.reshape(devices, share, 3 * LOCAL_HEAD_DIM), done, *out_pieces)
    return (hidden, grad_qkv, grad_out)


def solution(mesh):
    in_specs = (
        P(("ctx", "tp"), None),
        P(("ctx", "tp"), None),
        P(None, None, "tp"),
        P("tp", None),
        P(),
        P(),
        P(("ctx", "tp"), None),
    )
    out_specs = (P(("ctx", "tp"), None), P(None, ("ctx", "tp"), None), P(None, ("ctx", "tp"), None))
    return jax.shard_map(
        per_device, mesh=mesh, in_specs=in_specs, out_specs=out_specs, check_vma=False
    )
```

```python
import functools
import math

import jax
import jax.numpy as jnp
from jax import lax
from jax.experimental import pallas as pl
from jax.experimental.pallas import tpu as pltpu
from jax.sharding import PartitionSpec as P

PATCH = 8
HEAD_DIM = 128
LOCAL_HEADS = 8
LOCAL_HEAD_DIM = 128
EPS = 1e-06
F32 = jnp.float32
BF16 = jnp.bfloat16
MIB = 1 << 20
LARGE = 60
TOKEN = pltpu.VMEM((8, 128), jnp.float32)
LANES = 128
EDGE_ROWS = 16
DEN_ROWS = 8
BF16_ROWS = 16


def params(mib):
    return pltpu.CompilerParams(vmem_limit_bytes=mib * MIB)


def call(body, outs, scratch=(), mib=32):
    return pl.pallas_call(
        body,
        out_shape=[out if out is TOKEN else jax.ShapeDtypeStruct(*out) for out in outs],
        scratch_shapes=list(scratch),
        compiler_params=params(mib),
    )


class Held:
    def __init__(self, source, target, sem):
        self.ref, self.copy, self.waited = target, pltpu.make_async_copy(source, target, sem), False
        self.copy.start()

    def __call__(self):
        if not self.waited:
            self.copy.wait()
            self.waited = True
        return self.ref


class Sent:
    def __init__(self, source, target, sem):
        self.ref, self.copy, self.started = source, pltpu.make_async_copy(source, target, sem), False

    def send(self):
        self.copy.start()
        self.started = True


def staged(body, args, sent, outs=(), scratch=(), info=None, mib=16, flops=0, after=None, held=()):
    tokens = [] if after is None else [after]
    counts = [len(args), len(held), len(tokens), len(sent), len(outs)]
    counts += [len(held), len(sent), len(scratch)]

    def kernel(*refs):
        refs = list(refs)
        info_ref = [refs.pop(0)] if info is not None else []
        groups = []
        for count in counts:
            groups.append(refs[:count])
            del refs[:count]
        in_refs, held_far, _, sent_far, out_refs, held_near, sent_near, own = groups
        in_sems, out_sems = refs
        inputs = [Held(f, n, in_sems.at[i]) for i, (f, n) in enumerate(zip(held_far, held_near))]
        outputs = [Sent(n, f, out_sems.at[i]) for i, (f, n) in enumerate(zip(sent_far, sent_near))]
        body(*info_ref, *in_refs, *inputs, *outputs, *out_refs, *own)
        for output in outputs:
            if not output.started:
                output.send()
        for value in inputs:
            value()
        for output in outputs:
            output.copy.wait()

    here, there = pl.BlockSpec(memory_space=pltpu.VMEM), pl.BlockSpec(memory_space=pltpu.HBM)
    free = pl.BlockSpec(memory_space=pl.ANY)
    scalars = [] if info is None else [info]
    return pl.pallas_call(
        kernel,
        in_specs=[pl.BlockSpec(memory_space=pltpu.SMEM)] * len(scalars)
        + [here] * len(args)
        + [free] * (len(held) + len(tokens)),
        out_specs=[there] * len(sent) + [here] * len(outs),
        out_shape=[pltpu.HBM(shape, dtype) for shape, dtype in sent]
        + [out if out is TOKEN else jax.ShapeDtypeStruct(*out) for out in outs],
        scratch_shapes=[pltpu.VMEM(value.shape, value.dtype) for value in held]
        + [pltpu.VMEM(shape, dtype) for shape, dtype in sent]
        + list(scratch)
        + [pltpu.SemaphoreType.DMA((max(1, count),)) for count in (len(held), len(sent))],
        compiler_params=params(mib),
        cost_estimate=pl.CostEstimate(flops=flops, bytes_accessed=1 << 22, transcendentals=0),
    )(*scalars, *args, *held, *tokens)


def dot(a, b, dims=((1,), (0,))):
    return lax.dot_general(a, b, (dims, ((), ())), preferred_element_type=F32)


def swap(value, bits):
    count = lax.axis_size("tp")
    return lax.ppermute(value, "tp", [(source, source ^ bits) for source in range(count)])


def block_order(size):
    return list(range(0, size, 2)) + list(range(1, size, 2))


def gather(value, size):
    even = [value] + [swap(value, bits) for bits in range(2, size, 2)]
    return even + [swap(piece, 1) for piece in even]


def tie_body(*refs):
    pass


def tie(value, *after, mib=1):
    there = pl.BlockSpec(memory_space=pl.ANY)
    return pl.pallas_call(
        tie_body,
        in_specs=[there] * (1 + len(after)),
        out_specs=there,
        out_shape=jax.ShapeDtypeStruct(value.shape, value.dtype),
        input_output_aliases={0: 0},
        compiler_params=params(mib),
    )(value, *after)


def preload_body(parts, info_ref, w_ref, _, out_ref, info_out, sems):
    for index in range(info_ref.shape[0]):
        info_out[index] = info_ref[index]
    source = w_ref.at[0] if len(w_ref.shape) == 3 else w_ref
    size = source.shape[0] // parts
    copies = []
    for part in range(parts):
        at = pl.ds(part * size, size)
        copies.append(pltpu.make_async_copy(source.at[at], out_ref.at[at], sems.at[part]))
        copies[-1].start()
    for copy in copies:
        copy.wait()


def preload(weights, info, after, parts=8):
    there = pl.BlockSpec(memory_space=pl.ANY)
    scalar = pl.BlockSpec(memory_space=pltpu.SMEM)
    shape = weights.shape[-2:]
    return pl.pallas_call(
        functools.partial(preload_body, parts),
        in_specs=[scalar, there, there],
        out_specs=[pl.BlockSpec(memory_space=pltpu.VMEM), scalar],
        out_shape=[
            pltpu.VMEM(shape, weights.dtype),
            jax.ShapeDtypeStruct(info.shape, info.dtype),
        ],
        scratch_shapes=[pltpu.SemaphoreType.DMA((parts,))],
        compiler_params=params(50),
        cost_estimate=pl.CostEstimate(
            flops=0, bytes_accessed=2 * math.prod(shape), transcendentals=0
        ),
    )(info, weights, after)


def patch_norm_body(x_ref, out_ref, wide):
    patches = out_ref.shape[0]
    width = x_ref.shape[1]
    total = jnp.zeros((patches, LANES), F32)
    for c in range(width // LANES):
        wide[c] = x_ref[:, c * LANES : (c + 1) * LANES].astype(F32)
    for c in range(width // LANES):
        for b in range(PATCH):
            part = wide[c, pl.ds(b, patches, stride=PATCH), :]
            total += part * part
    scale = lax.rsqrt(jnp.sum(total, axis=-1, keepdims=True) / (PATCH * width) + EPS)
    for b in range(PATCH):
        for c in range(width // LANES):
            part = wide[c, pl.ds(b, patches, stride=PATCH), :]
            at = b * width + c * LANES
            out_ref[:, at : at + LANES] = (part * scale).astype(BF16)


def patch_norm(byte_embeds):
    rows, width = byte_embeds.shape
    return call(
        patch_norm_body,
        [((rows // PATCH, PATCH * width), BF16)],
        [pltpu.VMEM((width // LANES, rows, LANES), F32)],
        16,
    )(byte_embeds)[0]


def stack(refs):
    return jnp.concatenate([ref[...].astype(F32) for ref in refs], axis=0).astype(BF16)


def project_body(count, tp_count, info_ref, *refs):
    x_refs, refs = refs[:count], refs[count:]
    first_ref, pass_ref, w_ref, q, kv, passed, kv_ref, q_ref, held, wide, sems = refs
    kinds, rows, _ = held.shape
    depth = math.gcd(rows, 1024)
    copies = {}
    for c in range(kinds):
        for k in range(0, rows, depth):
            at = pl.ds(k, depth)
            copies[c, k] = pltpu.make_async_copy(
                w_ref.at[c + 1, at], held.at[c, at], sems.at[len(copies)]
            )
            copies[c, k].start()
    x = stack(x_refs)
    count_rows = x.shape[0]
    passed.ref[...] = pass_ref[...]
    passed.send()
    for c in range(kinds + 1):
        total = None
        for k in range(0, rows, depth):
            if c:
                copies[c - 1, k].wait()
                w = held[c - 1, k : k + depth, :]
            else:
                w = first_ref[k : k + depth, :]
            term = dot(x[:, k : k + depth], w)
            total = term if total is None else total + term
        for h in range(total.shape[1] // HEAD_DIM):
            at = slice(h * HEAD_DIM, (h + 1) * HEAD_DIM)
            part = total[:, at]
            if c < 2:
                part = part * lax.rsqrt(jnp.mean(part * part, axis=-1, keepdims=True) + EPS)
            if c == 0:
                wide[:, at] = part
            else:
                kv_ref[(c - 1) * count_rows : c * count_rows, at] = part.astype(BF16)
        if c == 0:
            q_ref[...] = wide[...].astype(BF16)
            q.ref[...] = q_ref[...]
            q.send()
            last = wide[pl.ds(last_row(info_ref, count_rows, tp_count), 1), :]
            spread = jnp.broadcast_to(last, (EDGE_ROWS, last.shape[1]))
            kv_ref[kinds * count_rows :, :] = spread.astype(BF16)


def project(info, pieces, first, weights, passed, tp_count):
    rows = sum(piece.shape[0] for piece in pieces)
    kinds, deep, width = weights.shape
    here, there = pl.BlockSpec(memory_space=pltpu.VMEM), pl.BlockSpec(memory_space=pltpu.HBM)
    outs = [((rows, width), BF16), (((kinds - 1) * rows + EDGE_ROWS, width), BF16)]
    outs.append((passed.shape, passed.dtype))
    count = len(pieces)

    def body(*refs):
        in_refs, refs = refs[: count + 4], refs[count + 4 :]
        far, kept, near, (held, wide, sems, out_sems) = refs[:3], refs[3:5], refs[5:8], refs[8:]
        outputs = [Sent(n, f, out_sems.at[i]) for i, (f, n) in enumerate(zip(far, near))]
        project_body(count, tp_count, *in_refs, *outputs, *kept, held, wide, sems)
        near[1][...] = kept[0][...]
        outputs[1].send()
        for output in outputs:
            output.copy.wait()

    return pl.pallas_call(
        body,
        in_specs=[pl.BlockSpec(memory_space=pltpu.SMEM)]
        + [here] * (count + 2)
        + [pl.BlockSpec(memory_space=pl.ANY)],
        out_specs=[there] * 3 + [here] * 2,
        out_shape=[pltpu.HBM(shape, dtype) for shape, dtype in outs]
        + [jax.ShapeDtypeStruct(*outs[1]), jax.ShapeDtypeStruct(*outs[0])],
        scratch_shapes=[pltpu.VMEM(shape, dtype) for shape, dtype in outs]
        + [
            pltpu.VMEM((kinds - 1, deep, width), BF16),
            pltpu.VMEM((rows, width), F32),
            pltpu.SemaphoreType.DMA(((kinds - 1) * deep // math.gcd(deep, 1024),)),
            pltpu.SemaphoreType.DMA((3,)),
        ],
        compiler_params=params(40),
    )(info, *pieces, first, passed, weights)


def heads_of(ref_width):
    return [slice(at, at + HEAD_DIM) for at in range(0, ref_width, HEAD_DIM)]


def last_row(info_ref, rows, tp_count):
    return block_place(info_ref[1] ^ (tp_count - 1), tp_count) * (rows // tp_count) + (
        rows // tp_count - 1
    )


def block_place(bits, size):
    return bits // 2 + (bits % 2) * (size // 2)


def split_den(dens, count):
    high = dens.astype(BF16).astype(F32)
    return high + pltpu.roll(dens - high, count, 1)


ROOT = 1.0 / math.sqrt(HEAD_DIM)


def weigh(q, k):
    expo = jnp.exp(dot(q, k, ((1,), (1,))) * ROOT)
    return expo, jnp.sum(expo, axis=-1, keepdims=True)


def den_lanes(rows):
    return -(-(rows + 1) // LANES) * LANES


def far_body(tp_count, info_ref, kv_ref, kv_in_ref, q3_ref, q2_ref, *refs):
    back3, back2, token_ref, far_top, far_den = refs
    token_ref[...] = jnp.zeros_like(token_ref)
    rows, width = q2_ref.shape
    heads = heads_of(width)
    count = len(heads)
    keys, values = slice(0, rows), slice(rows, 2 * rows)
    queries = jnp.concatenate([q3_ref[...], q2_ref[...], kv_ref[2 * rows :, :]], axis=0)
    lane = lax.broadcasted_iota(jnp.int32, far_den.shape, 1)
    dens = jnp.zeros(far_den.shape, F32)
    for h, at in enumerate(heads):
        k = jnp.concatenate([kv_ref[keys, at], kv_in_ref[keys, at]], axis=0)
        v = jnp.concatenate([kv_ref[values, at], kv_in_ref[values, at]], axis=0)
        expo, den = weigh(queries[:, at], k)
        far_top[:, at] = dot(expo.astype(BF16), v)
        dens = jnp.where(lane == h, den, dens)
    far_den[...] = dens

    def fill(back, start, edge_row):
        back.ref[:rows, :] = far_top[start : start + rows, :].astype(BF16)
        edge_den = jnp.broadcast_to(far_den[pl.ds(edge_row, 1), :], (den_lanes(rows) - rows, LANES))
        den = jnp.concatenate([far_den[start : start + rows, :], edge_den], axis=0)
        turned = split_den(den, count).T[:DEN_ROWS]
        rest = jnp.zeros((DEN_ROWS, width - turned.shape[1]), F32)
        edge = jnp.broadcast_to(far_top[pl.ds(edge_row, 1), :], (EDGE_ROWS - DEN_ROWS, width))
        tail = jnp.concatenate([jnp.concatenate([turned, rest], axis=1), edge], axis=0)
        back.ref[rows:, :] = tail.astype(BF16)
        back.send()

    fill(back2, rows, 2 * rows)
    fill(back3, 0, rows + last_row(info_ref, rows, tp_count))


def near_body(info_ref, q_ref, kv_ref, kv_in_ref, mask_ref, _, top_ref, den_ref, edge_ref):
    rows, width = q_ref.shape
    allowed = mask_ref[...] > 0
    linked = jnp.where(info_ref[3] % 2 == 1, 1.0, 0.0)
    lane = lax.broadcasted_iota(jnp.int32, (rows, LANES), 1)
    edge_lane = lax.broadcasted_iota(jnp.int32, (EDGE_ROWS, LANES), 1)
    dens = jnp.zeros((rows, LANES), F32)
    edge_dens = jnp.zeros((EDGE_ROWS, LANES), F32)
    keys, values = slice(0, rows), slice(rows, 2 * rows)
    for h, at in enumerate(heads_of(width)):
        k, v = kv_ref[keys, at], kv_ref[values, at]
        k_in, v_in = kv_in_ref[keys, at], kv_in_ref[values, at]
        q = q_ref[:, at]
        own = jnp.where(allowed, jnp.exp(dot(q, k, ((1,), (1,))) * ROOT), 0.0)
        own_den = jnp.sum(own, axis=-1, keepdims=True)
        other, other_den = weigh(q, k_in)
        top_ref[:, at] = dot(own.astype(BF16), v) + dot((other * linked).astype(BF16), v_in)
        dens = jnp.where(lane == h, own_den + other_den * linked, dens)
        edge, edge_den = weigh(kv_in_ref[2 * rows :, at], k_in)
        edge_ref[:, at] = dot((edge * linked).astype(BF16), v_in)
        edge_dens = jnp.where(edge_lane == h, edge_den * linked, edge_dens)
    den_ref[...] = dens
    edge_ref[:, width:] = edge_dens


def attend_paired(info, q, kv, q_near, kv_near, mask, tp_count):
    kv_in = lax.ppermute(kv, "ctx", [(0, 1), (2, 3)])
    far = [lax.ppermute(q, "ctx", [(c, 1)]) for c in (3, 2)]
    rows, width = q.shape
    back = ((rows + EDGE_ROWS, width), BF16)
    total = 2 * rows + EDGE_ROWS
    back3, back2, done = staged(
        functools.partial(far_body, tp_count),
        [kv_near, kv_in, *far],
        [back, back],
        [TOKEN],
        [pltpu.VMEM((total, width), F32), pltpu.VMEM((total, LANES), F32)],
        info,
    )
    back = [lax.ppermute(back3, "ctx", [(1, 3)]), lax.ppermute(back2, "ctx", [(1, 2)])]
    top, den, edge = staged(
        near_body,
        [q_near, kv_near, kv_in, mask, done],
        [],
        [((rows, width), F32), ((rows, LANES), F32), ((EDGE_ROWS, width + LANES), F32)],
        info=info,
    )
    return top, den, edge, back


def attend_all_body(tp_count, info_ref, mask_ref, q_ref, k_ref, v_ref, top_ref, den_ref, edge_ref):
    rows, width = q_ref.shape
    allowed = mask_ref[...] > 0
    lane = lax.broadcasted_iota(jnp.int32, den_ref.shape, 1)
    dens = jnp.zeros(den_ref.shape, F32)
    heads = heads_of(width)
    for h, at in enumerate(heads):
        scores = dot(q_ref[:, at], k_ref[:, at], ((1,), (1,))) * (1.0 / math.sqrt(HEAD_DIM))
        expo = jnp.where(allowed, jnp.exp(scores), 0.0)
        top_ref[:, at] = dot(expo.astype(BF16), v_ref[:, at])
        dens = jnp.where(lane == h, jnp.sum(expo, axis=-1, keepdims=True), dens)
    den_ref[...] = dens
    last = last_row(info_ref, rows, tp_count)
    count = edge_ref.shape[0]
    top = jnp.broadcast_to(top_ref[pl.ds(last, 1), :], (count, width))
    den = jnp.broadcast_to(den_ref[pl.ds(last, 1), :], (count, LANES))
    edge_ref[:, :width] = top
    edge_ref[:, width:] = den


def attend_all(info, q, kv, mask, tp_count):
    planes = lax.axis_size("ctx")
    rows, width = q.shape
    keys = lax.all_gather(kv[:rows], "ctx", axis=0, tiled=True)
    values = lax.all_gather(kv[rows : 2 * rows], "ctx", axis=0, tiled=True)
    here = pl.BlockSpec(memory_space=pltpu.VMEM)
    outs = [((rows, width), F32), ((rows, LANES), F32), ((EDGE_ROWS, width + LANES), F32)]
    top, den, edge = pl.pallas_call(
        functools.partial(attend_all_body, tp_count),
        in_specs=[pl.BlockSpec(memory_space=pltpu.SMEM)] + [here] * 4,
        out_specs=[here] * 3,
        out_shape=[jax.ShapeDtypeStruct(shape, dtype) for shape, dtype in outs],
        compiler_params=params(48),
    )(info, mask, q, keys, values)
    edge = lax.ppermute(edge, "ctx", [(c, c + 1) for c in range(planes - 1)])
    return top, den, edge, []


def output_body(count, tp_count, info_ref, *refs):
    back_refs = refs[:count]
    top_ref, den_ref, edge_ref, w_ref, odd_out, even_ref, whole, odd_ref, out_sems = refs[count:]
    depth = w_ref.shape[0]
    blocks, _, step = odd_ref.shape
    rows = top_ref.shape[0]
    heads = heads_of(depth)
    edges = []

    tails = [ref[rows:, :].astype(F32) for ref in back_refs]
    back_dens = []
    for tail in tails:
        turned = tail[:DEN_ROWS, : den_lanes(rows)]
        rest = jnp.zeros((LANES - DEN_ROWS, turned.shape[1]), F32)
        back_dens.append(jnp.concatenate([turned, rest], axis=0).T)

    some = EDGE_ROWS - DEN_ROWS
    for h, lanes in enumerate(heads):
        top, den = top_ref[:, lanes], den_ref[:, h : h + 1]
        edge, edge_den = edge_ref[:some, lanes], edge_ref[:some, depth + h : depth + h + 1]
        for ref, tail, value in zip(back_refs, tails, back_dens):
            both = value[:, h : h + 1] + value[:, len(heads) + h : len(heads) + h + 1]
            top += ref[:rows, lanes].astype(F32)
            edge += tail[DEN_ROWS:, lanes]
            den += both[:rows]
            edge_den += both[rows : rows + some]
        whole[:, lanes] = top / den
        edges.append(jnp.where(edge_den > 0, edge / jnp.where(edge_den > 0, edge_den, 1.0), 0.0))
    edge = jnp.concatenate(edges, axis=1)[:1]
    patches = rows // tp_count
    me = info_ref[1]
    before = []
    for bits in block_order(tp_count):
        peer = me ^ bits
        source = block_place(me ^ ((peer + tp_count - 1) % tp_count), tp_count)
        row = whole[pl.ds(source * patches + patches - 1, 1), :]
        before.append(jnp.where(peer == 0, edge, row))
    for index, row in enumerate(before):
        at = index * patches + patches - 1
        whole[at : at + 1, :] = row
    attended = whole[...].astype(BF16)
    half = rows // 2
    sends = []
    for n in range(blocks):
        at = pl.ds(n * step, step)
        out = dot(attended, w_ref[:, at])
        odd_ref[n] = out[half:].astype(BF16)
        sends.append(pltpu.make_async_copy(odd_ref.at[n], odd_out.at[:, at], out_sems.at[n]))
        sends[-1].start()
        even_ref[:, at] = out[:half].astype(BF16)
    for copy in sends:
        copy.wait()


def output_project(info, top, den, edge, back, weights, tp_count):
    rows, depth = top.shape
    width = weights.shape[1]
    step = min(width, 1024)
    here, there = pl.BlockSpec(memory_space=pltpu.VMEM), pl.BlockSpec(memory_space=pltpu.HBM)
    blocks = width // step
    odd, even = pl.pallas_call(
        functools.partial(output_body, len(back), tp_count),
        in_specs=[pl.BlockSpec(memory_space=pltpu.SMEM)] + [here] * (4 + len(back)),
        out_specs=[there, here],
        out_shape=[
            pltpu.HBM((rows // 2, width), BF16),
            jax.ShapeDtypeStruct((rows // 2, width), BF16),
        ],
        scratch_shapes=[
            pltpu.VMEM((rows, depth), F32),
            pltpu.VMEM((blocks, rows // 2, step), BF16),
            pltpu.SemaphoreType.DMA((blocks,)),
        ],
        compiler_params=params(16),
    )(info, *back, top, den, edge, weights)
    return even, odd


def pair_sum_body(mine_ref, other_ref, own_ref, *send_refs):
    patches = own_ref.shape[0]
    total = mine_ref[...].astype(F32) + other_ref[...].astype(F32)
    own_ref[...] = total[:patches]
    for index, ref in enumerate(send_refs):
        ref[...] = total[(index + 1) * patches : (index + 2) * patches].astype(BF16)


def scatter_sum(even, odd, patches):
    blocks = even.shape[0] // patches
    block = (patches, even.shape[1])
    pieces = call(pair_sum_body, [(block, F32)] + [(block, BF16)] * (blocks - 1))(
        even, swap(odd, 1)
    )
    return [pieces[0]] + [swap(pieces[k], 2 * k) for k in range(blocks - 1, 0, -1)]


def state_body(count, *refs):
    terms = refs[:count]
    local_ref, normed, state_out, normed_ref, wide = refs[count:]
    patches = terms[0].shape[0]
    width = normed_ref.shape[1]
    chunks = width // LANES
    for b in range(PATCH):
        at = slice(b * width, (b + 1) * width)
        total = terms[0][:, at]
        for term in terms[1:]:
            total += term[:, at].astype(F32)
        part = pltpu.roll(total.astype(BF16).astype(F32), 1, 0)
        for c in range(chunks):
            wide[c, pl.ds(b, patches, stride=PATCH), :] = part[:, c * LANES : (c + 1) * LANES]
    context = jnp.concatenate([wide[c] for c in range(chunks)], axis=1)
    state = local_ref[...].astype(F32) + context
    state_out.ref[...] = state
    state_out.send()
    mean = jnp.mean(state * state, axis=-1, keepdims=True)
    normed_ref[...] = (state * lax.rsqrt(mean + EPS)).astype(BF16)
    normed.ref[...] = normed_ref[...]


def byte_state(terms, local_embeds, after):
    rows, width = local_embeds.shape
    normed, state, normed_near = staged(
        functools.partial(state_body, len(terms)),
        [*terms, local_embeds],
        [((rows, width), BF16), ((rows, width), F32)],
        [((rows, width), BF16)],
        [pltpu.VMEM((width // LANES, rows, LANES), F32)],
        after=after,
    )
    return state, normed, normed_near


def unit(x):
    scale = lax.rsqrt(jnp.mean(x * x, axis=-1, keepdims=True) + EPS)
    return x * scale, scale


def unit_back(grad, y, scale):
    return scale * (grad - y * jnp.mean(grad * y, axis=-1, keepdims=True))


def prepare_body(parts, info_ref, gb_ref, wq_ref, wk_ref, wv_ref, wo_ref, token_ref, *refs):
    token_ref[...] = jnp.zeros_like(token_ref)
    weights_ref = refs[0]
    d = LOCAL_HEAD_DIM
    rows = refs[1].shape[0] // len(parts[0])
    for kind, ref in enumerate((wq_ref, wk_ref, wv_ref)):
        weights_ref[:, kind * d : (kind + 1) * d] = ref[0]
    for index, part in enumerate(parts):
        out_ref, core_ref = refs[1 + 2 * index : 3 + 2 * index]
        for place, bits in enumerate(part):
            at = pl.multiple_of((info_ref[1] ^ bits) * rows, rows)
            out_ref[place * rows : (place + 1) * rows, :] = gb_ref[pl.ds(at, rows), :]
        core_ref[...] = dot(out_ref[...], wo_ref[0], ((1,), (1,))).astype(BF16)


def prepare(info, gb_all, local_qkv, local_out, rows, parts):
    width = gb_all.shape[1]
    d = LOCAL_HEAD_DIM
    heads = LOCAL_HEADS

    def qkv_spec(kind):
        return pl.BlockSpec((1, width, d), lambda i, info: (0, 0, kind * heads + info[0]))

    outs = [(width, 3 * d)]
    for part in parts:
        outs += [(len(part) * rows, width), (len(part) * rows, d)]
    token, weights, *blocks = pl.pallas_call(
        functools.partial(prepare_body, parts),
        grid_spec=pltpu.PrefetchScalarGridSpec(
            num_scalar_prefetch=1,
            grid=(1,),
            in_specs=[
                pl.BlockSpec(gb_all.shape, lambda i, info: (0, 0)),
                qkv_spec(0),
                qkv_spec(1),
                qkv_spec(2),
                pl.BlockSpec((1, d, width), lambda i, info: (0, info[0], 0)),
            ],
            out_specs=[pl.BlockSpec(shape, lambda i, info: (0, 0)) for shape in [TOKEN.shape, *outs]],
        ),
        out_shape=[TOKEN] + [jax.ShapeDtypeStruct(shape, BF16) for shape in outs],
        compiler_params=params(LARGE),
    )(info, gb_all, local_qkv, local_qkv, local_qkv, local_out)
    return token, weights, blocks[0::2], blocks[1::2]


def window(rows):
    row = lax.broadcasted_iota(jnp.int32, (rows, rows), 0)
    column = lax.broadcasted_iota(jnp.int32, (rows, rows), 1)
    return (row // PATCH == column // PATCH) & (column <= row)


def core_weights(qkv, allowed):
    d = LOCAL_HEAD_DIM
    q, q_scale = unit(qkv[:, :d])
    k, k_scale = unit(qkv[:, d : 2 * d])
    qb, kb, vb = q.astype(BF16), k.astype(BF16), qkv[:, 2 * d :].astype(BF16)
    expo = jnp.where(allowed, jnp.exp(dot(qb, kb, ((1,), (1,))) * (1.0 / math.sqrt(d))), 0.0)
    weight = expo / jnp.sum(expo, axis=-1, keepdims=True)
    return (q, q_scale, qb), (k, k_scale, kb), vb, weight


def core_forward(weight, vb):
    return dot(weight.astype(BF16), vb).astype(BF16)


def core_backward(query, key, vb, weight, gradb):
    q, q_scale, qb = query
    k, k_scale, kb = key
    grad_v = dot(weight.astype(BF16), gradb, ((0,), (0,)))
    grad_w = dot(gradb, vb, ((1,), (1,)))
    mean = jnp.sum(weight * grad_w, axis=-1, keepdims=True)
    grad_s = (weight * (grad_w - mean) * (1.0 / math.sqrt(LOCAL_HEAD_DIM))).astype(BF16)
    grad_q = unit_back(dot(grad_s, kb), q, q_scale)
    grad_k = unit_back(dot(grad_s, qb, ((0,), (0,))), k, k_scale)
    return jnp.concatenate([grad_q, grad_k, grad_v], axis=1).astype(BF16)


def chunks_in(piece):
    return jnp.concatenate(
        [piece[:, at : at + LANES] for at in range(0, piece.shape[1], LANES)], axis=0
    )


def chunks_out(value, rows):
    return jnp.concatenate(
        [value[at : at + rows] for at in range(0, value.shape[0], rows)], axis=1
    )


def rows_of(refs):
    return jnp.concatenate([ref[...] for ref in refs], axis=0)


def local_body(count, *refs):
    x_refs, refs = refs[:count], refs[count:]
    (gb_ref, core_ref, w_ref), refs = refs[:3], refs[3:]
    carry, (gqkv_ref, gout_ref, ab_ref, token_ref) = refs[:-4], refs[-4:]
    token_ref[...] = jnp.zeros_like(token_ref)
    gqkv, gout, abs_ = local_grads(x_refs, gb_ref, core_ref, w_ref, carry)
    gqkv_ref[...] = gqkv
    gout_ref[...] = gout
    ab_ref[...] = jnp.concatenate(abs_, axis=0)


def local_grads(x_refs, gb_ref, core_ref, w_ref, carry):
    x = rows_of(x_refs)
    rows = x_refs[0].shape[0]
    tile = rows // 2 if rows % (2 * BF16_ROWS) == 0 else rows
    allowed = window(tile)
    qkv = dot(x, w_ref[...])
    abs_, gqs = [], []
    for start in range(0, x.shape[0], tile):
        at = slice(start, start + tile)
        query, key, vb, weight = core_weights(qkv[at], allowed)
        abs_.append(core_forward(weight, vb))
        gqs.append(core_backward(query, key, vb, weight, core_ref[at, :]))
    gqkv = dot(jnp.concatenate(gqs, axis=0), x, ((0,), (0,)))
    gout = dot(jnp.concatenate(abs_, axis=0), gb_ref[...], ((0,), (0,)))
    if carry:
        gqkv += carry[0][...]
        gout += carry[1][...]
    return gqkv, gout, abs_


def local_last_body(count, rounds, info_ref, *refs):
    x_refs, refs = refs[:count], refs[count:]
    gb_ref, core_ref, w_ref, *refs = refs
    *carry, ab0_ref = refs[:3]
    gqkv_out, message, *pieces = refs[3 : 4 + rounds]
    own_ref, held = refs[4 + rounds :]
    gqkv, gout, abs_ = local_grads(x_refs, gb_ref, core_ref, w_ref, carry)
    held[...] = gout
    deep = own_ref.shape[0]
    piece_rows = deep * LANES // held.shape[1]
    for k in range(rounds):
        at = pl.multiple_of((info_ref[2] ^ k) * piece_rows, piece_rows)
        piece = chunks_in(held[pl.ds(at, piece_rows), :]).astype(BF16)
        if k:
            pieces[k - 1].ref[...] = piece
            pieces[k - 1].send()
        else:
            own_ref[...] = piece
    gqkv_out.ref[...] = gqkv.T.astype(BF16)
    gqkv_out.send()
    rows = x_refs[0].shape[0]
    message.ref[:rows, :] = ab0_ref[rows:, :]
    message.ref[rows:, :] = jnp.concatenate(abs_, axis=0)


def relay_body(*refs):
    ab0_ref, ab1_ref, there_ref, *messages, own_ref = refs
    rows = ab0_ref.shape[0] // 2
    for k, message in enumerate(messages):
        message.ref[:rows, :] = ab1_ref[k * rows : (k + 1) * rows, :]
        message.ref[rows:, :] = there_ref[(k + 1) * rows : (k + 2) * rows, :]
        message.send()
    own_ref[:rows, :] = ab0_ref[:rows, :]
    own_ref[rows:, :] = there_ref[:rows, :]


def planes_body(rounds, planes, info_ref, *refs):
    pieces, outs, held = refs[:rounds], refs[rounds:-1], refs[-1]
    for k, piece in enumerate(pieces):
        held[k] = piece[...].astype(F32)
    for z, out in enumerate(outs):
        total = None
        for outer in range(rounds // planes):
            term = held[info_ref[2] ^ ((info_ref[3] ^ z) + outer * planes)]
            total = term if total is None else total + term
        out.ref[...] = total.astype(BF16)
        out.send()


def local_layer(normed, normed_near, info, parts, gbs, cores, weights, rounds, planes):
    rows, width = normed.shape
    d = LOCAL_HEAD_DIM
    near = [swap(normed, bits) for bits in parts[1]]
    count = len(near)
    totals = [((3 * d, width), F32), ((d, width), F32)]

    def step(index, xs, carry):
        return staged(
            functools.partial(local_body, len(xs)),
            [*xs, gbs[index], cores[index], weights, *carry],
            [],
            [*totals, ((len(xs) * rows, d), BF16), TOKEN],
            flops=1 << 34,
            mib=20,
        )

    *carry, ab0, done = step(0, [normed_near, swap(normed, 1)], [])
    near = [tie(block, done) for block in near]
    far = [swap(block, 1) for block in near]
    *carry, ab1, _ = step(1, near, carry)
    deep = d // rounds * width // LANES
    piece = ((deep, d), BF16)
    grad_qkv, message, *pieces, own = staged(
        functools.partial(local_last_body, count, rounds),
        [*far, gbs[2], cores[2], weights, *carry, ab0],
        [((width, 3 * d), BF16), (((count + 1) * rows, d), BF16)] + [piece] * (rounds - 1),
        [piece],
        [pltpu.VMEM((d, width), F32)],
        info,
        flops=1 << 34,
        mib=20,
    )
    pieces = [own] + [swap(value, k + 1) for k, value in enumerate(pieces)]
    block = ((2 * rows, d), BF16)
    *sent, own = staged(
        relay_body, [ab0, ab1, swap(message, 1)], [block] * count, [block]
    )
    messages = [swap(sent[k], 2 * (k + 1)) for k in range(count - 1, -1, -1)]
    messages = [own] + messages[::-1]
    pieces = staged(
        functools.partial(planes_body, rounds, planes),
        pieces,
        [piece] * planes,
        scratch=[pltpu.VMEM((rounds, deep, d), F32)],
        info=info,
    )
    return messages, pieces, grad_qkv


def hidden_body(heads, info_ref, state_ref, w_ref, *refs):
    *messages, out_ref, token_ref = refs
    token_ref[...] = jnp.zeros_like(token_ref)
    rows = state_ref.shape[0]
    d = LOCAL_HEAD_DIM
    total = state_ref[...]
    for bits in range(2 * len(messages)):
        at = bits % 2 * rows
        head = heads(info_ref[1] ^ bits)
        weights = w_ref[0, pl.ds(pl.multiple_of(head * d, d), d), :]
        total += dot(messages[bits // 2][at : at + rows, :], weights)
    out_ref[...] = total.astype(BF16)


def final_body(heads, parts_ref, _, *refs):
    *terms, gqkv_ref, gout_ref = refs
    gout = sum(term[...].astype(F32) for term in terms)
    gout_ref[0] = chunks_out(gout, gout_ref.shape[1])
    d = LOCAL_HEAD_DIM
    tp_count = len(heads)
    for h in range(LOCAL_HEADS):
        total = None
        for source in range(parts_ref.shape[0]):
            if heads[source % tp_count] == h:
                term = parts_ref[source].astype(F32)
                total = term if total is None else total + term
        for kind in range(3):
            at = (kind * LOCAL_HEADS + h) * d
            gqkv_ref[0, :, at : at + d] = total[:, kind * d : (kind + 1) * d]


def swap_planes(pieces):
    count = len(pieces)
    return [pieces[0]] + [
        lax.ppermute(pieces[k], "ctx", [(c, c ^ k) for c in range(count)]) for k in range(1, count)
    ]


def per_device(byte_embeds, local_embeds, global_qkv, global_out, local_qkv, local_out, cotangent):
    byte_count, width = byte_embeds.shape
    patches = byte_count // PATCH
    planes, tp_count = lax.axis_size("ctx"), lax.axis_size("tp")
    plane, me = lax.axis_index("ctx"), lax.axis_index("tp")
    order = block_order(tp_count)
    shard_rows = tp_count * patches
    devices = planes * tp_count

    group = min(tp_count, LOCAL_HEADS)
    share = width // devices
    rounds = LOCAL_HEAD_DIM // share
    plane_heads = LOCAL_HEADS // planes

    def head_of(t):
        return (t % rounds) % planes * plane_heads + t // rounds

    heads = [head_of(t) for t in range(tp_count)]
    head_info = jnp.stack([head_of(me), me, me % rounds, plane]).astype(jnp.int32)

    patch_in = patch_norm(byte_embeds)
    mine = swap(patch_in, 1)
    weights_in, head_info = preload(global_qkv, head_info, mine)
    even = [tie(swap(patch_in, bits), head_info) for bits in range(2, tp_count, 2)]
    pieces = [patch_in, *even, mine, *(swap(piece, 1) for piece in even)]
    q, kv, gb, kv_near, q_near = project(head_info, pieces, weights_in, global_qkv, cotangent, tp_count)

    place = (
        (me ^ jnp.array(order, jnp.int32))[:, None] * patches
        + jnp.arange(patches, dtype=jnp.int32)[None, :]
    ).reshape(-1)
    fits = den_lanes(shard_rows) < q.shape[1] and 2 * q.shape[1] // HEAD_DIM <= DEN_ROWS
    if planes == 4 and fits:
        mask = (place[None, :] <= place[:, None]).astype(F32)
        top, den, edge, back = attend_paired(
            head_info, q, kv, q_near, kv_near, mask, tp_count
        )
    else:
        key_place = (
            jnp.arange(planes, dtype=jnp.int32)[:, None] * shard_rows + place[None, :]
        ).reshape(-1)
        mask = (key_place[None, :] <= (plane * shard_rows + place)[:, None]).astype(F32)
        top, den, edge, back = attend_all(head_info, q, kv, mask, tp_count)

    weights_out, _ = preload(global_out, head_info, den)
    even, odd = output_project(head_info, top, den, edge, back, weights_out, tp_count)

    parts = [[0, 1], list(range(2, group, 2)), list(range(3, group, 2))]
    gb_all = lax.all_gather(gb, "tp", axis=0, tiled=True)
    prepared, weights, gbs, cores = prepare(head_info, gb_all, local_qkv, local_out, byte_count, parts)
    state, normed, normed_near = byte_state(
        scatter_sum(even, odd, patches), local_embeds, prepared
    )
    messages, out_pieces, grad_qkv = local_layer(
        normed, normed_near, head_info, parts, gbs, cores, weights, rounds, planes
    )
    grad_qkv = lax.all_to_all(grad_qkv, ("ctx", "tp"), 0, 0, tiled=True)
    out_pieces = swap_planes(out_pieces)
    here = pl.BlockSpec(memory_space=pltpu.VMEM)
    hidden, done = pl.pallas_call(
        functools.partial(hidden_body, head_of),
        in_specs=[pl.BlockSpec(memory_space=pltpu.SMEM)] + [here] * (2 + len(messages)),
        out_specs=[here, here],
        out_shape=[jax.ShapeDtypeStruct((byte_count, width), BF16), TOKEN],
        compiler_params=params(16),
    )(head_info, state, local_out, *messages)
    grad_qkv, grad_out = call(
        functools.partial(final_body, heads),
        [((1, share, 3 * width), F32), ((1, share, width), F32)],
        mib=16,
    )(grad_qkv.reshape(devices, share, 3 * LOCAL_HEAD_DIM), done, *out_pieces)
    return (hidden, grad_qkv, grad_out)


def solution(mesh):
    in_specs = (
        P(("ctx", "tp"), None),
        P(("ctx", "tp"), None),
        P(None, None, "tp"),
        P("tp", None),
        P(),
        P(),
        P(("ctx", "tp"), None),
    )
    out_specs = (P(("ctx", "tp"), None), P(None, ("ctx", "tp"), None), P(None, ("ctx", "tp"), None))
    return jax.shard_map(
        per_device, mesh=mesh, in_specs=in_specs, out_specs=out_specs, check_vma=False
    )
```
